128 devices in a mesh: ctx: 32 (over x, y, core), req: 4 (over z).
Axes of the slice: x: 4, y: 4, z: 4, core: 2. Of those that a mesh axis runs over, the one named last changes fastest.
Arguments:
- queries: bfloat16 [128, 4, 128, 576], P(('req', 'ctx')), may hold values from -32 to 32
- top_rows: int32 [128, 4, 2048], P(('req', 'ctx')), may hold values from 0 to 16383, as said below
- lengths: int32 [128], P(('req', 'ctx')), may hold values from 8196 to 16384, as said below
- span_map: int32 [64], replicated, may hold values from 0 to 31, as said below
- latent_cache: bfloat16 [128, 16384, 576], P('req', 'ctx'), may hold values from -5 to 5
- up_weight: bfloat16 [128, 512, 128], P('req'), may hold values from -2 to 2
- out_weight: bfloat16 [16384, 7168], P('req', 'ctx'), may hold values from -0.046875 to 0.046875
Outputs:
- attended: bfloat16 [128, 4, 7168], P('req', None, 'ctx')
The draws below stay inside these ranges and needn't reach their ends.
Inputs may be any that keep to these rules, and one draw needn't show every extreme that they name: Each list top_rows[r, s] names 2048 distinct positions of request r, among them its newest position limit[r, s] - 1; positions at or past limit[r, s] may occur. At most 96 positions of one list are stored on one ctx device, and in every list one device stores exactly 96 of them. Step s of request r sees limit lengths[r] - 3 + s. `span_map`: entries c and 63 - c name the same device; every ctx device is named by exactly two entries, one in each half.
All inputs are finite; a program needn't handle non-finite values.
Results may differ from the reference program's by a relative error of at most 0.015.
Values may be sent and summed in bfloat16 or wider, within the bound.
A program may use at most 192 MiB of HBM per device.

```python
import jax
import jax.numpy as jnp
from jax import lax

D = 7168
HEADS = 128
LATENT = 512
ROPE = 64
HEAD_V = 128
TOPK = 2048
LEN = 16384
STEPS = 4
REQS = 128
SPANS = 64
CAP = 96


def layout(key):
    key = jax.random.fold_in(key, 101)
    first, second, third = jax.random.split(key, 3)
    order = jax.random.permutation(first, SPANS // 2).astype(jnp.int32)
    span_map = jnp.concatenate([order, order[::-1]])
    lengths = jax.random.randint(second, (REQS,), LEN // 2 + STEPS, LEN + 1, dtype=jnp.int32)
    longest = jax.random.randint(third, (), 0, REQS, dtype=jnp.int32)
    lengths = jnp.where(jnp.arange(REQS, dtype=jnp.int32) == longest, LEN, lengths)
    return (span_map, lengths)


def draw_span_map(key, part):
    return layout(key)[0]


def draw_lengths(key, part):
    return layout(key)[1]


def draw_top_rows(key, part):
    span_map, lengths = layout(key)
    key = jax.random.fold_in(key, 7)
    first, second = jax.random.split(key)
    devices = SPANS // 2
    width = LEN // SPANS
    local_rows = 2 * width
    lines = jnp.arange(local_rows, dtype=jnp.int32)
    place = jnp.argsort(span_map[:devices]).astype(jnp.int32)
    block = jnp.where(lines[None, :] < width, place[:, None], SPANS - 1 - place[:, None])
    where_is = block * width + lines[None, :] % width
    limits = lengths[:, None] + jnp.arange(STEPS, dtype=jnp.int32)[None, :] - STEPS + 1
    current = limits - 1
    current_block = current // width
    hot = jnp.take(span_map, current_block)
    current_line = jnp.where(current_block >= devices, width, 0) + current % width
    noise = jax.random.randint(first, (REQS, STEPS, devices, local_rows), 0, 2 ** 19, dtype=jnp.int32)
    score = noise * local_rows + lines
    own_row = (jnp.arange(devices, dtype=jnp.int32)[None, None, :, None] == hot[:, :, None, None]) & (lines[None, None, None, :] == current_line[:, :, None, None])
    score = jnp.where(own_row, 2 ** 30, score)
    ranked = jnp.argsort(-score, axis=-1)[..., :CAP].astype(jnp.int32)
    slots = jnp.arange(TOPK, dtype=jnp.int32)
    later = jnp.maximum(slots - CAP, 0)
    holder = jnp.where(slots[None, None, :] < CAP, hot[..., None], (hot[..., None] + 1 + later[None, None, :] % (devices - 1)) % devices)
    rank = jnp.where(slots < CAP, slots, later // (devices - 1))
    line = jnp.take_along_axis(ranked.reshape(REQS, STEPS, devices * CAP), holder * CAP + rank[None, None, :], axis=-1)
    positions = jnp.take(where_is.reshape(-1), holder * local_rows + line)
    shuffle = jax.random.randint(second, (REQS, STEPS, TOPK), 0, 2 ** 19, dtype=jnp.int32) * TOPK + slots
    order = jnp.argsort(shuffle, axis=-1)
    return jnp.take_along_axis(positions, order, axis=-1).astype(jnp.int32)


def draw_latent_cache(key, part):
    key = jax.random.fold_in(key, 5)
    shape = (REQS, LEN, LATENT + ROPE)
    rows = jnp.clip(jax.random.normal(key, shape, jnp.float32), -5.0, 5.0)
    return rows.astype(jnp.bfloat16)


def draw_queries(key, part):
    key = jax.random.fold_in(key, 9)
    first = jax.random.fold_in(key, 0)
    shape = (REQS, STEPS, HEADS, LATENT + ROPE)
    rows = jnp.clip(jax.random.normal(first, shape, jnp.float32), -5.0, 5.0)
    return rows.astype(jnp.bfloat16)


def levels(key, extent, cuts, least, high):
    loudness, own = 1.0, jax.random.fold_in(key, 6)
    for axis_at, shards_of in cuts:
        steps = jnp.exp(jax.random.uniform(jax.random.fold_in(own, axis_at), (shards_of,), jnp.float32, least / len(cuts), high / len(cuts)))
        loudness = loudness * jnp.repeat(steps, extent[axis_at] // shards_of).reshape([-1 if axis == axis_at else 1 for axis in range(len(extent))])
    return loudness


def centred(own_key, extent, scale, reach, cuts=(), held_as=jnp.bfloat16):
    level = levels(own_key, extent, cuts, -0.22, 0.18) if cuts else 1.0
    result = jax.random.normal(own_key, extent, jnp.float32) * scale * level
    return jnp.minimum(jnp.maximum(result, -reach), reach).astype(held_as)


def setup_inputs(seed: int = 0) -> dict:
    splits = jax.random.split(jax.random.key(seed), 8)
    queries = draw_queries(jax.random.fold_in(splits[7], 71), 0)
    top_rows = draw_top_rows(jax.random.fold_in(splits[7], 71), 0)
    lengths = draw_lengths(jax.random.fold_in(splits[7], 71), 0)
    span_map = draw_span_map(jax.random.fold_in(splits[7], 71), 0)
    latent_cache = draw_latent_cache(jax.random.fold_in(splits[7], 71), 0)
    up_weight = centred(splits[5], (HEADS, LATENT, HEAD_V), 0.35, 2.0, ((0, 4),))
    out_weight = centred(splits[6], (HEADS * HEAD_V, D), (HEADS * HEAD_V) ** -0.5, 0.046875, ((0, 4), (1, 32)))
    return dict(queries=queries, top_rows=top_rows, lengths=lengths, span_map=span_map, latent_cache=latent_cache, up_weight=up_weight, out_weight=out_weight)


score_scale = 192.0 ** -0.5


def reference(queries, top_rows, lengths, span_map, latent_cache, up_weight, out_weight):
    devices = SPANS // 2
    width = LEN // SPANS
    blocks = top_rows // width
    holder = jnp.take(span_map, blocks)
    stored = holder * (2 * width) + jnp.where(blocks >= devices, width, 0) + top_rows % width
    ahead = jnp.arange(STEPS, dtype=jnp.int32) - STEPS + 1
    limits = lengths[:, None] + ahead[None, :]

    def one_request(pieces):
        query, picks, rows, limit, cache = pieces
        keys = jnp.take(cache, rows.astype(jnp.int32), axis=0)
        scores = jnp.einsum("shd,skd->shk", query.astype(jnp.float32), keys.astype(jnp.float32)) * score_scale
        valid = picks < limit[:, None]
        scores = jnp.where(valid[:, None, :], scores, -jnp.inf)
        top = jnp.max(scores, axis=-1, keepdims=True)
        weights = jnp.exp(scores - top)
        probs = (weights / jnp.sum(weights, axis=-1, keepdims=True)).astype(jnp.bfloat16)
        mixed = jnp.einsum("shk,skc->shc", probs.astype(jnp.float32), keys[..., :LATENT].astype(jnp.float32))
        return mixed.astype(jnp.bfloat16)

    latent_out = lax.map(one_request, (queries, top_rows, stored, limits, latent_cache))
    head_values = jnp.einsum("rshl,hle->rshe", latent_out.astype(jnp.float32), up_weight.astype(jnp.float32)).astype(jnp.bfloat16)
    flat = head_values.reshape(REQS * STEPS, HEADS * HEAD_V)
    attended = jnp.dot(flat, out_weight, preferred_element_type=jnp.float32).astype(jnp.bfloat16)
    return attended.reshape(REQS, STEPS, D)
```

```python
import functools

import jax
import jax.numpy as jnp
from jax import lax
from jax.experimental import pallas as pl
from jax.experimental.pallas import tpu as pltpu
from jax.sharding import PartitionSpec as P

score_scale = 192.0 ** (-0.5)
log2_scale = score_scale * 1.4426950408889634
masked = -1e30
lowest = -16384.0


def stored_index(top_rows, limits, span_map, width):
    spans = span_map.shape[0]
    blocks = top_rows // width
    marks = blocks[..., None] == jnp.arange(spans, dtype=jnp.int32)
    holder = jnp.sum(jnp.where(marks, span_map, 0), axis=-1)
    local = jnp.where(blocks >= spans // 2, width, 0) + top_rows % width
    stored = holder * (2 * width) + local
    return jnp.where(top_rows < limits[..., None], stored, -1)


def mask_kernel(stored_ref, bias_ref):
    steps, picks = stored_ref.shape
    rows, lanes = bias_ref.shape[1:]
    for step in range(steps):
        line = stored_ref[step : step + 1, :]
        high = jnp.where(line < 0, -1, line // lanes)
        low = line % lanes
        row_hot = lax.broadcasted_iota(jnp.int32, (rows, picks), 0) == high
        lane_hot = lax.broadcasted_iota(jnp.int32, (lanes, picks), 0) == low
        count = lax.dot_general(
            row_hot.astype(jnp.float32).astype(jnp.bfloat16),
            lane_hot.astype(jnp.float32).astype(jnp.bfloat16),
            (((1,), (1,)), ((), ())),
            preferred_element_type=jnp.float32,
        )
        bias_ref[step] = jnp.where(count > 0.5, 0.0, masked).astype(jnp.bfloat16)


def unit(cache_t, bias, query_t, hot):
    latent = 512
    left = jnp.concatenate([cache_t, bias], axis=0)
    right = jnp.concatenate([query_t, hot], axis=0)
    scores = lax.dot_general(
        left, right, (((0,), (0,)), ((), ())), preferred_element_type=jnp.float32
    )
    top = jnp.max(scores, axis=0, keepdims=True) * log2_scale
    top = jnp.maximum(top, lowest).astype(jnp.bfloat16).astype(jnp.float32)
    weights = jnp.exp2(scores * log2_scale - top)
    total = jnp.sum(weights, axis=0, keepdims=True)
    mixed = jnp.dot(
        cache_t[:latent], weights.astype(jnp.bfloat16), preferred_element_type=jnp.float32
    )
    return mixed, top, total


def hot_rows(columns):
    row = lax.broadcasted_iota(jnp.int32, (16, columns), 0)
    col = lax.broadcasted_iota(jnp.int32, (16, columns), 1)
    return row, col // 128


def attend_kernel(cache_ref, bias_ref, query_ref, out_ref, stat_ref):
    pair = pl.program_id(1)
    row, step = hot_rows(256)
    hot = jnp.where(row == step + 2 * pair, 1.0, 0.0).astype(jnp.bfloat16)
    mixed, top, total = unit(cache_ref[0], bias_ref[0], query_ref[0, 0], hot)
    out_ref[0, 0] = mixed.astype(jnp.bfloat16)
    stat_ref[0, 0, 0:1] = top
    stat_ref[0, 0, 1:2] = total


def per_device(queries, top_rows, lengths, span_map, latent_cache, up_weight, out_weight):
    devices = lax.axis_size("ctx")
    groups = lax.axis_size("req")
    owned, steps, heads, depth = queries.shape
    latent = up_weight.shape[1]
    local_rows = latent_cache.shape[1]
    width = local_rows // 2
    requests = latent_cache.shape[0]
    ahead = jnp.arange(steps, dtype=jnp.int32) - steps + 1
    limits = lengths[:, None] + ahead[None, :]
    stored = stored_index(top_rows, limits, span_map, width)[0]
    bias = pl.pallas_call(
        mask_kernel,
        out_shape=jax.ShapeDtypeStruct((steps, 128, 128), jnp.bfloat16),
    )(stored)
    bias = bias.reshape(steps, devices, local_rows).transpose(1, 0, 2)
    bias = lax.all_to_all(bias, "ctx", split_axis=0, concat_axis=0, tiled=True)
    bias = jnp.pad(bias, ((0, 0), (0, 12), (0, 0)))

    query_t = jnp.swapaxes(queries, 2, 3).reshape(2, 2, depth, heads)
    query_t = query_t.transpose(0, 2, 1, 3).reshape(1, 2, depth, 2 * heads)
    query_t = lax.all_gather(query_t, "ctx", axis=0, tiled=True)
    cache_t = jnp.swapaxes(latent_cache, 1, 2)
    mixed, stats = pl.pallas_call(
        attend_kernel,
        grid=(requests, 2),
        in_specs=[
            pl.BlockSpec((1, depth, local_rows), lambda r, p: (r, 0, 0)),
            pl.BlockSpec((1, 16, local_rows), lambda r, p: (r, 0, 0)),
            pl.BlockSpec((1, 1, depth, 256), lambda r, p: (r, p, 0, 0)),
        ],
        out_specs=[
            pl.BlockSpec((1, 1, latent, 256), lambda r, p: (r, p, 0, 0)),
            pl.BlockSpec((1, 1, 2, 256), lambda r, p: (r, p, 0, 0)),
        ],
        out_shape=[
            jax.ShapeDtypeStruct((requests, 2, latent, 256), jnp.bfloat16),
            jax.ShapeDtypeStruct((requests, 2, 2, 256), jnp.float32),
        ],
    )(cache_t, bias, query_t)
    top = lax.pmax(stats[:, :, 0], "ctx")
    factor = jnp.exp2(stats[:, :, 0] - top)
    total = lax.psum_scatter(stats[:, :, 1] * factor, "ctx", scatter_dimension=0, tiled=True)
    mixed = (mixed.astype(jnp.float32) * factor[:, :, None, :]).astype(jnp.bfloat16)
    mixed = lax.psum_scatter(mixed, "ctx", scatter_dimension=0, tiled=True)
    latent_t = (mixed.astype(jnp.float32) / total[:, :, None, :]).astype(jnp.bfloat16)
    latent_out = latent_t.reshape(1, 2, latent, 2, heads).transpose(0, 1, 3, 4, 2)
    latent_out = latent_out.reshape(1, steps, heads, latent)

    regrouped = lax.all_to_all(latent_out, "req", split_axis=2, concat_axis=0, tiled=True)
    head_values = jnp.einsum(
        "rshl,hle->rshe", regrouped, up_weight, preferred_element_type=jnp.float32
    ).astype(jnp.bfloat16)
    head_values = head_values.reshape(
        groups, owned * steps, head_values.shape[2] * head_values.shape[3]
    )
    terms = jnp.einsum(
        "gmf,fd->gmd",
        lax.all_gather(head_values, "ctx", axis=1, tiled=True),
        out_weight,
        preferred_element_type=jnp.float32,
    )
    summed = lax.psum_scatter(
        terms.astype(jnp.bfloat16), "req", scatter_dimension=0, tiled=True
    ).astype(jnp.float32)
    return summed.reshape(-1, steps, out_weight.shape[1]).astype(jnp.bfloat16)


def solution(mesh):
    return jax.shard_map(
        per_device,
        mesh=mesh,
        in_specs=(
            P(("req", "ctx"), None, None, None),
            P(("req", "ctx"), None, None),
            P(("req", "ctx")),
            P(),
            P("req", "ctx", None),
            P("req", None, None),
            P("req", "ctx"),
        ),
        out_specs=P("req", None, "ctx"),
        check_vma=False,
    )
```

```python
import functools

import jax
import jax.numpy as jnp
from jax import lax
from jax.experimental import pallas as pl
from jax.experimental.pallas import tpu as pltpu
from jax.sharding import PartitionSpec as P

score_scale = 192.0 ** (-0.5)
log2_scale = score_scale * 1.4426950408889634
masked = -1e30
lowest = -16384.0


def stored_index(top_rows, limits, span_map, width):
    spans = span_map.shape[0]
    blocks = top_rows // width
    marks = blocks[..., None] == jnp.arange(spans, dtype=jnp.int32)
    holder = jnp.sum(jnp.where(marks, span_map, 0), axis=-1)
    local = jnp.where(blocks >= spans // 2, width, 0) + top_rows % width
    stored = holder * (2 * width) + local
    return jnp.where(top_rows < limits[..., None], stored, -1)


def mask_kernel(stored_ref, bias_ref):
    steps, picks = stored_ref.shape
    rows, lanes = bias_ref.shape[1:]
    for step in range(steps):
        line = stored_ref[step : step + 1, :]
        high = jnp.where(line < 0, -1, line // lanes)
        low = line % lanes
        row_hot = lax.broadcasted_iota(jnp.int32, (rows, picks), 0) == high
        lane_hot = lax.broadcasted_iota(jnp.int32, (lanes, picks), 0) == low
        count = lax.dot_general(
            row_hot.astype(jnp.float32).astype(jnp.bfloat16),
            lane_hot.astype(jnp.float32).astype(jnp.bfloat16),
            (((1,), (1,)), ((), ())),
            preferred_element_type=jnp.float32,
        )
        bias_ref[step] = jnp.where(count > 0.5, 0.0, masked).astype(jnp.bfloat16)


MESH = pl.DeviceIdType.MESH
side = 4
slots = side * side
key_rows = 592
latent_rows = 512
part_rows = 528


def attend_unit(keys, query):
    scores = lax.dot_general(
        query, keys, (((0,), (0,)), ((), ())), preferred_element_type=jnp.float32
    )
    top = jnp.max(scores, axis=1, keepdims=True) * log2_scale
    top = jnp.maximum(top, lowest).astype(jnp.bfloat16).astype(jnp.float32)
    weights = jnp.exp2(scores * log2_scale - top)
    total = jnp.sum(weights, axis=1, keepdims=True)
    mixed = lax.dot_general(
        weights.astype(jnp.bfloat16),
        keys[:latent_rows],
        (((1,), (1,)), ((), ())),
        preferred_element_type=jnp.float32,
    )
    mixed = jnp.swapaxes(mixed.astype(jnp.bfloat16), 0, 1)
    top = jnp.swapaxes(jnp.broadcast_to(top, (256, 128)), 0, 1)[0:16]
    total = jnp.swapaxes(jnp.broadcast_to(total, (256, 128)), 0, 1)[0:16]
    return mixed, stat_rows(top, total)


def stat_rows(top, total):
    row = lax.broadcasted_iota(jnp.int32, (16, 256), 0)
    high = total.astype(jnp.bfloat16).astype(jnp.float32)
    rows = jnp.where(row == 0, top, jnp.where(row == 1, high, total - high))
    return jnp.where(row < 3, rows, 0.0).astype(jnp.bfloat16)


def merge_weights(refs):
    stats = [ref[latent_rows:part_rows].astype(jnp.float32) for ref in refs]
    top = functools.reduce(jnp.maximum, [stat[0:1] for stat in stats])
    factors = [jnp.exp2(stat[0:1] - top) for stat in stats]
    total = sum(f * (stat[1:2] + stat[2:3]) for f, stat in zip(factors, stats))
    return top, factors, total


def merge(refs, out):
    top, factors, total = merge_weights(refs)

    def chunk(i, carry):
        rows = pl.ds(pl.multiple_of(i * 64, 64), 64)
        parts = [f * ref[rows].astype(jnp.float32) for f, ref in zip(factors, refs)]
        out[rows] = sum(parts[1:], parts[0]).astype(jnp.bfloat16)
        return carry

    lax.fori_loop(0, latent_rows // 64, chunk, 0)
    shape = (16, 256)
    out[latent_rows:part_rows] = stat_rows(
        jnp.broadcast_to(top, shape), jnp.broadcast_to(total, shape)
    )


def gather_attend_kernel(
    query_ref, bias_ref, cache_ref, out_ref,
    own, sib, kept, from_sib, ring_in, last_in, keys,
    load_sem, key_sem, own_recv, sib_recv, a_send, b_send, sib_send,
    part_send, part_recv, ring_send, ring_recv, last_send, last_recv,
):
    me = lax.axis_index("ctx")
    core = me % 2
    chip = me // 2
    a_step = 4 - 3 * core
    b_step = 1 + 3 * core
    a = (chip // a_step) % 4
    b = (chip // b_step) % 4

    def device(da, db):
        return (((a + da + 4) % 4) * a_step + ((b + db + 4) % 4) * b_step) * 2 + core

    sibling = chip * 2 + 1 - core
    barrier = pltpu.get_barrier_semaphore()
    partners = [device(1, 0), device(3, 0), device(2, 0), device(0, 1), device(0, 3), sibling]
    for partner in partners:
        pl.semaphore_signal(barrier, inc=1, device_id={"ctx": partner}, device_id_type=MESH)

    def own_request(flow, slot):
        da, db = slot % 4, slot // 4
        if flow == 0:
            da, db = 4 - da, 4 - db
        return (((a + da) % 4) * a_step + ((b + db) % 4) * b_step) * 2 + core

    def sib_request(flow, slot):
        da, db = slot % 4, slot // 4
        if flow == 0:
            da, db = 4 - da, 4 - db
        return (((b + da) % 4) * b_step + ((a + db) % 4) * a_step) * 2 + 1 - core

    def key_copies(slot, place):
        copies = []
        for flow in range(2):
            for which, request in ((0, own_request(flow, slot)), (1, sib_request(flow, slot))):
                at = 2 * which + flow
                copies.append(pltpu.make_async_copy(
                    cache_ref.at[request], keys.at[place, at, pl.ds(0, 576)],
                    key_sem.at[place, at, 0]))
                copies.append(pltpu.make_async_copy(
                    bias_ref.at[request], keys.at[place, at, pl.ds(576, 16)],
                    key_sem.at[place, at, 1]))
        return copies

    def remote(src, dst, send, recv, target):
        return pltpu.make_async_remote_copy(
            src_ref=src, dst_ref=dst, send_sem=send, recv_sem=recv,
            device_id={"ctx": target}, device_id_type=MESH)

    body = pl.ds(0, 576)

    def a_copy(flow, slot):
        return remote(own.at[flow, slot, body], own.at[flow, slot + 1, body],
                      a_send.at[flow, slot], own_recv.at[flow, slot + 1],
                      device(1 - 2 * flow, 0))

    def b_copy(flow, slot):
        return remote(own.at[flow, slot, body], own.at[flow, slot + 4, body],
                      b_send.at[flow, slot], own_recv.at[flow, slot + 4],
                      device(0, 1 - 2 * flow))

    def sib_copy(flow, slot):
        return remote(own.at[flow, slot, body], sib.at[flow, slot, body],
                      sib_send.at[flow, slot], sib_recv.at[flow, slot], sibling)

    part = pl.ds(0, part_rows)

    def part_copy(flow, slot):
        return remote(sib.at[flow, slot, part], from_sib.at[flow, slot],
                      part_send.at[flow, slot], part_recv.at[flow, slot], sibling)

    def ring_copy(flow, slot):
        return remote(kept.at[flow, slot], ring_in.at[flow, slot - 4],
                      ring_send.at[flow, slot - 4], ring_recv.at[flow, slot - 4],
                      device(0, 1 - 2 * flow))

    def last_copy(flow, da):
        return remote(kept.at[flow, da], last_in.at[flow, da - 1],
                      last_send.at[flow, da - 1], last_recv.at[flow, da - 1],
                      device(-da if flow == 0 else da - 4, 0))

    loads = [
        pltpu.make_async_copy(
            query_ref.at[2 * flow + half],
            own.at[flow, 0, body, pl.ds(128 * half, 128)],
            load_sem.at[flow, half])
        for flow in range(2) for half in range(2)
    ]
    for copy in loads:
        copy.start()
    for copy in key_copies(0, 0):
        copy.start()

    row = lax.broadcasted_iota(jnp.int32, (16, 256), 0)
    step = lax.broadcasted_iota(jnp.int32, (16, 256), 1) // 128
    for flow in range(2):
        hot = jnp.where(row == step + 2 * flow, 1.0, 0.0).astype(jnp.bfloat16)

        def fill(slot, carry):
            own[flow, slot, 576:key_rows] = hot
            sib[flow, slot, 576:key_rows] = hot
            return carry

        lax.fori_loop(0, slots, fill, 0)
    for copy in loads:
        copy.wait()
    pl.semaphore_wait(barrier, len(partners))

    def combine(slot):
        for flow in range(2):
            part_copy(flow, slot).wait_recv()

        @pl.when(slot < 8)
        def _():
            for flow in range(2):
                merge([kept.at[flow, slot], from_sib.at[flow, slot]], kept.at[flow, slot])
                ring_copy(flow, slot).start()

        @pl.when(slot >= 8)
        def _():
            for flow in range(2):
                ring_copy(flow, slot - 4).wait_recv()
                merge([kept.at[flow, slot], from_sib.at[flow, slot], ring_in.at[flow, slot - 8]],
                      kept.at[flow, slot])
                ring_copy(flow, slot).start()

    def iteration(slot, carry):
        place = slot % 2

        @pl.when(slot > 0)
        def _():
            for flow in range(2):
                b_or_a = remote(own.at[flow, slot, body], own.at[flow, slot, body],
                                a_send.at[flow, 0], own_recv.at[flow, slot], sibling)
                b_or_a.wait_recv()

        @pl.when(slot < 3)
        def _():
            for flow in range(2):
                a_copy(flow, slot).start()

        @pl.when(slot < 12)
        def _():
            for flow in range(2):
                b_copy(flow, slot).start()

        for flow in range(2):
            sib_copy(flow, slot).start()

        @pl.when(slot < slots - 1)
        def _():
            for copy in key_copies(slot + 1, 1 - place):
                copy.start()

        for copy in key_copies(slot, place):
            copy.wait()

        for flow in range(2):
            mixed, stats = attend_unit(keys[place, flow], own[flow, slot])
            kept[flow, slot, 0:latent_rows] = mixed
            kept[flow, slot, latent_rows:part_rows] = stats

        for flow in range(2):
            sib_copy(flow, slot).wait_recv()
        results = [attend_unit(keys[place, 2 + flow], sib[flow, slot]) for flow in range(2)]
        for flow in range(2):
            mixed, stats = results[flow]
            sib[flow, slot, 0:latent_rows] = mixed
            sib[flow, slot, latent_rows:part_rows] = stats
            part_copy(flow, slot).start()

        @pl.when(slot > 4)
        def _():
            combine(slot - 1)

        return carry

    lax.fori_loop(0, slots, iteration, 0)
    combine(slots - 1)

    for da in (1, 2, 3, 0):
        for flow in range(2):
            part_copy(flow, da).wait_recv()
            ring_copy(flow, 12 + da).wait_recv()
            merge([kept.at[flow, da], from_sib.at[flow, da], ring_in.at[flow, 8 + da]],
                  kept.at[flow, da])
            if da:
                last_copy(flow, da).start()
    for flow in range(2):
        for da in (1, 2, 3):
            last_copy(flow, da).wait_recv()
        refs = [kept.at[flow, 0]] + [last_in.at[flow, i] for i in range(3)]
        top, factors, total = merge_weights(refs)
        scale = 1.0 / total
        for i in range(latent_rows // 128):
            rows = pl.ds(128 * i, 128)
            parts = [f * scale * ref[rows].astype(jnp.float32) for f, ref in zip(factors, refs)]
            final = sum(parts[1:], parts[0]).astype(jnp.bfloat16)
            out_ref[flow, :, 128 * i : 128 * (i + 1)] = jnp.swapaxes(final, 0, 1)

    for flow in range(2):
        def drain(slot, carry):
            sib_copy(flow, slot).wait_send()
            part_copy(flow, slot).wait_send()

            @pl.when(slot < 3)
            def _():
                a_copy(flow, slot).wait_send()

            @pl.when(slot < 12)
            def _():
                b_copy(flow, slot).wait_send()
                ring_copy(flow, slot + 4).wait_send()

            return carry

        lax.fori_loop(0, slots, drain, 0)
        for da in (1, 2, 3):
            last_copy(flow, da).wait_send()


def gather_attend(query_t, bias, cache_t):
    dma = pltpu.SemaphoreType.DMA
    bf16 = jnp.bfloat16
    return pl.pallas_call(
        gather_attend_kernel,
        in_specs=[pl.BlockSpec(memory_space=pl.ANY)] * 3,
        out_specs=pl.BlockSpec(memory_space=pltpu.VMEM),
        out_shape=jax.ShapeDtypeStruct((2, 256, latent_rows), bf16),
        scratch_shapes=[
            pltpu.VMEM((2, slots, key_rows, 256), bf16),
            pltpu.VMEM((2, slots, key_rows, 256), bf16),
            pltpu.VMEM((2, slots, part_rows, 256), bf16),
            pltpu.VMEM((2, slots, part_rows, 256), bf16),
            pltpu.VMEM((2, 12, part_rows, 256), bf16),
            pltpu.VMEM((2, 3, part_rows, 256), bf16),
            pltpu.VMEM((2, 4, key_rows, 512), bf16),
            dma((2, 2)),
            dma((2, 4, 2)),
            dma((2, slots)),
            dma((2, slots)),
            dma((2, 3)),
            dma((2, 12)),
            dma((2, slots)),
            dma((2, slots)),
            dma((2, slots)),
            dma((2, 12)),
            dma((2, 12)),
            dma((2, 3)),
            dma((2, 3)),
        ],
        compiler_params=pltpu.CompilerParams(
            collective_id=0, has_side_effects=True, vmem_limit_bytes=58 * 2**20
        ),
        cost_estimate=pl.CostEstimate(
            flops=18_000_000_000, bytes_accessed=40_000_000, transcendentals=8_000_000
        ),
    )(query_t, bias, cache_t)


def per_device(queries, top_rows, lengths, span_map, latent_cache, up_weight, out_weight):
    devices = lax.axis_size("ctx")
    groups = lax.axis_size("req")
    owned, steps, heads, depth = queries.shape
    latent = up_weight.shape[1]
    local_rows = latent_cache.shape[1]
    width = local_rows // 2
    ahead = jnp.arange(steps, dtype=jnp.int32) - steps + 1
    limits = lengths[:, None] + ahead[None, :]
    stored = stored_index(top_rows, limits, span_map, width)[0]
    bias = pl.pallas_call(
        mask_kernel,
        out_shape=jax.ShapeDtypeStruct((steps, 128, 128), jnp.bfloat16),
    )(stored)
    bias = bias.reshape(steps, devices, local_rows).transpose(1, 0, 2)
    bias = lax.all_to_all(bias, "ctx", split_axis=0, concat_axis=0, tiled=True)
    bias = jnp.pad(bias, ((0, 0), (0, 12), (0, 0)))

    query_t = jnp.swapaxes(queries, 2, 3)[0]
    cache_t = jnp.swapaxes(latent_cache, 1, 2)
    mixed = gather_attend(query_t, bias, cache_t)
    latent_out = mixed.reshape(1, steps, heads, latent)

    regrouped = lax.all_to_all(latent_out, "req", split_axis=2, concat_axis=0, tiled=True)
    head_values = jnp.einsum(
        "rshl,hle->rshe", regrouped, up_weight, preferred_element_type=jnp.float32
    ).astype(jnp.bfloat16)
    head_values = head_values.reshape(
        groups, owned * steps, head_values.shape[2] * head_values.shape[3]
    )
    terms = jnp.einsum(
        "gmf,fd->gmd",
        lax.all_gather(head_values, "ctx", axis=1, tiled=True),
        out_weight,
        preferred_element_type=jnp.float32,
    )
    summed = lax.psum_scatter(
        terms.astype(jnp.bfloat16), "req", scatter_dimension=0, tiled=True
    ).astype(jnp.float32)
    return summed.reshape(-1, steps, out_weight.shape[1]).astype(jnp.bfloat16)


def solution(mesh):
    return jax.shard_map(
        per_device,
        mesh=mesh,
        in_specs=(
            P(("req", "ctx"), None, None, None),
            P(("req", "ctx"), None, None),
            P(("req", "ctx")),
            P(),
            P("req", "ctx", None),
            P("req", None, None),
            P("req", "ctx"),
        ),
        out_specs=P("req", None, "ctx"),
        check_vma=False,
    )
```

```python
import functools

import jax
import jax.numpy as jnp
from jax import lax
from jax.experimental import pallas as pl
from jax.experimental.pallas import tpu as pltpu
from jax.sharding import PartitionSpec as P

score_scale = 192.0 ** (-0.5)
log2_scale = score_scale * 1.4426950408889634
masked = -1e30
lowest = -16384.0


def stored_index(top_rows, limits, span_map, width):
    spans = span_map.shape[0]
    blocks = top_rows // width
    marks = blocks[..., None] == jnp.arange(spans, dtype=jnp.int32)
    holder = jnp.sum(jnp.where(marks, span_map, 0), axis=-1)
    local = jnp.where(blocks >= spans // 2, width, 0) + top_rows % width
    stored = holder * (2 * width) + local
    return jnp.where(top_rows < limits[..., None], stored, -1)


def mask_kernel(stored_ref, bias_ref):
    steps, picks = stored_ref.shape
    rows, lanes = bias_ref.shape[1:]
    for step in range(steps):
        line = stored_ref[step : step + 1, :]
        high = jnp.where(line < 0, -1, line // lanes)
        low = line % lanes
        row_hot = lax.broadcasted_iota(jnp.int32, (rows, picks), 0) == high
        lane_hot = lax.broadcasted_iota(jnp.int32, (lanes, picks), 0) == low
        count = lax.dot_general(
            row_hot.astype(jnp.float32).astype(jnp.bfloat16),
            lane_hot.astype(jnp.float32).astype(jnp.bfloat16),
            (((1,), (1,)), ((), ())),
            preferred_element_type=jnp.float32,
        )
        bias_ref[step] = jnp.where(count > 0.5, 0.0, masked).astype(jnp.bfloat16)


MESH = pl.DeviceIdType.MESH
side = 4
slots = side * side
key_rows = 592
latent_rows = 512
part_rows = 528


def attend_unit(keys, query):
    scores = lax.dot_general(
        query, keys, (((0,), (0,)), ((), ())), preferred_element_type=jnp.float32
    )
    top = jnp.max(scores, axis=1, keepdims=True) * log2_scale
    top = jnp.maximum(top, lowest).astype(jnp.bfloat16).astype(jnp.float32)
    weights = jnp.exp2(scores * log2_scale - top)
    total = jnp.sum(weights, axis=1, keepdims=True)
    mixed = lax.dot_general(
        weights.astype(jnp.bfloat16),
        keys[:latent_rows],
        (((1,), (1,)), ((), ())),
        preferred_element_type=jnp.float32,
    )
    mixed = jnp.swapaxes(mixed.astype(jnp.bfloat16), 0, 1)
    top = jnp.swapaxes(jnp.broadcast_to(top, (256, 128)), 0, 1)[0:16]
    total = jnp.swapaxes(jnp.broadcast_to(total, (256, 128)), 0, 1)[0:16]
    return mixed, stat_rows(top, total)


def stat_rows(top, total):
    row = lax.broadcasted_iota(jnp.int32, (16, 256), 0)
    high = total.astype(jnp.bfloat16).astype(jnp.float32)
    rows = jnp.where(row == 0, top, jnp.where(row == 1, high, total - high))
    return jnp.where(row < 3, rows, 0.0).astype(jnp.bfloat16)


def merge_weights(refs):
    stats = [ref[latent_rows:part_rows].astype(jnp.float32) for ref in refs]
    top = functools.reduce(jnp.maximum, [stat[0:1] for stat in stats])
    factors = [jnp.exp2(stat[0:1] - top) for stat in stats]
    total = sum(f * (stat[1:2] + stat[2:3]) for f, stat in zip(factors, stats))
    return top, factors, total


def merge(refs, out):
    top, factors, total = merge_weights(refs)

    def chunk(i, carry):
        rows = pl.ds(pl.multiple_of(i * 64, 64), 64)
        parts = [f * ref[rows].astype(jnp.float32) for f, ref in zip(factors, refs)]
        out[rows] = sum(parts[1:], parts[0]).astype(jnp.bfloat16)
        return carry

    lax.fori_loop(0, latent_rows // 64, chunk, 0)
    shape = (16, 256)
    out[latent_rows:part_rows] = stat_rows(
        jnp.broadcast_to(top, shape), jnp.broadcast_to(total, shape)
    )


def gather_attend_kernel(
    query_ref, bias_ref, cache_ref, out_ref,
    own, sib, kept, from_sib, ring_in, last_in, keys,
    load_sem, key_sem, own_recv, sib_recv, a_send, b_send, sib_send,
    part_send, part_recv, ring_send, ring_recv, last_send, last_recv,
):
    me = lax.axis_index("ctx")
    core = me % 2
    chip = me // 2
    a_step = 4 - 3 * core
    b_step = 1 + 3 * core
    a = (chip // a_step) % 4
    b = (chip // b_step) % 4

    def device(da, db):
        return (((a + da + 4) % 4) * a_step + ((b + db + 4) % 4) * b_step) * 2 + core

    sibling = chip * 2 + 1 - core
    barrier = pltpu.get_barrier_semaphore()
    partners = [device(1, 0), device(3, 0), device(2, 0), device(0, 1), device(0, 3), sibling]
    for partner in partners:
        pl.semaphore_signal(barrier, inc=1, device_id={"ctx": partner}, device_id_type=MESH)

    def own_request(flow, slot):
        da, db = slot % 4, slot // 4
        if flow == 0:
            da, db = 4 - da, 4 - db
        return (((a + da) % 4) * a_step + ((b + db) % 4) * b_step) * 2 + core

    def sib_request(flow, slot):
        da, db = slot % 4, slot // 4
        if flow == 0:
            da, db = 4 - da, 4 - db
        return (((b + da) % 4) * b_step + ((a + db) % 4) * a_step) * 2 + 1 - core

    def key_copies(slot, place):
        copies = []
        for flow in range(2):
            for which, request in ((0, own_request(flow, slot)), (1, sib_request(flow, slot))):
                at = 2 * which + flow
                copies.append(pltpu.make_async_copy(
                    cache_ref.at[request], keys.at[place, at, pl.ds(0, 576)],
                    key_sem.at[place, at, 0]))
                copies.append(pltpu.make_async_copy(
                    bias_ref.at[request], keys.at[place, at, pl.ds(576, 16)],
                    key_sem.at[place, at, 1]))
        return copies

    def remote(src, dst, send, recv, target):
        return pltpu.make_async_remote_copy(
            src_ref=src, dst_ref=dst, send_sem=send, recv_sem=recv,
            device_id={"ctx": target}, device_id_type=MESH)

    body = pl.ds(0, 576)

    def a_copy(flow, slot):
        return remote(own.at[flow, slot, body], own.at[flow, slot + 1, body],
                      a_send.at[flow, slot], own_recv.at[flow, slot + 1],
                      device(1 - 2 * flow, 0))

    def b_copy(flow, slot):
        return remote(own.at[flow, slot, body], own.at[flow, slot + 4, body],
                      b_send.at[flow, slot], own_recv.at[flow, slot + 4],
                      device(0, 1 - 2 * flow))

    def sib_copy(flow, slot):
        return remote(own.at[flow, slot, body], sib.at[flow, slot, body],
                      sib_send.at[flow, slot], sib_recv.at[flow, slot], sibling)

    part = pl.ds(0, part_rows)

    def part_copy(flow, slot):
        return remote(sib.at[flow, slot, part], from_sib.at[flow, slot],
                      part_send.at[flow, slot], part_recv.at[flow, slot], sibling)

    def ring_copy(flow, slot):
        return remote(kept.at[flow, slot], ring_in.at[flow, slot - 4],
                      ring_send.at[flow, slot - 4], ring_recv.at[flow, slot - 4],
                      device(0, 1 - 2 * flow))

    def last_copy(flow, da):
        return remote(kept.at[flow, da], last_in.at[flow, da - 1],
                      last_send.at[flow, da - 1], last_recv.at[flow, da - 1],
                      device(-da if flow == 0 else da - 4, 0))

    loads = [
        pltpu.make_async_copy(
            query_ref.at[2 * flow + half],
            own.at[flow, 0, body, pl.ds(128 * half, 128)],
            load_sem.at[flow, half])
        for flow in range(2) for half in range(2)
    ]
    for copy in loads:
        copy.start()
    for copy in key_copies(0, 0):
        copy.start()

    row = lax.broadcasted_iota(jnp.int32, (16, 256), 0)
    step = lax.broadcasted_iota(jnp.int32, (16, 256), 1) // 128
    for flow in range(2):
        hot = jnp.where(row == step + 2 * flow, 1.0, 0.0).astype(jnp.bfloat16)

        def fill(slot, carry):
            own[flow, slot, 576:key_rows] = hot
            sib[flow, slot, 576:key_rows] = hot
            return carry

        lax.fori_loop(0, slots, fill, 0)
    for copy in loads:
        copy.wait()
    pl.semaphore_wait(barrier, len(partners))

    def combine(slot):
        for flow in range(2):
            part_copy(flow, slot).wait_recv()

        @pl.when(slot < 8)
        def _():
            for flow in range(2):
                merge([kept.at[flow, slot], from_sib.at[flow, slot]], kept.at[flow, slot])
                ring_copy(flow, slot).start()

        @pl.when(slot >= 8)
        def _():
            for flow in range(2):
                ring_copy(flow, slot - 4).wait_recv()
                merge([kept.at[flow, slot], from_sib.at[flow, slot], ring_in.at[flow, slot - 8]],
                      kept.at[flow, slot])
                ring_copy(flow, slot).start()

    def iteration(slot, carry):
        place = slot % 2

        @pl.when(slot > 0)
        def _():
            for flow in range(2):
                b_or_a = remote(own.at[flow, slot, body], own.at[flow, slot, body],
                                a_send.at[flow, 0], own_recv.at[flow, slot], sibling)
                b_or_a.wait_recv()

        @pl.when(slot < 3)
        def _():
            for flow in range(2):
                a_copy(flow, slot).start()

        @pl.when(slot < 12)
        def _():
            for flow in range(2):
                b_copy(flow, slot).start()

        for flow in range(2):
            sib_copy(flow, slot).start()

        @pl.when(slot < slots - 1)
        def _():
            for copy in key_copies(slot + 1, 1 - place):
                copy.start()

        for copy in key_copies(slot, place):
            copy.wait()

        for flow in range(2):
            mixed, stats = attend_unit(keys[place, flow], own[flow, slot])
            kept[flow, slot, 0:latent_rows] = mixed
            kept[flow, slot, latent_rows:part_rows] = stats

        for flow in range(2):
            sib_copy(flow, slot).wait_recv()
        results = [attend_unit(keys[place, 2 + flow], sib[flow, slot]) for flow in range(2)]
        for flow in range(2):
            mixed, stats = results[flow]
            sib[flow, slot, 0:latent_rows] = mixed
            sib[flow, slot, latent_rows:part_rows] = stats
            part_copy(flow, slot).start()

        @pl.when(slot > 4)
        def _():
            combine(slot - 1)

        return carry

    lax.fori_loop(0, slots, iteration, 0)
    combine(slots - 1)

    for da in (1, 2, 3, 0):
        for flow in range(2):
            part_copy(flow, da).wait_recv()
            ring_copy(flow, 12 + da).wait_recv()
            merge([kept.at[flow, da], from_sib.at[flow, da], ring_in.at[flow, 8 + da]],
                  kept.at[flow, da])
            if da:
                last_copy(flow, da).start()
    for flow in range(2):
        for da in (1, 2, 3):
            last_copy(flow, da).wait_recv()
        refs = [kept.at[flow, 0]] + [last_in.at[flow, i] for i in range(3)]
        top, factors, total = merge_weights(refs)
        scale = 1.0 / total
        for i in range(latent_rows // 128):
            rows = pl.ds(128 * i, 128)
            parts = [f * scale * ref[rows].astype(jnp.float32) for f, ref in zip(factors, refs)]
            final = sum(parts[1:], parts[0]).astype(jnp.bfloat16)
            out_ref[flow, :, 128 * i : 128 * (i + 1)] = jnp.swapaxes(final, 0, 1)

    for flow in range(2):
        def drain(slot, carry):
            sib_copy(flow, slot).wait_send()
            part_copy(flow, slot).wait_send()

            @pl.when(slot < 3)
            def _():
                a_copy(flow, slot).wait_send()

            @pl.when(slot < 12)
            def _():
                b_copy(flow, slot).wait_send()
                ring_copy(flow, slot + 4).wait_send()

            return carry

        lax.fori_loop(0, slots, drain, 0)
        for da in (1, 2, 3):
            last_copy(flow, da).wait_send()


def gather_attend(query_t, bias, cache_t):
    dma = pltpu.SemaphoreType.DMA
    bf16 = jnp.bfloat16
    return pl.pallas_call(
        gather_attend_kernel,
        in_specs=[pl.BlockSpec(memory_space=pl.ANY)] * 3,
        out_specs=pl.BlockSpec(memory_space=pltpu.VMEM),
        out_shape=jax.ShapeDtypeStruct((2, 256, latent_rows), bf16),
        scratch_shapes=[
            pltpu.VMEM((2, slots, key_rows, 256), bf16),
            pltpu.VMEM((2, slots, key_rows, 256), bf16),
            pltpu.VMEM((2, slots, part_rows, 256), bf16),
            pltpu.VMEM((2, slots, part_rows, 256), bf16),
            pltpu.VMEM((2, 12, part_rows, 256), bf16),
            pltpu.VMEM((2, 3, part_rows, 256), bf16),
            pltpu.VMEM((2, 4, key_rows, 512), bf16),
            dma((2, 2)),
            dma((2, 4, 2)),
            dma((2, slots)),
            dma((2, slots)),
            dma((2, 3)),
            dma((2, 12)),
            dma((2, slots)),
            dma((2, slots)),
            dma((2, slots)),
            dma((2, 12)),
            dma((2, 12)),
            dma((2, 3)),
            dma((2, 3)),
        ],
        compiler_params=pltpu.CompilerParams(
            collective_id=0, has_side_effects=True, vmem_limit_bytes=58 * 2**20
        ),
        cost_estimate=pl.CostEstimate(
            flops=18_000_000_000, bytes_accessed=40_000_000, transcendentals=8_000_000
        ),
    )(query_t, bias, cache_t)


def project_kernel(
    mixed_ref, up_ref, out_weight_ref, out_ref,
    taken, wide, up, weight, values, sums, give, get,
    load_sem, take_send, take_recv, own_recv, sib_recv, a_send, b_send, sib_send,
    give_send, give_recv,
):
    me = lax.axis_index("ctx")
    group = lax.axis_index("req")
    core = me % 2
    chip = me // 2
    a_step = 4 - 3 * core
    b_step = 1 + 3 * core
    a = (chip // a_step) % 4
    b = (chip // b_step) % 4

    def device(da, db):
        return {"ctx": (((a + da) % 4) * a_step + ((b + db) % 4) * b_step) * 2 + core}

    def plane(d):
        return {"req": (group + d) % 4}

    sibling = {"ctx": chip * 2 + 1 - core}
    partners = [device(1, 0), device(3, 0), device(0, 1), device(0, 3), sibling]
    partners += [plane(1), plane(2), plane(3)]
    barrier = pltpu.get_barrier_semaphore()
    for partner in partners:
        pl.semaphore_signal(barrier, inc=1, device_id=partner, device_id_type=MESH)

    def remote(src, dst, send, recv, target):
        return pltpu.make_async_remote_copy(
            src_ref=src, dst_ref=dst, send_sem=send, recv_sem=recv,
            device_id=target, device_id_type=MESH)

    def heads_of(z):
        return mixed_ref.at[:, pl.ds(pl.multiple_of(z * 32, 32), 32)]

    loads = [
        pltpu.make_async_copy(heads_of(group), taken.at[0], load_sem.at[0]),
        pltpu.make_async_copy(up_ref, up, load_sem.at[1]),
        pltpu.make_async_copy(out_weight_ref, weight.at[pl.ds(0, 224)], load_sem.at[2]),
    ]
    for copy in loads:
        copy.start()
    pl.semaphore_wait(barrier, len(partners))
    takes = [
        remote(heads_of((group + d) % 4), taken.at[d], take_send.at[d - 1],
               take_recv.at[d - 1], plane(d))
        for d in (1, 2, 3)
    ]
    for copy in takes:
        copy.start()

    weight[224:256] = jnp.zeros((32, 4096), jnp.bfloat16)
    sums[...] = jnp.zeros_like(sums)
    loads[0].wait()
    loads[1].wait()
    for d in range(4):
        if d:
            takes[d - 1].wait_recv()
        for s in range(4):
            rows = taken[d, s].astype(jnp.float32)
            for i in range(4):
                wide[i, 128 * d + 32 * s : 128 * d + 32 * s + 32] = rows[:, 128 * i : 128 * i + 128]

    def a_copy(flow, slot):
        return remote(values.at[flow, slot, 0], values.at[flow, slot + 1, 0],
                      a_send.at[flow, slot], own_recv.at[flow, slot + 1],
                      device(1 if flow == 0 else 3, 0))

    def b_copy(flow, slot):
        return remote(values.at[flow, slot, 0], values.at[flow, slot + 4, 0],
                      b_send.at[flow, slot], own_recv.at[flow, slot + 4],
                      device(0, 1 if flow == 0 else 3))

    def sib_copy(flow, slot):
        return remote(values.at[flow, slot, 0], values.at[flow, slot, 1],
                      sib_send.at[flow, slot], sib_recv.at[flow, slot], sibling)

    def forward(flow, slot):
        if slot < 3:
            a_copy(flow, slot).start()
        if slot < 12:
            b_copy(flow, slot).start()
        sib_copy(flow, slot).start()

    for flow in range(2):
        for i in range(16):
            head = 16 * flow + i
            rows = [wide[j, pl.ds(head, 16, stride=32), :] for j in range(4)]
            rows = jnp.concatenate(rows, axis=1).astype(jnp.bfloat16)
            value = jnp.dot(rows, up[head], preferred_element_type=jnp.float32)
            values[flow, 0, 0, :, 128 * i : 128 * i + 128] = value.astype(jnp.bfloat16)
        forward(flow, 0)

    loads[2].wait()
    for slot in range(slots):
        for flow in range(2):
            if slot:
                (a_copy(flow, slot - 1) if slot < 4 else b_copy(flow, slot - 4)).wait_recv()
                forward(flow, slot)
        if slot % 4 != 3:
            continue
        db = slot // 4
        for flow in range(2):
            for da in range(4):
                sib_copy(flow, 4 * db + da).wait_recv()
            left = values[flow, 4 * db : 4 * db + 4].reshape(128, 2048)
            term = lax.dot_general(
                left, weight[:, 2048 * flow : 2048 * flow + 2048],
                (((1,), (1,)), ((), ())), preferred_element_type=jnp.float32)
            for da in range(4):
                ua, ub = (4 - da, 4 - db) if flow == 0 else (da, db)
                origins = (
                    (((a + ua) % 4) * a_step + ((b + ub) % 4) * b_step) * 2 + core,
                    (((b + ua) % 4) * b_step + ((a + ub) % 4) * a_step) * 2 + 1 - core,
                )
                for which, origin in enumerate(origins):
                    at = 16 * (2 * da + which)
                    place = pl.ds(pl.multiple_of(origin * 16, 16), 16)
                    for i in range(2):
                        sums[i, place] += term[at : at + 16, 128 * i : 128 * i + 128]

    def share(d, s):
        return jnp.concatenate(
            [sums[i, pl.ds(4 * d + s, 32, stride=16), :] for i in range(2)], axis=1)

    gives = []
    for d in (1, 2, 3):
        for s in range(4):
            give[d - 1, s] = share(d, s).astype(jnp.bfloat16)
        copy = remote(give.at[d - 1], get.at[d - 1], give_send.at[d - 1], give_recv.at[d - 1],
                      plane(4 - d))
        copy.start()
        gives.append(copy)
    for copy in gives:
        copy.wait_recv()
    for s in range(4):
        total = share(0, s)
        for i in range(3):
            total = total + get[i, s].astype(jnp.float32)
        out_ref[s] = total[:, :224].astype(jnp.bfloat16)

    for copy in takes + gives:
        copy.wait_send()
    for flow in range(2):
        for slot in range(slots):
            sib_copy(flow, slot).wait_send()
            if slot < 3:
                a_copy(flow, slot).wait_send()
            if slot < 12:
                b_copy(flow, slot).wait_send()


def project(mixed, up_weight, out_weight_t):
    dma = pltpu.SemaphoreType.DMA
    bf16, f32 = jnp.bfloat16, jnp.float32
    return pl.pallas_call(
        project_kernel,
        in_specs=[pl.BlockSpec(memory_space=pl.ANY)] * 3,
        out_specs=pl.BlockSpec(memory_space=pltpu.VMEM),
        out_shape=jax.ShapeDtypeStruct((4, 32, 224), bf16),
        scratch_shapes=[
            pltpu.VMEM((4, 4, 32, 512), bf16),
            pltpu.VMEM((4, 512, 128), f32),
            pltpu.VMEM((32, 512, 128), bf16),
            pltpu.VMEM((256, 4096), bf16),
            pltpu.VMEM((2, slots, 2, 16, 2048), bf16),
            pltpu.VMEM((2, 512, 128), f32),
            pltpu.VMEM((3, 4, 32, 256), bf16),
            pltpu.VMEM((3, 4, 32, 256), bf16),
            dma((3,)),
            dma((3,)),
            dma((3,)),
            dma((2, slots)),
            dma((2, slots)),
            dma((2, 3)),
            dma((2, 12)),
            dma((2, slots)),
            dma((3,)),
            dma((3,)),
        ],
        compiler_params=pltpu.CompilerParams(
            collective_id=1, has_side_effects=True, vmem_limit_bytes=40 * 2**20
        ),
        cost_estimate=pl.CostEstimate(
            flops=1_100_000_000, bytes_accessed=8_000_000, transcendentals=0
        ),
    )(mixed, up_weight, out_weight_t)


def per_device(queries, top_rows, lengths, span_map, latent_cache, up_weight, out_weight):
    devices = lax.axis_size("ctx")
    steps, heads = queries.shape[1:3]
    local_rows = latent_cache.shape[1]
    width = local_rows // 2
    ahead = jnp.arange(steps, dtype=jnp.int32) - steps + 1
    limits = lengths[:, None] + ahead[None, :]
    stored = stored_index(top_rows, limits, span_map, width)[0]
    bias = pl.pallas_call(
        mask_kernel,
        out_shape=jax.ShapeDtypeStruct((steps, 128, 128), jnp.bfloat16),
    )(stored)
    bias = bias.reshape(steps, devices, local_rows).transpose(1, 0, 2)
    bias = lax.all_to_all(bias, "ctx", split_axis=0, concat_axis=0, tiled=True)
    bias = jnp.pad(bias, ((0, 0), (0, 12), (0, 0)))

    query_t = jnp.swapaxes(queries, 2, 3)[0]
    cache_t = jnp.swapaxes(latent_cache, 1, 2)
    mixed = gather_attend(query_t, bias, cache_t)
    out = project(mixed.reshape(steps, heads, -1), up_weight, out_weight.T)
    return jnp.swapaxes(out, 0, 1)


def solution(mesh):
    return jax.shard_map(
        per_device,
        mesh=mesh,
        in_specs=(
            P(("req", "ctx"), None, None, None),
            P(("req", "ctx"), None, None),
            P(("req", "ctx")),
            P(),
            P("req", "ctx", None),
            P("req", None, None),
            P("req", "ctx"),
        ),
        out_specs=P("req", None, "ctx"),
        check_vma=False,
    )
```

```python
import functools

import jax
import jax.numpy as jnp
from jax import lax
from jax.experimental import pallas as pl
from jax.experimental.pallas import tpu as pltpu
from jax.sharding import PartitionSpec as P

score_scale = 192.0 ** (-0.5)
log2_scale = score_scale * 1.4426950408889634
masked = -1e30
lowest = -16384.0


MESH = pl.DeviceIdType.MESH
side = 4
slots = side * side
key_rows = 592
latent_rows = 512
part_rows = 528
ahead = 2


def attend_unit(keys, query):
    scores = lax.dot_general(
        query, keys, (((0,), (0,)), ((), ())), preferred_element_type=jnp.float32
    )
    top = jnp.max(scores, axis=1, keepdims=True) * log2_scale
    top = jnp.maximum(top, lowest).astype(jnp.bfloat16).astype(jnp.float32)
    weights = jnp.exp2(scores * log2_scale - top)
    total = jnp.sum(weights, axis=1, keepdims=True)
    mixed = lax.dot_general(
        weights.astype(jnp.bfloat16),
        keys[:latent_rows],
        (((1,), (1,)), ((), ())),
        preferred_element_type=jnp.float32,
    )
    mixed = jnp.swapaxes(mixed.astype(jnp.bfloat16), 0, 1)
    top = jnp.swapaxes(jnp.broadcast_to(top, (256, 128)), 0, 1)[0:16]
    total = jnp.swapaxes(jnp.broadcast_to(total, (256, 128)), 0, 1)[0:16]
    return mixed, stat_rows(top, total)


def stat_rows(top, total):
    row = lax.broadcasted_iota(jnp.int32, (16, 256), 0)
    high = total.astype(jnp.bfloat16).astype(jnp.float32)
    rows = jnp.where(row == 0, top, jnp.where(row == 1, high, total - high))
    return jnp.where(row < 3, rows, 0.0).astype(jnp.bfloat16)


def merge_weights(refs):
    stats = [ref[latent_rows:part_rows].astype(jnp.float32) for ref in refs]
    top = functools.reduce(jnp.maximum, [stat[0:1] for stat in stats])
    factors = [jnp.exp2(stat[0:1] - top) for stat in stats]
    total = sum(f * (stat[1:2] + stat[2:3]) for f, stat in zip(factors, stats))
    return top, factors, total


def merge(refs, out):
    top, factors, total = merge_weights(refs)

    def chunk(i, carry):
        rows = pl.ds(pl.multiple_of(i * 64, 64), 64)
        parts = [f * ref[rows].astype(jnp.float32) for f, ref in zip(factors, refs)]
        out[rows] = sum(parts[1:], parts[0]).astype(jnp.bfloat16)
        return carry

    lax.fori_loop(0, latent_rows // 64, chunk, 0)
    shape = (16, 256)
    out[latent_rows:part_rows] = stat_rows(
        jnp.broadcast_to(top, shape), jnp.broadcast_to(total, shape)
    )


def make_mask(span_ref, length_ref, rows_ref, line, place_in, mask_one, core, a, b):
    picks = rows_ref[...]
    block = picks // 256
    holder = jnp.zeros_like(block)
    for c in range(64):
        holder = jnp.where(block == c, span_ref[c], holder)
    place_in[...] = jnp.where(block >= 32, 256, 0) + picks % 256
    x, y = holder // 8, (holder // 2) % 4
    ea = (x * (1 - core) + y * core - a + 4) % 4
    eb = (y * (1 - core) + x * core - b + 4) % 4
    ec = (holder + core) % 2
    step = lax.broadcasted_iota(jnp.int32, picks.shape, 0)
    limit = length_ref[0] - 3 + step
    line[...] = jnp.where(picks < limit, 32 * ea + 16 * ec + 4 * eb + step, -1)

    def chunk(i, count):
        columns = pl.ds(pl.multiple_of(i * 512, 512), 512)
        for s in range(4):
            left = lax.broadcasted_iota(jnp.int32, (128, 512), 0) == line[s : s + 1, columns]
            right = lax.broadcasted_iota(jnp.int32, (512, 512), 0) == place_in[s : s + 1, columns]
            count += lax.dot_general(
                left.astype(jnp.float32).astype(jnp.bfloat16),
                right.astype(jnp.float32).astype(jnp.bfloat16),
                (((1,), (1,)), ((), ())), preferred_element_type=jnp.float32)
        return count

    count = lax.fori_loop(0, 4, chunk, jnp.zeros((128, 512), jnp.float32))
    bias = jnp.where(count > 0.5, 0.0, masked).astype(jnp.bfloat16)
    mask_one[...] = bias.reshape(4, 2, 16, 512)


def gather_attend_kernel(
    span_ref, length_ref, rows_ref, query_ref, cache_ref, out_ref,
    own, sib, kept, from_sib, ring_in, last_in, keys,
    line, place_in, mask_one, mask_mid, mask_two, mask_got, mask_own, mask_sib,
    one_send, one_recv, two_send, two_recv, three_send, three_recv,
    load_sem, key_sem, own_recv, sib_recv, a_send, b_send, sib_send,
    part_send, part_recv, ring_send, ring_recv, last_send, last_recv,
):
    me = lax.axis_index("ctx")
    core = me % 2
    chip = me // 2
    a_step = 4 - 3 * core
    b_step = 1 + 3 * core
    a = (chip // a_step) % 4
    b = (chip // b_step) % 4

    def device(da, db):
        return (((a + da + 4) % 4) * a_step + ((b + db + 4) % 4) * b_step) * 2 + core

    sibling = chip * 2 + 1 - core
    barrier = pltpu.get_barrier_semaphore()
    partners = [device(d, 0) for d in (1, 2, 3)] + [device(0, d) for d in (1, 2, 3)] + [sibling]
    for partner in partners:
        pl.semaphore_signal(barrier, inc=1, device_id={"ctx": partner}, device_id_type=MESH)

    def own_request(flow, slot):
        da, db = slot % 4, slot // 4
        if flow == 0:
            da, db = 4 - da, 4 - db
        return (((a + da) % 4) * a_step + ((b + db) % 4) * b_step) * 2 + core

    def sib_request(flow, slot):
        da, db = slot % 4, slot // 4
        if flow == 0:
            da, db = 4 - da, 4 - db
        return (((b + da) % 4) * b_step + ((a + db) % 4) * a_step) * 2 + 1 - core

    def key_copies(slot, place):
        copies = []
        for flow in range(2):
            for which, request in ((0, own_request(flow, slot)), (1, sib_request(flow, slot))):
                at = 2 * which + flow
                copies.append(pltpu.make_async_copy(
                    cache_ref.at[request], keys.at[place, at, pl.ds(0, 576)],
                    key_sem.at[place, at]))
        return copies

    def remote(src, dst, send, recv, target):
        return pltpu.make_async_remote_copy(
            src_ref=src, dst_ref=dst, send_sem=send, recv_sem=recv,
            device_id={"ctx": target}, device_id_type=MESH)

    body = pl.ds(0, 576)

    def a_copy(flow, da):
        return remote(own.at[flow, 0, body], own.at[flow, da, body],
                      a_send.at[flow, da - 1], own_recv.at[flow, da],
                      device(da if flow == 0 else 4 - da, 0))

    def b_copy(flow, slot):
        return remote(own.at[flow, slot, body], own.at[flow, slot + 4, body],
                      b_send.at[flow, slot], own_recv.at[flow, slot + 4],
                      device(0, 1 - 2 * flow))

    def sib_copy(flow, slot):
        return remote(own.at[flow, slot, body], sib.at[flow, slot, body],
                      sib_send.at[flow, slot], sib_recv.at[flow, slot], sibling)

    partial = pl.ds(0, part_rows)

    def part_copy(flow, slot):
        return remote(sib.at[flow, slot, partial], from_sib.at[flow, slot],
                      part_send.at[flow, slot], part_recv.at[flow, slot], sibling)

    def ring_copy(flow, slot):
        return remote(kept.at[flow, slot], ring_in.at[flow, slot - 4],
                      ring_send.at[flow, slot - 4], ring_recv.at[flow, slot - 4],
                      device(0, 1 - 2 * flow))

    def last_copy(flow, da):
        return remote(kept.at[flow, da], last_in.at[flow, da - 1],
                      last_send.at[flow, da - 1], last_recv.at[flow, da - 1],
                      device(-da if flow == 0 else da - 4, 0))

    loads = [
        pltpu.make_async_copy(
            query_ref.at[2 * flow + half],
            own.at[flow, 0, body, pl.ds(128 * half, 128)],
            load_sem.at[flow, half])
        for flow in range(2) for half in range(2)
    ]
    for copy in loads:
        copy.start()
    for copy in key_copies(0, 0):
        copy.start()

    make_mask(span_ref, length_ref, rows_ref, line, place_in, mask_one, core, a, b)

    row = lax.broadcasted_iota(jnp.int32, (16, 256), 0)
    step = lax.broadcasted_iota(jnp.int32, (16, 256), 1) // 128
    for flow in range(2):

        def fill(slot, carry):
            da = slot % 4 if flow == 0 else (4 - slot % 4) % 4
            hot = jnp.where(row == step + 2 * flow + 4 * da, 1.0, 0.0).astype(jnp.bfloat16)
            own[flow, slot, 576:key_rows] = hot
            sib[flow, slot, 576:key_rows] = hot
            return carry

        lax.fori_loop(0, slots, fill, 0)
    for copy in loads:
        copy.wait()
    pl.semaphore_wait(barrier, len(partners))

    ones = [remote(mask_one.at[d], mask_mid.at[d], one_send.at[d - 1], one_recv.at[d - 1],
                   device(d, 0)) for d in (1, 2, 3)]
    for copy in ones:
        copy.start()
    for flow in range(2):
        b_copy(flow, 0).start()
        for da in (1, 2, 3):
            a_copy(flow, da).start()
        sib_copy(flow, 0).start()
    for copy in ones:
        copy.wait_recv()
    for which in range(2):
        lists = [mask_one[0, which].astype(jnp.float32)]
        lists += [mask_mid[d, which].astype(jnp.float32) for d in (1, 2, 3)]
        for eb in range(4):
            rows = [part[4 * eb : 4 * eb + 4] for part in lists]
            mask_two[eb, which] = jnp.concatenate(rows, axis=0).astype(jnp.bfloat16)
    twos = [remote(mask_two.at[d], mask_got.at[d], two_send.at[d - 1], two_recv.at[d - 1],
                   device(0, d)) for d in (1, 2, 3)]
    for copy in twos:
        copy.start()
    for slot in (1, 2, 3):
        for flow in range(2):
            a_copy(flow, slot).wait_recv()
            b_copy(flow, slot).start()
            sib_copy(flow, slot).start()
    for copy in twos:
        copy.wait_recv()
    mask_own[0] = mask_two[0, 0]
    mask_own[4] = mask_two[0, 1]
    for d in (1, 2, 3):
        mask_own[d] = mask_got[d, 0]
        mask_own[4 + d] = mask_got[d, 1]
    three = remote(mask_own.at[pl.ds(4, 4)], mask_sib, three_send, three_recv, sibling)
    three.start()
    three.wait_recv()

    def combine(slot):
        for flow in range(2):
            part_copy(flow, slot).wait_recv()

        @pl.when(slot < 8)
        def _():
            for flow in range(2):
                merge([kept.at[flow, slot], from_sib.at[flow, slot]], kept.at[flow, slot])
                ring_copy(flow, slot).start()

        @pl.when(slot >= 8)
        def _():
            for flow in range(2):
                ring_copy(flow, slot - 4).wait_recv()
                merge([kept.at[flow, slot], from_sib.at[flow, slot], ring_in.at[flow, slot - 8]],
                      kept.at[flow, slot])
                ring_copy(flow, slot).start()

    def iteration(slot, carry):
        place = slot % 2

        @pl.when((slot >= 4 - ahead) & (slot < slots - ahead))
        def _():
            for flow in range(2):
                b_copy(flow, slot + ahead - 4).wait_recv()

        @pl.when((slot >= 4 - ahead) & (slot < 12 - ahead))
        def _():
            for flow in range(2):
                b_copy(flow, slot + ahead).start()

        @pl.when((slot >= 4 - ahead) & (slot < slots - ahead))
        def _():
            for flow in range(2):
                sib_copy(flow, slot + ahead).start()

        @pl.when(slot < slots - 1)
        def _():
            for copy in key_copies(slot + 1, 1 - place):
                copy.start()

        for copy in key_copies(slot, place):
            copy.wait()
        for flow in range(2):
            db = slot // 4 if flow == 0 else (4 - slot // 4) % 4
            keys[place, flow, 576:key_rows] = mask_own[db]
            keys[place, 2 + flow, 576:key_rows] = mask_sib[db]

        for flow in range(2):
            mixed, stats = attend_unit(keys[place, flow], own[flow, slot])
            kept[flow, slot, 0:latent_rows] = mixed
            kept[flow, slot, latent_rows:part_rows] = stats

        for flow in range(2):
            sib_copy(flow, slot).wait_recv()
        results = [attend_unit(keys[place, 2 + flow], sib[flow, slot]) for flow in range(2)]
        for flow in range(2):
            mixed, stats = results[flow]
            sib[flow, slot, 0:latent_rows] = mixed
            sib[flow, slot, latent_rows:part_rows] = stats
            part_copy(flow, slot).start()

        @pl.when(slot > 4)
        def _():
            combine(slot - 1)

        return carry

    lax.fori_loop(0, slots, iteration, 0)
    combine(slots - 1)

    for da in (1, 2, 3, 0):
        for flow in range(2):
            part_copy(flow, da).wait_recv()
            ring_copy(flow, 12 + da).wait_recv()
            merge([kept.at[flow, da], from_sib.at[flow, da], ring_in.at[flow, 8 + da]],
                  kept.at[flow, da])
            if da:
                last_copy(flow, da).start()
    for flow in range(2):
        for da in (1, 2, 3):
            last_copy(flow, da).wait_recv()
        refs = [kept.at[flow, 0]] + [last_in.at[flow, i] for i in range(3)]
        top, factors, total = merge_weights(refs)
        scale = 1.0 / total
        for i in range(latent_rows // 128):
            rows = pl.ds(128 * i, 128)
            parts = [f * scale * ref[rows].astype(jnp.float32) for f, ref in zip(factors, refs)]
            final = sum(parts[1:], parts[0]).astype(jnp.bfloat16)
            out_ref[flow, :, 128 * i : 128 * (i + 1)] = jnp.swapaxes(final, 0, 1)

    for flow in range(2):
        def drain(slot, carry):
            sib_copy(flow, slot).wait_send()
            part_copy(flow, slot).wait_send()

            @pl.when(slot < 12)
            def _():
                b_copy(flow, slot).wait_send()
                ring_copy(flow, slot + 4).wait_send()

            return carry

        lax.fori_loop(0, slots, drain, 0)
        for da in (1, 2, 3):
            a_copy(flow, da).wait_send()
            last_copy(flow, da).wait_send()
    for copy in ones + twos + [three]:
        copy.wait_send()


def gather_attend(span_map, lengths, top_rows, query_t, cache_t):
    dma = pltpu.SemaphoreType.DMA
    bf16 = jnp.bfloat16
    return pl.pallas_call(
        gather_attend_kernel,
        in_specs=[pl.BlockSpec(memory_space=pltpu.SMEM)] * 2
        + [pl.BlockSpec(memory_space=pltpu.VMEM)]
        + [pl.BlockSpec(memory_space=pl.ANY)] * 2,
        out_specs=pl.BlockSpec(memory_space=pltpu.VMEM),
        out_shape=jax.ShapeDtypeStruct((2, 256, latent_rows), bf16),
        scratch_shapes=[
            pltpu.VMEM((2, slots, key_rows, 256), bf16),
            pltpu.VMEM((2, slots, key_rows, 256), bf16),
            pltpu.VMEM((2, slots, part_rows, 256), bf16),
            pltpu.VMEM((2, slots, part_rows, 256), bf16),
            pltpu.VMEM((2, 12, part_rows, 256), bf16),
            pltpu.VMEM((2, 3, part_rows, 256), bf16),
            pltpu.VMEM((2, 4, key_rows, 512), bf16),
            pltpu.VMEM((4, 2048), jnp.int32),
            pltpu.VMEM((4, 2048), jnp.int32),
            pltpu.VMEM((4, 2, 16, 512), bf16),
            pltpu.VMEM((4, 2, 16, 512), bf16),
            pltpu.VMEM((4, 2, 16, 512), bf16),
            pltpu.VMEM((4, 2, 16, 512), bf16),
            pltpu.VMEM((8, 16, 512), bf16),
            pltpu.VMEM((4, 16, 512), bf16),
            dma((3,)),
            dma((3,)),
            dma((3,)),
            dma((3,)),
            dma,
            dma,
            dma((2, 2)),
            dma((2, 4)),
            dma((2, slots)),
            dma((2, slots)),
            dma((2, 3)),
            dma((2, 12)),
            dma((2, slots)),
            dma((2, slots)),
            dma((2, slots)),
            dma((2, 12)),
            dma((2, 12)),
            dma((2, 3)),
            dma((2, 3)),
        ],
        compiler_params=pltpu.CompilerParams(
            collective_id=0, has_side_effects=True, vmem_limit_bytes=58 * 2**20
        ),
        cost_estimate=pl.CostEstimate(
            flops=18_000_000_000, bytes_accessed=40_000_000, transcendentals=8_000_000
        ),
    )(span_map, lengths, top_rows, query_t, cache_t)


def project_kernel(
    mixed_ref, up_ref, out_weight_ref, out_ref,
    taken, wide, up, weight, values, sums, give, get,
    load_sem, take_send, take_recv, own_recv, sib_recv, a_send, b_send, sib_send,
    give_send, give_recv,
):
    me = lax.axis_index("ctx")
    group = lax.axis_index("req")
    core = me % 2
    chip = me // 2
    a_step = 4 - 3 * core
    b_step = 1 + 3 * core
    a = (chip // a_step) % 4
    b = (chip // b_step) % 4

    def device(da, db):
        return {"ctx": (((a + da) % 4) * a_step + ((b + db) % 4) * b_step) * 2 + core}

    def plane(d):
        return {"req": (group + d) % 4}

    sibling = {"ctx": chip * 2 + 1 - core}
    partners = [device(1, 0), device(2, 0), device(3, 0), device(0, 1), device(0, 3), sibling]
    partners += [plane(1), plane(2), plane(3)]
    barrier = pltpu.get_barrier_semaphore()
    for partner in partners:
        pl.semaphore_signal(barrier, inc=1, device_id=partner, device_id_type=MESH)

    def remote(src, dst, send, recv, target):
        return pltpu.make_async_remote_copy(
            src_ref=src, dst_ref=dst, send_sem=send, recv_sem=recv,
            device_id=target, device_id_type=MESH)

    def heads_of(z):
        return mixed_ref.at[:, pl.ds(pl.multiple_of(z * 32, 32), 32)]

    loads = [
        pltpu.make_async_copy(heads_of(group), taken.at[0], load_sem.at[0]),
        pltpu.make_async_copy(up_ref, up, load_sem.at[1]),
        pltpu.make_async_copy(out_weight_ref, weight.at[pl.ds(0, 224)], load_sem.at[2]),
    ]
    for copy in loads:
        copy.start()
    pl.semaphore_wait(barrier, len(partners))
    takes = [
        remote(heads_of((group + d) % 4), taken.at[d], take_send.at[d - 1],
               take_recv.at[d - 1], plane(d))
        for d in (1, 2, 3)
    ]
    for copy in takes:
        copy.start()

    weight[224:256] = jnp.zeros((32, 4096), jnp.bfloat16)
    sums[...] = jnp.zeros_like(sums)
    loads[0].wait()
    loads[1].wait()
    for d in range(4):
        if d:
            takes[d - 1].wait_recv()
        for s in range(4):
            rows = taken[d, s].astype(jnp.float32)
            for i in range(4):
                wide[i, 128 * d + 32 * s : 128 * d + 32 * s + 32] = rows[:, 128 * i : 128 * i + 128]

    def a_copy(flow, da):
        return remote(values.at[flow, 0, 0], values.at[flow, da, 0],
                      a_send.at[flow, da - 1], own_recv.at[flow, da],
                      device(da if flow == 0 else 4 - da, 0))

    def b_copy(flow, slot):
        return remote(values.at[flow, slot, 0], values.at[flow, slot + 4, 0],
                      b_send.at[flow, slot], own_recv.at[flow, slot + 4],
                      device(0, 1 if flow == 0 else 3))

    def sib_copy(flow, slot):
        return remote(values.at[flow, slot, 0], values.at[flow, slot, 1],
                      sib_send.at[flow, slot], sib_recv.at[flow, slot], sibling)

    def forward(flow, slot):
        if slot < 12:
            b_copy(flow, slot).start()
        if slot == 0:
            for da in (1, 2, 3):
                a_copy(flow, da).start()
        sib_copy(flow, slot).start()

    for flow in range(2):
        for i in range(16):
            head = 16 * flow + i
            rows = [wide[j, pl.ds(head, 16, stride=32), :] for j in range(4)]
            rows = jnp.concatenate(rows, axis=1).astype(jnp.bfloat16)
            value = jnp.dot(rows, up[head], preferred_element_type=jnp.float32)
            values[flow, 0, 0, :, 128 * i : 128 * i + 128] = value.astype(jnp.bfloat16)
        forward(flow, 0)

    loads[2].wait()
    for slot in range(slots):
        for flow in range(2):
            if slot:
                (a_copy(flow, slot) if slot < 4 else b_copy(flow, slot - 4)).wait_recv()
                forward(flow, slot)
        if slot % 4 != 3:
            continue
        db = slot // 4
        for flow in range(2):
            for da in range(4):
                sib_copy(flow, 4 * db + da).wait_recv()
            left = values[flow, 4 * db : 4 * db + 4].reshape(128, 2048)
            term = lax.dot_general(
                left, weight[:, 2048 * flow : 2048 * flow + 2048],
                (((1,), (1,)), ((), ())), preferred_element_type=jnp.float32)
            for da in range(4):
                ua, ub = (4 - da, 4 - db) if flow == 0 else (da, db)
                origins = (
                    (((a + ua) % 4) * a_step + ((b + ub) % 4) * b_step) * 2 + core,
                    (((b + ua) % 4) * b_step + ((a + ub) % 4) * a_step) * 2 + 1 - core,
                )
                for which, origin in enumerate(origins):
                    at = 16 * (2 * da + which)
                    place = pl.ds(pl.multiple_of(origin * 16, 16), 16)
                    for i in range(2):
                        sums[i, place] += term[at : at + 16, 128 * i : 128 * i + 128]

    def share(d, s):
        return jnp.concatenate(
            [sums[i, pl.ds(4 * d + s, 32, stride=16), :] for i in range(2)], axis=1)

    gives = []
    for d in (1, 2, 3):
        for s in range(4):
            give[d - 1, s] = share(d, s).astype(jnp.bfloat16)
        copy = remote(give.at[d - 1], get.at[d - 1], give_send.at[d - 1], give_recv.at[d - 1],
                      plane(4 - d))
        copy.start()
        gives.append(copy)
    for copy in gives:
        copy.wait_recv()
    for s in range(4):
        total = share(0, s)
        for i in range(3):
            total = total + get[i, s].astype(jnp.float32)
        out_ref[s] = total[:, :224].astype(jnp.bfloat16)

    for copy in takes + gives:
        copy.wait_send()
    for flow in range(2):
        for slot in range(slots):
            sib_copy(flow, slot).wait_send()
            if 0 < slot < 4:
                a_copy(flow, slot).wait_send()
            if slot < 12:
                b_copy(flow, slot).wait_send()


def project(mixed, up_weight, out_weight_t):
    dma = pltpu.SemaphoreType.DMA
    bf16, f32 = jnp.bfloat16, jnp.float32
    return pl.pallas_call(
        project_kernel,
        in_specs=[pl.BlockSpec(memory_space=pl.ANY)] * 3,
        out_specs=pl.BlockSpec(memory_space=pltpu.VMEM),
        out_shape=jax.ShapeDtypeStruct((4, 32, 224), bf16),
        scratch_shapes=[
            pltpu.VMEM((4, 4, 32, 512), bf16),
            pltpu.VMEM((4, 512, 128), f32),
            pltpu.VMEM((32, 512, 128), bf16),
            pltpu.VMEM((256, 4096), bf16),
            pltpu.VMEM((2, slots, 2, 16, 2048), bf16),
            pltpu.VMEM((2, 512, 128), f32),
            pltpu.VMEM((3, 4, 32, 256), bf16),
            pltpu.VMEM((3, 4, 32, 256), bf16),
            dma((3,)),
            dma((3,)),
            dma((3,)),
            dma((2, slots)),
            dma((2, slots)),
            dma((2, 3)),
            dma((2, 12)),
            dma((2, slots)),
            dma((3,)),
            dma((3,)),
        ],
        compiler_params=pltpu.CompilerParams(
            collective_id=1, has_side_effects=True, vmem_limit_bytes=40 * 2**20
        ),
        cost_estimate=pl.CostEstimate(
            flops=1_100_000_000, bytes_accessed=8_000_000, transcendentals=0
        ),
    )(mixed, up_weight, out_weight_t)


def per_device(queries, top_rows, lengths, span_map, latent_cache, up_weight, out_weight):
    steps, heads = queries.shape[1:3]
    query_t = jnp.swapaxes(queries, 2, 3)[0]
    cache_t = jnp.swapaxes(latent_cache, 1, 2)
    mixed = gather_attend(span_map, lengths, top_rows[0], query_t, cache_t)
    out = project(mixed.reshape(steps, heads, -1), up_weight, out_weight.T)
    return jnp.swapaxes(out, 0, 1)


def solution(mesh):
    return jax.shard_map(
        per_device,
        mesh=mesh,
        in_specs=(
            P(("req", "ctx"), None, None, None),
            P(("req", "ctx"), None, None),
            P(("req", "ctx")),
            P(),
            P("req", "ctx", None),
            P("req", None, None),
            P("req", "ctx"),
        ),
        out_specs=P("req", None, "ctx"),
        check_vma=False,
    )
```

```python
import functools

import jax
import jax.numpy as jnp
from jax import lax
from jax.experimental import pallas as pl
from jax.experimental.pallas import tpu as pltpu
from jax.sharding import PartitionSpec as P

score_scale = 192.0 ** (-0.5)
log2_scale = score_scale * 1.4426950408889634
masked = -1e30
lowest = -16384.0


MESH = pl.DeviceIdType.MESH
side = 4
slots = side * side
key_rows = 592
latent_rows = 512
ahead = 2


def attend_unit(keys, query):
    scores = lax.dot_general(
        query, keys, (((0,), (0,)), ((), ())), preferred_element_type=jnp.float32
    )
    top = jnp.max(scores, axis=1, keepdims=True) * log2_scale
    top = jnp.maximum(top, lowest).astype(jnp.bfloat16).astype(jnp.float32)
    weights = jnp.exp2(scores * log2_scale - top)
    total = jnp.sum(weights, axis=1, keepdims=True)
    mixed = lax.dot_general(
        weights.astype(jnp.bfloat16),
        keys[:latent_rows],
        (((1,), (1,)), ((), ())),
        preferred_element_type=jnp.float32,
    )
    return mixed.astype(jnp.bfloat16), top, total


def pack_stats(top, total):
    lane = lax.broadcasted_iota(jnp.int32, (256, 128), 1)
    high = total.astype(jnp.bfloat16).astype(jnp.float32)
    packed = jnp.where(lane == 0, top, jnp.where(lane == 1, high, total - high))
    return packed.astype(jnp.bfloat16)


def merge_stats(stats):
    top = functools.reduce(jnp.maximum, [t for t, _ in stats])
    return top, sum(jnp.exp2(t - top) * l for t, l in stats)


def roll_rows(block, count):
    count = count % 8
    if count == 0:
        return block
    return jnp.concatenate([block[8 - count :], block[: 8 - count]], axis=0)


def make_mask(span_ref, length_ref, rows_ref, line, place_in, mask_one, core, a, b):
    picks = rows_ref[...]
    block = picks // 256
    holder = jnp.zeros_like(block)
    for c in range(64):
        holder = jnp.where(block == c, span_ref[c], holder)
    place_in[...] = jnp.where(block >= 32, 256, 0) + picks % 256
    x, y = holder // 8, (holder // 2) % 4
    ea = (x * (1 - core) + y * core - a + 4) % 4
    eb = (y * (1 - core) + x * core - b + 4) % 4
    ec = (holder + core) % 2
    step = lax.broadcasted_iota(jnp.int32, picks.shape, 0)
    limit = length_ref[0] - 3 + step
    line[...] = jnp.where(picks < limit, 32 * ea + 16 * ec + 4 * eb + step, -1)

    def chunk(i, count):
        columns = pl.ds(pl.multiple_of(i * 512, 512), 512)
        for s in range(4):
            left = lax.broadcasted_iota(jnp.int32, (128, 512), 0) == line[s : s + 1, columns]
            right = lax.broadcasted_iota(jnp.int32, (512, 512), 0) == place_in[s : s + 1, columns]
            count += lax.dot_general(
                left.astype(jnp.float32).astype(jnp.bfloat16),
                right.astype(jnp.float32).astype(jnp.bfloat16),
                (((1,), (1,)), ((), ())), preferred_element_type=jnp.float32)
        return count

    count = lax.fori_loop(0, 4, chunk, jnp.zeros((128, 512), jnp.float32))
    bias = jnp.where(count > 0.5, 0.0, masked).astype(jnp.bfloat16)
    mask_one[...] = bias.reshape(4, 2, 16, 512)


def gather_attend_kernel(
    span_ref, length_ref, rows_ref, query_ref, cache_ref, up_ref, out_ref, far_up,
    own, sib, kept, to_sib, from_sib, own_stat, keys,
    line, place_in, mask_one, mask_mid, mask_two, mask_got, mask_own, mask_sib,
    stats, stats_a, stats_mid, stats_b, factor, up, wide, partial, ring_in, last_out, last_in,
    one_send, one_recv, two_send, two_recv, three_send, three_recv,
    load_sem, key_sem, own_recv, sib_recv, a_send, b_send, sib_send,
    part_send, part_recv, credit, far_send, far_recv, pass_send, pass_recv, up_sem,
    stat_a_send, stat_a_recv, stat_b_send, stat_b_recv,
    ring_send, ring_recv, last_send, last_recv,
):
    me = lax.axis_index("ctx")
    core = me % 2
    chip = me // 2
    a_step = 4 - 3 * core
    b_step = 1 + 3 * core
    a = (chip // a_step) % 4
    b = (chip // b_step) % 4

    def device(da, db):
        return (((a + da + 4) % 4) * a_step + ((b + db + 4) % 4) * b_step) * 2 + core

    group = lax.axis_index("req")
    sibling = chip * 2 + 1 - core
    barrier = pltpu.get_barrier_semaphore()
    partners = [device(d, 0) for d in (1, 2, 3)] + [device(0, d) for d in (1, 2, 3)] + [sibling]
    partners = [{"ctx": partner} for partner in partners]
    partners += [{"req": (group + 1) % 4}, {"req": (group + 3) % 4}]
    for partner in partners:
        pl.semaphore_signal(barrier, inc=1, device_id=partner, device_id_type=MESH)

    def own_request(flow, slot):
        da, db = slot % 4, slot // 4
        if flow == 0:
            da, db = 4 - da, 4 - db
        return (((a + da) % 4) * a_step + ((b + db) % 4) * b_step) * 2 + core

    def sib_request(flow, slot):
        da, db = slot % 4, slot // 4
        if flow == 0:
            da, db = 4 - da, 4 - db
        return (((b + da) % 4) * b_step + ((a + db) % 4) * a_step) * 2 + 1 - core

    def key_copies(slot, place):
        copies = []
        for flow in range(2):
            for which, request in ((0, own_request(flow, slot)), (1, sib_request(flow, slot))):
                at = 2 * which + flow
                copies.append(pltpu.make_async_copy(
                    cache_ref.at[request], keys.at[place, at, pl.ds(0, 576)],
                    key_sem.at[place, at]))
        return copies

    def remote(src, dst, send, recv, target):
        return pltpu.make_async_remote_copy(
            src_ref=src, dst_ref=dst, send_sem=send, recv_sem=recv,
            device_id={"ctx": target}, device_id_type=MESH)

    body = pl.ds(0, 576)

    def a_copy(flow, da):
        return remote(own.at[flow, 0, body], own.at[flow, da, body],
                      a_send.at[flow, da - 1], own_recv.at[flow, da],
                      device(da if flow == 0 else 4 - da, 0))

    def b_copy(flow, slot):
        return remote(own.at[flow, slot, body], own.at[flow, slot + 4, body],
                      b_send.at[flow, slot], own_recv.at[flow, slot + 4],
                      device(0, 1 - 2 * flow))

    def sib_copy(flow, slot):
        return remote(own.at[flow, slot, body], sib.at[flow, slot, body],
                      sib_send.at[flow, slot], sib_recv.at[flow, slot], sibling)

    def part_copy(flow, slot):
        return remote(to_sib.at[flow, slot % 2], from_sib.at[flow, slot % 4],
                      part_send.at[flow, slot % 2], part_recv.at[flow, slot % 4], sibling)

    def far_copy(piece):
        quarter = pl.ds(16 * core + 8 * (piece % 2), 8)
        if piece < 4:
            src, ahead_z = up_ref.at[quarter], (1 if piece < 2 else 3)
        else:
            src = far_up.at[0 if piece == 4 else 1, quarter]
            ahead_z = 1 if piece == 4 else 3
        return pltpu.make_async_remote_copy(
            src_ref=src, dst_ref=far_up.at[piece // 2, quarter],
            send_sem=far_send.at[piece], recv_sem=far_recv.at[piece],
            device_id={"req": (group + ahead_z) % 4}, device_id_type=MESH)

    def pass_copy(piece):
        quarter = far_up.at[piece // 2, pl.ds(16 * core + 8 * (piece % 2), 8)]
        return remote(quarter, quarter, pass_send.at[piece], pass_recv.at[piece], sibling)

    def stat_a_copy(d):
        return remote(stats, stats_a.at[d - 1], stat_a_send.at[d - 1], stat_a_recv.at[d - 1],
                      device(d, 0))

    def stat_b_copy(d):
        return remote(stats_mid, stats_b.at[d - 1], stat_b_send.at[d - 1],
                      stat_b_recv.at[d - 1], device(0, d))

    def ring_copy(flow, gi, db):
        return remote(partial.at[flow, gi, db], ring_in.at[flow, gi, db - 1],
                      ring_send.at[flow, gi, db - 1], ring_recv.at[flow, gi, db - 1],
                      device(0, 1 - 2 * flow))

    def last_copy(flow, da):
        return remote(last_out.at[flow, da - 1], last_in.at[flow, da - 1],
                      last_send.at[flow, da - 1], last_recv.at[flow, da - 1],
                      device(-da if flow == 0 else da - 4, 0))

    loads = [
        pltpu.make_async_copy(
            query_ref.at[2 * flow + half],
            own.at[flow, 0, body, pl.ds(128 * half, 128)],
            load_sem.at[flow, half])
        for flow in range(2) for half in range(2)
    ]
    for copy in loads:
        copy.start()
    for copy in key_copies(0, 0):
        copy.start()

    make_mask(span_ref, length_ref, rows_ref, line, place_in, mask_one, core, a, b)

    row = lax.broadcasted_iota(jnp.int32, (16, 256), 0)
    step = lax.broadcasted_iota(jnp.int32, (16, 256), 1) // 128
    for flow in range(2):

        def fill(slot, carry):
            da = slot % 4 if flow == 0 else (4 - slot % 4) % 4
            hot = jnp.where(row == step + 2 * flow + 4 * da, 1.0, 0.0).astype(jnp.bfloat16)
            own[flow, slot, 576:key_rows] = hot
            sib[flow, slot, 576:key_rows] = hot
            return carry

        lax.fori_loop(0, slots, fill, 0)
    for copy in loads:
        copy.wait()
    pl.semaphore_wait(barrier, len(partners))

    ones = [remote(mask_one.at[d], mask_mid.at[d], one_send.at[d - 1], one_recv.at[d - 1],
                   device(d, 0)) for d in (1, 2, 3)]
    for copy in ones:
        copy.start()
    for piece in (0, 3, 1, 2):
        far_copy(piece).start()
    for flow in range(2):
        b_copy(flow, 0).start()
        for da in (1, 2, 3):
            a_copy(flow, da).start()
        sib_copy(flow, 0).start()
    for copy in ones:
        copy.wait_recv()
    for which in range(2):
        lists = [mask_one[0, which].astype(jnp.float32)]
        lists += [mask_mid[d, which].astype(jnp.float32) for d in (1, 2, 3)]
        for eb in range(4):
            rows = [part[4 * eb : 4 * eb + 4] for part in lists]
            mask_two[eb, which] = jnp.concatenate(rows, axis=0).astype(jnp.bfloat16)
    twos = [remote(mask_two.at[d], mask_got.at[d], two_send.at[d - 1], two_recv.at[d - 1],
                   device(0, d)) for d in (1, 2, 3)]
    for copy in twos:
        copy.start()
    for slot in (1, 2, 3):
        for flow in range(2):
            a_copy(flow, slot).wait_recv()
            b_copy(flow, slot).start()
            sib_copy(flow, slot).start()
    for copy in twos:
        copy.wait_recv()
    mask_own[0] = mask_two[0, 0]
    mask_own[4] = mask_two[0, 1]
    for d in (1, 2, 3):
        mask_own[d] = mask_got[d, 0]
        mask_own[4 + d] = mask_got[d, 1]
    three = remote(mask_own.at[pl.ds(4, 4)], mask_sib, three_send, three_recv, sibling)
    three.start()
    three.wait_recv()

    row8 = lax.broadcasted_iota(jnp.int32, (8, 128), 0)

    def combine(slot):
        db, da = slot // 4, slot % 4
        for flow in range(2):
            part_copy(flow, slot).wait_recv()
            for half in range(2):
                rows = slice(128 * half, 128 * half + 128)
                got = from_sib[flow, slot % 4, rows, 512:640].astype(jnp.float32)
                top_1, total_1 = own_stat[slot % 2, flow, 0, rows], own_stat[slot % 2, flow, 1, rows]
                top_2 = jnp.broadcast_to(got[:, 0:1], (128, 128))
                total_2 = jnp.broadcast_to(got[:, 1:2] + got[:, 2:3], (128, 128))
                top = jnp.maximum(top_1, top_2)
                factor_1, factor_2 = jnp.exp2(top_1 - top), jnp.exp2(top_2 - top)
                total = factor_1 * total_1 + factor_2 * total_2
                for i in range(4):
                    lanes = slice(128 * i, 128 * i + 128)
                    value = factor_1 * kept[flow, slot, rows, lanes].astype(jnp.float32)
                    value += factor_2 * from_sib[flow, slot % 4, rows, lanes].astype(jnp.float32)
                    kept[flow, slot, rows, lanes] = value.astype(jnp.bfloat16)
                for i, value in enumerate((top, total)):
                    value = jnp.swapaxes(value, 0, 1)[0:8]
                    stats[i, flow, db] = jnp.where(
                        row8 == 2 * da + half, value, stats[i, flow, db])

    def give_credit():
        pl.semaphore_signal(credit, inc=1, device_id={"ctx": sibling}, device_id_type=MESH)

    def iteration(slot, carry):
        place = slot % 2

        @pl.when((slot >= 4 - ahead) & (slot < slots - ahead))
        def _():
            for flow in range(2):
                b_copy(flow, slot + ahead - 4).wait_recv()

        @pl.when((slot >= 4 - ahead) & (slot < 12 - ahead))
        def _():
            for flow in range(2):
                b_copy(flow, slot + ahead).start()

        @pl.when((slot >= 4 - ahead) & (slot < slots - ahead))
        def _():
            for flow in range(2):
                sib_copy(flow, slot + ahead).start()

        @pl.when(slot < slots - 1)
        def _():
            for copy in key_copies(slot + 1, 1 - place):
                copy.start()

        for copy in key_copies(slot, place):
            copy.wait()
        for flow in range(2):
            db = slot // 4 if flow == 0 else (4 - slot // 4) % 4
            keys[place, flow, 576:key_rows] = mask_own[db]
            keys[place, 2 + flow, 576:key_rows] = mask_sib[db]

        results = [attend_unit(keys[place, flow], own[flow, slot]) for flow in range(2)]
        for flow in range(2):
            mixed, top, total = results[flow]
            kept[flow, slot] = mixed
            own_stat[place, flow, 0] = jnp.broadcast_to(top, (256, 128))
            own_stat[place, flow, 1] = jnp.broadcast_to(total, (256, 128))

        for flow in range(2):
            sib_copy(flow, slot).wait_recv()

        @pl.when(slot >= 2)
        def _():
            for flow in range(2):
                part_copy(flow, slot).wait_send()

        results = [attend_unit(keys[place, 2 + flow], sib[flow, slot]) for flow in range(2)]
        for flow in range(2):
            mixed, top, total = results[flow]
            to_sib[flow, place, :, 0:512] = mixed
            to_sib[flow, place, :, 512:640] = pack_stats(top, total)

        @pl.when(slot >= 4)
        def _():
            pl.semaphore_wait(credit, 1)

        for flow in range(2):
            part_copy(flow, slot).start()

        @pl.when(slot > 0)
        def _():
            combine(slot - 1)

        @pl.when((slot > 0) & (slot < 13))
        def _():
            give_credit()

        @pl.when(slot == 8)
        def _():
            for piece in (0, 3):
                far_copy(piece).wait_recv()
                pass_copy(piece).start()
            far_copy(4).start()
            far_copy(5).start()

        @pl.when(slot == 12)
        def _():
            for piece in (1, 2):
                far_copy(piece).wait_recv()
                pass_copy(piece).start()

        return carry

    stats[...] = jnp.zeros_like(stats)
    lax.fori_loop(0, slots, iteration, 0)

    def up_copy(gi):
        src = up_ref if gi == 0 else far_up.at[gi - 1]
        return pltpu.make_async_copy(src, up.at[gi % 2], up_sem.at[gi % 2])

    up_copy(0).start()
    combine(slots - 1)
    for d in (1, 2, 3):
        stat_a_copy(d).start()
    for piece in (0, 1):
        pass_copy(piece).wait_recv()
    up_copy(1).start()
    for d in (1, 2, 3):
        stat_a_copy(d).wait_recv()
    for flow in range(2):
        for db in range(4):
            parts = [(stats[0, flow, db], stats[1, flow, db])]
            for d in (1, 2, 3):
                turn = 2 * d if flow == 0 else -2 * d
                parts.append(tuple(roll_rows(stats_a[d - 1, i, flow, db], turn) for i in range(2)))
            stats_mid[0, flow, db], stats_mid[1, flow, db] = merge_stats(parts)
    for d in (1, 2, 3):
        stat_b_copy(d).start()
    for piece in (4, 5):
        far_copy(piece).wait_recv()
        pass_copy(piece).start()
    for d in (1, 2, 3):
        stat_b_copy(d).wait_recv()
    for flow in range(2):
        for db in range(4):
            parts = [(stats_mid[0, flow, db], stats_mid[1, flow, db])]
            for d in (1, 2, 3):
                other = (db - d) % 4 if flow == 0 else (db + d) % 4
                parts.append((stats_b[d - 1, 0, flow, other], stats_b[d - 1, 1, flow, other]))
            top, total = merge_stats(parts)
            value = jnp.exp2(stats[0, flow, db] - top) / total
            turned = value
            for z in (1, 2, 3):
                shifted = jnp.concatenate([value[:, 32 * z :], value[:, : 32 * z]], axis=1)
                turned = jnp.where(group == z, shifted, turned)
            factor[32 * flow + 8 * db : 32 * flow + 8 * db + 8] = turned

    def chain(gi, db):
        for flow in range(2):
            ring_copy(flow, gi, db - 1).wait_recv()
            value = partial[flow, gi, db].astype(jnp.float32)
            value += ring_in[flow, gi, db - 2].astype(jnp.float32)
            partial[flow, gi, db] = value.astype(jnp.bfloat16)
            ring_copy(flow, gi, db).start()

    ahead_of = (0, 3, 1, 2)
    for gi in range(4):
        up_copy(gi).wait()
        first_head = pl.multiple_of(32 * ((group + ahead_of[gi]) % 4), 32)
        for flow in range(2):

            def fill_wide(slot, carry):
                for half in range(2):
                    rows = pl.ds(pl.multiple_of(128 * half + first_head, 32), 32)
                    value = kept[flow, slot, rows].astype(jnp.float32)
                    at = pl.ds(pl.multiple_of(32 * (32 * flow + 2 * slot + half), 32), 32)
                    for i in range(4):
                        wide[i, at] = value[:, 128 * i : 128 * i + 128]
                return carry

            lax.fori_loop(0, slots, fill_wide, 0)
        weight = factor[...]
        for hj in range(16):
            values = []
            for head in (hj, 16 + hj):
                rows = [wide[i, pl.ds(head, 64, stride=32), :] for i in range(4)]
                rows = jnp.concatenate(rows, axis=1).astype(jnp.bfloat16)
                value = jnp.dot(rows, up[gi % 2, head], preferred_element_type=jnp.float32)
                lane = 32 * ahead_of[gi] + head
                values.append(value * weight[:, lane : lane + 1])
            for flow in range(2):
                for db in range(4):
                    at = 32 * flow + 8 * db
                    both = jnp.concatenate([value[at : at + 8] for value in values], axis=0)
                    partial[flow, gi, db, :, 128 * hj : 128 * hj + 128] = both.astype(jnp.bfloat16)
        for flow in range(2):
            ring_copy(flow, gi, 1).start()
        if gi == 0:
            for piece in (2, 3):
                pass_copy(piece).wait_recv()
            up_copy(2).start()
        if gi == 1:
            for piece in (4, 5):
                pass_copy(piece).wait_recv()
            up_copy(3).start()
        if gi >= 1:
            chain(gi - 1, 2)
        if gi >= 2:
            chain(gi - 2, 3)
    chain(3, 2)
    chain(2, 3)
    chain(3, 3)

    whole = []
    for flow in range(2):
        ends = []
        for gi in range(4):
            ring_copy(flow, gi, 3).wait_recv()
            value = partial[flow, gi, 0].astype(jnp.float32)
            ends.append(value + ring_in[flow, gi, 2].astype(jnp.float32))

        def rows_of(da):
            picked = [end[8 * c + 2 * da : 8 * c + 2 * da + 2] for end in ends for c in range(2)]
            return jnp.concatenate(picked, axis=0)

        for da in (1, 2, 3):
            last_out[flow, da - 1] = rows_of(da).astype(jnp.bfloat16)
            last_copy(flow, da).start()
        whole.append(rows_of(0))
    for flow in range(2):
        for da in (1, 2, 3):
            last_copy(flow, da).wait_recv()
            whole[flow] = whole[flow] + last_in[flow, da - 1].astype(jnp.float32)
    for gi in range(4):
        picked = [whole[flow][4 * gi + 2 * c : 4 * gi + 2 * c + 2]
                  for c in range(2) for flow in range(2)]
        out_ref[gi] = jnp.concatenate(picked, axis=0)

    for flow in range(2):
        def drain(slot, carry):
            sib_copy(flow, slot).wait_send()

            @pl.when(slot < 12)
            def _():
                b_copy(flow, slot).wait_send()

            return carry

        lax.fori_loop(0, slots, drain, 0)
        for slot in (14, 15):
            part_copy(flow, slot).wait_send()
        for da in (1, 2, 3):
            a_copy(flow, da).wait_send()
            last_copy(flow, da).wait_send()
            for gi in range(4):
                ring_copy(flow, gi, da).wait_send()
    for piece in range(6):
        far_copy(piece).wait_send()
        pass_copy(piece).wait_send()
    for d in (1, 2, 3):
        stat_a_copy(d).wait_send()
        stat_b_copy(d).wait_send()
    for copy in ones + twos + [three]:
        copy.wait_send()


def gather_attend(span_map, lengths, top_rows, query_t, cache_t, up_weight):
    dma = pltpu.SemaphoreType.DMA
    bf16, f32 = jnp.bfloat16, jnp.float32
    return pl.pallas_call(
        gather_attend_kernel,
        in_specs=[pl.BlockSpec(memory_space=pltpu.SMEM)] * 2
        + [pl.BlockSpec(memory_space=pltpu.VMEM)]
        + [pl.BlockSpec(memory_space=pl.ANY)] * 3,
        out_specs=[pl.BlockSpec(memory_space=pltpu.VMEM), pl.BlockSpec(memory_space=pl.ANY)],
        out_shape=[
            jax.ShapeDtypeStruct((4, 8, 2048), f32),
            jax.ShapeDtypeStruct((3,) + up_weight.shape, bf16),
        ],
        scratch_shapes=[
            pltpu.VMEM((2, slots, key_rows, 256), bf16),
            pltpu.VMEM((2, slots, key_rows, 256), bf16),
            pltpu.VMEM((2, slots, 256, 512), bf16),
            pltpu.VMEM((2, 2, 256, 640), bf16),
            pltpu.VMEM((2, 4, 256, 640), bf16),
            pltpu.VMEM((2, 2, 2, 256, 128), f32),
            pltpu.VMEM((2, 4, key_rows, 512), bf16),
            pltpu.VMEM((4, 2048), jnp.int32),
            pltpu.VMEM((4, 2048), jnp.int32),
            pltpu.VMEM((4, 2, 16, 512), bf16),
            pltpu.VMEM((4, 2, 16, 512), bf16),
            pltpu.VMEM((4, 2, 16, 512), bf16),
            pltpu.VMEM((4, 2, 16, 512), bf16),
            pltpu.VMEM((8, 16, 512), bf16),
            pltpu.VMEM((4, 16, 512), bf16),
            pltpu.VMEM((2, 2, 4, 8, 128), f32),
            pltpu.VMEM((3, 2, 2, 4, 8, 128), f32),
            pltpu.VMEM((2, 2, 4, 8, 128), f32),
            pltpu.VMEM((3, 2, 2, 4, 8, 128), f32),
            pltpu.VMEM((64, 128), f32),
            pltpu.VMEM((2, 32, 512, 128), bf16),
            pltpu.VMEM((4, 2048, 128), f32),
            pltpu.VMEM((2, 4, 4, 16, 2048), bf16),
            pltpu.VMEM((2, 4, 3, 16, 2048), bf16),
            pltpu.VMEM((2, 3, 16, 2048), bf16),
            pltpu.VMEM((2, 3, 16, 2048), bf16),
            dma((3,)),
            dma((3,)),
            dma((3,)),
            dma((3,)),
            dma,
            dma,
            dma((2, 2)),
            dma((2, 4)),
            dma((2, slots)),
            dma((2, slots)),
            dma((2, 3)),
            dma((2, 12)),
            dma((2, slots)),
            dma((2, 2)),
            dma((2, 4)),
            pltpu.SemaphoreType.REGULAR,
            dma((6,)),
            dma((6,)),
            dma((6,)),
            dma((6,)),
            dma((2,)),
            dma((3,)),
            dma((3,)),
            dma((3,)),
            dma((3,)),
            dma((2, 4, 3)),
            dma((2, 4, 3)),
            dma((2, 3)),
            dma((2, 3)),
        ],
        compiler_params=pltpu.CompilerParams(
            collective_id=0, has_side_effects=True, vmem_limit_bytes=60 * 2**20
        ),
        cost_estimate=pl.CostEstimate(
            flops=19_000_000_000, bytes_accessed=60_000_000, transcendentals=8_000_000
        ),
    )(span_map, lengths, top_rows, query_t, cache_t, up_weight)[0]


def project_kernel(
    head_ref, out_weight_ref, out_ref,
    taken, weight, values, sums, give, get,
    load_sem, take_send, take_recv, own_recv, sib_recv, a_send, b_send, sib_send,
    give_send, give_recv,
):
    me = lax.axis_index("ctx")
    group = lax.axis_index("req")
    core = me % 2
    chip = me // 2
    a_step = 4 - 3 * core
    b_step = 1 + 3 * core
    a = (chip // a_step) % 4
    b = (chip // b_step) % 4

    def device(da, db):
        return {"ctx": (((a + da) % 4) * a_step + ((b + db) % 4) * b_step) * 2 + core}

    def plane(d):
        return {"req": (group + d) % 4}

    sibling = {"ctx": chip * 2 + 1 - core}
    partners = [device(1, 0), device(2, 0), device(3, 0), device(0, 1), device(0, 3), sibling]
    partners += [plane(1), plane(2), plane(3)]
    barrier = pltpu.get_barrier_semaphore()
    for partner in partners:
        pl.semaphore_signal(barrier, inc=1, device_id=partner, device_id_type=MESH)

    def remote(src, dst, send, recv, target):
        return pltpu.make_async_remote_copy(
            src_ref=src, dst_ref=dst, send_sem=send, recv_sem=recv,
            device_id=target, device_id_type=MESH)

    loads = [
        pltpu.make_async_copy(head_ref.at[0], taken.at[0], load_sem.at[0]),
        pltpu.make_async_copy(out_weight_ref, weight.at[pl.ds(0, 224)], load_sem.at[1]),
    ]
    for copy in loads:
        copy.start()
    pl.semaphore_wait(barrier, len(partners))
    takes = [
        remote(head_ref.at[(0, 2, 3, 1)[d]], taken.at[d], take_send.at[d - 1],
               take_recv.at[d - 1], plane(d))
        for d in (1, 2, 3)
    ]
    for copy in takes:
        copy.start()

    weight[224:256] = jnp.zeros((32, 4096), jnp.bfloat16)
    sums[...] = jnp.zeros_like(sums)
    loads[0].wait()
    for copy in takes:
        copy.wait_recv()

    def a_copy(flow, da):
        return remote(values.at[flow, 0, 0], values.at[flow, da, 0],
                      a_send.at[flow, da - 1], own_recv.at[flow, da],
                      device(da if flow == 0 else 4 - da, 0))

    def b_copy(flow, slot):
        return remote(values.at[flow, slot, 0], values.at[flow, slot + 4, 0],
                      b_send.at[flow, slot], own_recv.at[flow, slot + 4],
                      device(0, 1 if flow == 0 else 3))

    def sib_copy(flow, slot):
        return remote(values.at[flow, slot, 0], values.at[flow, slot, 1],
                      sib_send.at[flow, slot], sib_recv.at[flow, slot], sibling)

    def forward(flow, slot):
        if slot < 12:
            b_copy(flow, slot).start()
        if slot == 0:
            for da in (1, 2, 3):
                a_copy(flow, da).start()
        sib_copy(flow, slot).start()

    for flow in range(2):
        rows = [taken[d, 4 * flow : 4 * flow + 4] for d in range(4)]
        values[flow, 0, 0] = jnp.concatenate(rows, axis=0).astype(jnp.bfloat16)
        forward(flow, 0)

    loads[1].wait()
    for slot in range(slots):
        for flow in range(2):
            if slot:
                (a_copy(flow, slot) if slot < 4 else b_copy(flow, slot - 4)).wait_recv()
                forward(flow, slot)
        if slot % 4 != 3:
            continue
        db = slot // 4
        for flow in range(2):
            for da in range(4):
                sib_copy(flow, 4 * db + da).wait_recv()
            left = values[flow, 4 * db : 4 * db + 4].reshape(128, 2048)
            term = lax.dot_general(
                left, weight[:, 2048 * flow : 2048 * flow + 2048],
                (((1,), (1,)), ((), ())), preferred_element_type=jnp.float32)
            for da in range(4):
                ua, ub = (4 - da, 4 - db) if flow == 0 else (da, db)
                origins = (
                    (((a + ua) % 4) * a_step + ((b + ub) % 4) * b_step) * 2 + core,
                    (((b + ua) % 4) * b_step + ((a + ub) % 4) * a_step) * 2 + 1 - core,
                )
                for which, origin in enumerate(origins):
                    at = 16 * (2 * da + which)
                    place = pl.ds(pl.multiple_of(origin * 16, 16), 16)
                    for i in range(2):
                        sums[i, place] += term[at : at + 16, 128 * i : 128 * i + 128]

    def share(d, s):
        return jnp.concatenate(
            [sums[i, pl.ds(4 * d + s, 32, stride=16), :] for i in range(2)], axis=1)

    gives = []
    for d in (1, 2, 3):
        for s in range(4):
            give[d - 1, s] = share(d, s).astype(jnp.bfloat16)
        copy = remote(give.at[d - 1], get.at[d - 1], give_send.at[d - 1], give_recv.at[d - 1],
                      plane(4 - d))
        copy.start()
        gives.append(copy)
    for copy in gives:
        copy.wait_recv()
    for s in range(4):
        total = share(0, s)
        for i in range(3):
            total = total + get[i, s].astype(jnp.float32)
        out_ref[s] = total[:, :224].astype(jnp.bfloat16)

    for copy in takes + gives:
        copy.wait_send()
    for flow in range(2):
        for slot in range(slots):
            sib_copy(flow, slot).wait_send()
            if 0 < slot < 4:
                a_copy(flow, slot).wait_send()
            if slot < 12:
                b_copy(flow, slot).wait_send()


def project(head_values, out_weight_t):
    dma = pltpu.SemaphoreType.DMA
    bf16, f32 = jnp.bfloat16, jnp.float32
    return pl.pallas_call(
        project_kernel,
        in_specs=[pl.BlockSpec(memory_space=pl.ANY)] * 2,
        out_specs=pl.BlockSpec(memory_space=pltpu.VMEM),
        out_shape=jax.ShapeDtypeStruct((4, 32, 224), bf16),
        scratch_shapes=[
            pltpu.VMEM((4, 8, 2048), f32),
            pltpu.VMEM((256, 4096), bf16),
            pltpu.VMEM((2, slots, 2, 16, 2048), bf16),
            pltpu.VMEM((2, 512, 128), f32),
            pltpu.VMEM((3, 4, 32, 256), bf16),
            pltpu.VMEM((3, 4, 32, 256), bf16),
            dma((2,)),
            dma((3,)),
            dma((3,)),
            dma((2, slots)),
            dma((2, slots)),
            dma((2, 3)),
            dma((2, 12)),
            dma((2, slots)),
            dma((3,)),
            dma((3,)),
        ],
        compiler_params=pltpu.CompilerParams(
            collective_id=1, has_side_effects=True, vmem_limit_bytes=40 * 2**20
        ),
        cost_estimate=pl.CostEstimate(
            flops=1_100_000_000, bytes_accessed=8_000_000, transcendentals=0
        ),
    )(head_values, out_weight_t)


def per_device(queries, top_rows, lengths, span_map, latent_cache, up_weight, out_weight):
    query_t = jnp.swapaxes(queries, 2, 3)[0]
    cache_t = jnp.swapaxes(latent_cache, 1, 2)
    head_values = gather_attend(span_map, lengths, top_rows[0], query_t, cache_t, up_weight)
    out = project(head_values, out_weight.T)
    return jnp.swapaxes(out, 0, 1)


def solution(mesh):
    return jax.shard_map(
        per_device,
        mesh=mesh,
        in_specs=(
            P(("req", "ctx"), None, None, None),
            P(("req", "ctx"), None, None),
            P(("req", "ctx")),
            P(),
            P("req", "ctx", None),
            P("req", None, None),
            P("req", "ctx"),
        ),
        out_specs=P("req", None, "ctx"),
        check_vma=False,
    )
```

```python
import functools

import jax
import jax.numpy as jnp
from jax import lax
from jax.experimental import pallas as pl
from jax.experimental.pallas import tpu as pltpu
from jax.sharding import PartitionSpec as P

score_scale = 192.0 ** (-0.5)
log2_scale = score_scale * 1.4426950408889634
masked = -1e30
lowest = -16384.0


MESH = pl.DeviceIdType.MESH
side = 4
slots = side * side
key_rows = 592
latent_rows = 512


def attend_unit(keys, query):
    scores = lax.dot_general(
        query, keys, (((0,), (0,)), ((), ())), preferred_element_type=jnp.float32
    )
    top = jnp.max(scores, axis=1, keepdims=True) * log2_scale
    top = jnp.maximum(top, lowest).astype(jnp.bfloat16).astype(jnp.float32)
    weights = jnp.exp2(scores * log2_scale - top)
    total = jnp.sum(weights, axis=1, keepdims=True)
    mixed = lax.dot_general(
        weights.astype(jnp.bfloat16),
        keys[:latent_rows],
        (((1,), (1,)), ((), ())),
        preferred_element_type=jnp.float32,
    )
    return mixed.astype(jnp.bfloat16), top, total


def pack_stats(top, total):
    lane = lax.broadcasted_iota(jnp.int32, (256, 128), 1)
    high = total.astype(jnp.bfloat16).astype(jnp.float32)
    packed = jnp.where(lane == 0, top, jnp.where(lane == 1, high, total - high))
    return packed.astype(jnp.bfloat16)


def spread(i):
    return i + (i // 2) * (5 - 2 * i)


def merge_stats(stats):
    top = functools.reduce(jnp.maximum, [t for t, _ in stats])
    return top, sum(jnp.exp2(t - top) * l for t, l in stats)


def roll_rows(block, count):
    count = count % 8
    if count == 0:
        return block
    return jnp.concatenate([block[8 - count :], block[: 8 - count]], axis=0)


def make_mask(span_ref, length_ref, rows_ref, line, place_in, mask_one, core, a, b):
    picks = rows_ref[...]
    block = picks // 256
    holder = jnp.zeros_like(block)
    for c in range(64):
        holder = jnp.where(block == c, span_ref[c], holder)
    place_in[...] = jnp.where(block >= 32, 256, 0) + picks % 256
    x, y = holder // 8, (holder // 2) % 4
    ea = (x * (1 - core) + y * core - a + 4) % 4
    eb = (y * (1 - core) + x * core - b + 4) % 4
    ec = (holder + core) % 2
    step = lax.broadcasted_iota(jnp.int32, picks.shape, 0)
    limit = length_ref[0] - 3 + step
    line[...] = jnp.where(picks < limit, 32 * ea + 16 * ec + 4 * eb + step, -1)

    def chunk(i, count):
        columns = pl.ds(pl.multiple_of(i * 512, 512), 512)
        for s in range(4):
            left = lax.broadcasted_iota(jnp.int32, (128, 512), 0) == line[s : s + 1, columns]
            right = lax.broadcasted_iota(jnp.int32, (512, 512), 0) == place_in[s : s + 1, columns]
            count += lax.dot_general(
                left.astype(jnp.float32).astype(jnp.bfloat16),
                right.astype(jnp.float32).astype(jnp.bfloat16),
                (((1,), (1,)), ((), ())), preferred_element_type=jnp.float32)
        return count

    count = lax.fori_loop(0, 4, chunk, jnp.zeros((128, 512), jnp.float32))
    bias = jnp.where(count > 0.5, 0.0, masked).astype(jnp.bfloat16)
    mask_one[...] = bias.reshape(4, 2, 16, 512)


def gather_attend_kernel(
    span_ref, length_ref, rows_ref, query_ref, cache_ref, up_ref, out_ref, far_up,
    own, sib, kept, to_sib, from_sib, own_stat, keys,
    line, place_in, mask_one, mask_mid, mask_two, mask_got, mask_own, mask_sib,
    stats, stats_a, stats_mid, stats_b, factor, up, wide, raw, partial, ring_in, last_out, last_in,
    one_send, one_recv, two_send, two_recv, three_send, three_recv,
    load_sem, key_sem, own_recv, sib_recv, a_send, b_send, sib_send,
    part_send, part_recv, credit, far_send, far_recv, pass_send, pass_recv, up_sem,
    stat_a_send, stat_a_recv, stat_b_send, stat_b_recv,
    ring_send, ring_recv, last_send, last_recv,
):
    me = lax.axis_index("ctx")
    core = me % 2
    chip = me // 2
    a_step = 4 - 3 * core
    b_step = 1 + 3 * core
    a = (chip // a_step) % 4
    b = (chip // b_step) % 4

    def device(da, db):
        return (((a + da + 4) % 4) * a_step + ((b + db + 4) % 4) * b_step) * 2 + core

    group = lax.axis_index("req")
    sibling = chip * 2 + 1 - core
    barrier = pltpu.get_barrier_semaphore()
    partners = [device(d, 0) for d in (1, 2, 3)] + [device(0, d) for d in (1, 2, 3)] + [sibling]
    partners = [{"ctx": partner} for partner in partners]
    partners += [{"req": (group + 1) % 4}, {"req": (group + 3) % 4}]
    for partner in partners:
        pl.semaphore_signal(barrier, inc=1, device_id=partner, device_id_type=MESH)

    def own_request(flow, slot):
        da, db = spread(slot % 4), spread(slot // 4)
        if flow == 0:
            da, db = 4 - da, 4 - db
        return (((a + da) % 4) * a_step + ((b + db) % 4) * b_step) * 2 + core

    def sib_request(flow, slot):
        da, db = spread(slot % 4), spread(slot // 4)
        if flow == 0:
            da, db = 4 - da, 4 - db
        return (((b + da) % 4) * b_step + ((a + db) % 4) * a_step) * 2 + 1 - core

    def key_copies(slot, place):
        copies = []
        for flow in range(2):
            for which, request in ((0, own_request(flow, slot)), (1, sib_request(flow, slot))):
                at = 2 * which + flow
                copies.append(pltpu.make_async_copy(
                    cache_ref.at[request], keys.at[place, at, pl.ds(0, 576)],
                    key_sem.at[place, at]))
        return copies

    def remote(src, dst, send, recv, target):
        return pltpu.make_async_remote_copy(
            src_ref=src, dst_ref=dst, send_sem=send, recv_sem=recv,
            device_id={"ctx": target}, device_id_type=MESH)

    body = pl.ds(0, 576)

    def a_copy(flow, slot):
        side_step = 1 if (flow == 0) != (slot == 2) else 3
        return remote(own.at[flow, 1 if slot == 3 else 0, body], own.at[flow, slot, body],
                      a_send.at[flow, slot - 1], own_recv.at[flow, slot], device(side_step, 0))

    def b_copy(flow, slot, row):
        side_step = 1 if (flow == 0) != (row == 2) else 3
        return remote(own.at[flow, slot - (4 if row == 1 else 8), body], own.at[flow, slot, body],
                      b_send.at[flow, slot - 4], own_recv.at[flow, slot], device(0, side_step))

    def arrive(flow, slot):
        place = own.at[flow, slot, body]
        remote(place, place, sib_send.at[flow, slot], own_recv.at[flow, slot], sibling).wait_recv()

    def sib_copy(flow, slot):
        return remote(own.at[flow, slot, body], sib.at[flow, slot, body],
                      sib_send.at[flow, slot], sib_recv.at[flow, slot], sibling)

    def part_copy(flow, slot):
        return remote(to_sib.at[flow, slot % 2], from_sib.at[flow, slot % 4],
                      part_send.at[flow, slot % 2], part_recv.at[flow, slot % 4], sibling)

    def far_copy(piece):
        quarter = pl.ds(16 * core + 8 * (piece % 2), 8)
        if piece < 4:
            src, ahead_z = up_ref.at[quarter], (1 if piece < 2 else 3)
        else:
            src = far_up.at[0 if piece == 4 else 1, quarter]
            ahead_z = 1 if piece == 4 else 3
        return pltpu.make_async_remote_copy(
            src_ref=src, dst_ref=far_up.at[piece // 2, quarter],
            send_sem=far_send.at[piece], recv_sem=far_recv.at[piece],
            device_id={"req": (group + ahead_z) % 4}, device_id_type=MESH)

    def pass_copy(piece):
        quarter = far_up.at[piece // 2, pl.ds(16 * core + 8 * (piece % 2), 8)]
        return remote(quarter, quarter, pass_send.at[piece], pass_recv.at[piece], sibling)

    def stat_a_copy(d):
        return remote(stats, stats_a.at[d - 1], stat_a_send.at[d - 1], stat_a_recv.at[d - 1],
                      device(d, 0))

    def stat_b_copy(d):
        return remote(stats_mid, stats_b.at[d - 1], stat_b_send.at[d - 1],
                      stat_b_recv.at[d - 1], device(0, d))

    def ring_copy(flow, gi, db):
        side_step = 1 if (flow == 0) != (db == 1) else 3
        return remote(partial.at[flow, gi, db], ring_in.at[flow, gi, db - 1],
                      ring_send.at[flow, gi, db - 1], ring_recv.at[flow, gi, db - 1],
                      device(0, side_step))

    def last_copy(flow, da):
        return remote(last_out.at[flow, da - 1], last_in.at[flow, da - 1],
                      last_send.at[flow, da - 1], last_recv.at[flow, da - 1],
                      device(-da if flow == 0 else da - 4, 0))

    loads = [
        pltpu.make_async_copy(
            query_ref.at[2 * flow + half],
            own.at[flow, 0, body, pl.ds(128 * half, 128)],
            load_sem.at[flow, half])
        for flow in range(2) for half in range(2)
    ]
    for copy in loads:
        copy.start()
    for copy in key_copies(0, 0):
        copy.start()

    make_mask(span_ref, length_ref, rows_ref, line, place_in, mask_one, core, a, b)

    row = lax.broadcasted_iota(jnp.int32, (16, 256), 0)
    step = lax.broadcasted_iota(jnp.int32, (16, 256), 1) // 128
    for flow in range(2):

        def fill(slot, carry):
            da = spread(slot % 4)
            da = da if flow == 0 else (4 - da) % 4
            hot = jnp.where(row == step + 2 * flow + 4 * da, 1.0, 0.0).astype(jnp.bfloat16)
            own[flow, slot, 576:key_rows] = hot
            sib[flow, slot, 576:key_rows] = hot
            return carry

        lax.fori_loop(0, slots, fill, 0)
    for copy in loads:
        copy.wait()
    pl.semaphore_wait(barrier, len(partners))

    ones = [remote(mask_one.at[d], mask_mid.at[d], one_send.at[d - 1], one_recv.at[d - 1],
                   device(d, 0)) for d in (1, 2, 3)]
    for copy in ones:
        copy.start()
    for piece in (0, 3, 1, 2):
        far_copy(piece).start()
    for flow in range(2):
        for slot in (1, 2):
            a_copy(flow, slot).start()
        b_copy(flow, 4, 1).start()
        b_copy(flow, 8, 2).start()
        sib_copy(flow, 0).start()
    for copy in ones:
        copy.wait_recv()
    for which in range(2):
        lists = [mask_one[0, which].astype(jnp.float32)]
        lists += [mask_mid[d, which].astype(jnp.float32) for d in (1, 2, 3)]
        for eb in range(4):
            rows = [part[4 * eb : 4 * eb + 4] for part in lists]
            mask_two[eb, which] = jnp.concatenate(rows, axis=0).astype(jnp.bfloat16)
    twos = [remote(mask_two.at[d], mask_got.at[d], two_send.at[d - 1], two_recv.at[d - 1],
                   device(0, d)) for d in (1, 2, 3)]
    for copy in twos:
        copy.start()
    for copy in twos:
        copy.wait_recv()
    mask_own[0] = mask_two[0, 0]
    mask_own[4] = mask_two[0, 1]
    for d in (1, 2, 3):
        mask_own[d] = mask_got[d, 0]
        mask_own[4 + d] = mask_got[d, 1]
    three = remote(mask_own.at[pl.ds(4, 4)], mask_sib, three_send, three_recv, sibling)
    three.start()
    three.wait_recv()

    row8 = lax.broadcasted_iota(jnp.int32, (8, 128), 0)

    def combine(slot):
        db, da = spread(slot // 4), spread(slot % 4)
        for flow in range(2):
            part_copy(flow, slot).wait_recv()
            for half in range(2):
                rows = slice(128 * half, 128 * half + 128)
                got = from_sib[flow, slot % 4, rows, 512:640].astype(jnp.float32)
                top_1, total_1 = own_stat[slot % 2, flow, 0, rows], own_stat[slot % 2, flow, 1, rows]
                top_2 = jnp.broadcast_to(got[:, 0:1], (128, 128))
                total_2 = jnp.broadcast_to(got[:, 1:2] + got[:, 2:3], (128, 128))
                top = jnp.maximum(top_1, top_2)
                factor_1, factor_2 = jnp.exp2(top_1 - top), jnp.exp2(top_2 - top)
                total = factor_1 * total_1 + factor_2 * total_2
                for i in range(4):
                    lanes = slice(128 * i, 128 * i + 128)
                    value = factor_1 * kept[flow, slot, rows, lanes].astype(jnp.float32)
                    value += factor_2 * from_sib[flow, slot % 4, rows, lanes].astype(jnp.float32)
                    kept[flow, slot, rows, lanes] = value.astype(jnp.bfloat16)
                for i, value in enumerate((top, total)):
                    value = jnp.swapaxes(value, 0, 1)[0:8]
                    stats[i, flow, db] = jnp.where(
                        row8 == 2 * da + half, value, stats[i, flow, db])

    def give_credit():
        pl.semaphore_signal(credit, inc=1, device_id={"ctx": sibling}, device_id_type=MESH)

    def iteration(slot, carry):
        place = slot % 2

        def first_row(at):
            for flow in range(2):
                arrive(flow, at)
                if at == 1:
                    a_copy(flow, 3).start()
                b_copy(flow, 4 + at, 1).start()
                b_copy(flow, 8 + at, 2).start()
                sib_copy(flow, at).start()

        @pl.when(slot == 1)
        def _():
            first_row(1)
            first_row(2)

        @pl.when(slot == 2)
        def _():
            first_row(3)

        @pl.when((slot >= 2) & (slot < 6))
        def _():
            for flow in range(2):
                arrive(flow, slot + 2)
                b_copy(flow, slot + 10, 3).start()

        @pl.when((slot >= 6) & (slot < 14))
        def _():
            for flow in range(2):
                arrive(flow, slot + 2)

        @pl.when((slot >= 2) & (slot < 14))
        def _():
            for flow in range(2):
                sib_copy(flow, slot + 2).start()

        @pl.when(slot < slots - 1)
        def _():
            for copy in key_copies(slot + 1, 1 - place):
                copy.start()

        for copy in key_copies(slot, place):
            copy.wait()
        for flow in range(2):
            db = spread(slot // 4)
            db = db if flow == 0 else (4 - db) % 4
            keys[place, flow, 576:key_rows] = mask_own[db]
            keys[place, 2 + flow, 576:key_rows] = mask_sib[db]

        results = [attend_unit(keys[place, flow], own[flow, slot]) for flow in range(2)]
        for flow in range(2):
            mixed, top, total = results[flow]
            kept[flow, slot] = mixed
            own_stat[place, flow, 0] = jnp.broadcast_to(top, (256, 128))
            own_stat[place, flow, 1] = jnp.broadcast_to(total, (256, 128))

        for flow in range(2):
            sib_copy(flow, slot).wait_recv()

        @pl.when(slot >= 2)
        def _():
            for flow in range(2):
                part_copy(flow, slot).wait_send()

        results = [attend_unit(keys[place, 2 + flow], sib[flow, slot]) for flow in range(2)]
        for flow in range(2):
            mixed, top, total = results[flow]
            to_sib[flow, place, :, 0:512] = mixed
            to_sib[flow, place, :, 512:640] = pack_stats(top, total)

        @pl.when(slot >= 4)
        def _():
            pl.semaphore_wait(credit, 1)

        for flow in range(2):
            part_copy(flow, slot).start()

        @pl.when(slot > 0)
        def _():
            combine(slot - 1)

        @pl.when((slot > 0) & (slot < 13))
        def _():
            give_credit()

        @pl.when(slot == 8)
        def _():
            for piece in (0, 3):
                far_copy(piece).wait_recv()
                pass_copy(piece).start()
            far_copy(4).start()
            far_copy(5).start()

        @pl.when(slot == 12)
        def _():
            for piece in (1, 2):
                far_copy(piece).wait_recv()
                pass_copy(piece).start()

        return carry

    stats[...] = jnp.zeros_like(stats)
    lax.fori_loop(0, slots, iteration, 0)

    def up_copy(gi):
        src = up_ref if gi == 0 else far_up.at[gi - 1]
        return pltpu.make_async_copy(src, up.at[gi % 2], up_sem.at[gi % 2])

    def fill_group(gi):
        first_head = pl.multiple_of(32 * ((group + ahead_of[gi]) % 4), 32)
        for flow in range(2):

            def fill_wide(slot, carry):
                place = 4 * spread(slot // 4) + spread(slot % 4)
                for half in range(2):
                    rows = pl.ds(pl.multiple_of(128 * half + first_head, 32), 32)
                    value = kept[flow, slot, rows].astype(jnp.float32)
                    at = pl.ds(pl.multiple_of(32 * (32 * flow + 2 * place + half), 32), 32)
                    for i in range(4):
                        wide[i, at] = value[:, 128 * i : 128 * i + 128]
                return carry

            lax.fori_loop(0, slots, fill_wide, 0)

    def product(gi, head):
        rows = [wide[i, pl.ds(head, 64, stride=32), :] for i in range(4)]
        rows = jnp.concatenate(rows, axis=1).astype(jnp.bfloat16)
        return jnp.dot(rows, up[gi % 2, head], preferred_element_type=jnp.float32)

    def scaled(gi, head, value, weight):
        lane = 32 * ahead_of[gi] + head
        return value * weight[:, lane : lane + 1]

    def store_pair(gi, hj, values):
        for flow in range(2):
            for db in range(4):
                at = 32 * flow + 8 * db
                both = jnp.concatenate([value[at : at + 8] for value in values], axis=0)
                partial[flow, gi, db, :, 128 * hj : 128 * hj + 128] = both.astype(jnp.bfloat16)

    ahead_of = (0, 3, 1, 2)
    up_copy(0).start()
    combine(slots - 1)
    for d in (1, 2, 3):
        stat_a_copy(d).start()
    for piece in (0, 1):
        pass_copy(piece).wait_recv()
    up_copy(1).start()
    fill_group(0)
    up_copy(0).wait()
    for d in (1, 2, 3):
        stat_a_copy(d).wait_recv()
    for flow in range(2):
        for db in range(4):
            parts = [(stats[0, flow, db], stats[1, flow, db])]
            for d in (1, 2, 3):
                turn = 2 * d if flow == 0 else -2 * d
                parts.append(tuple(roll_rows(stats_a[d - 1, i, flow, db], turn) for i in range(2)))
            stats_mid[0, flow, db], stats_mid[1, flow, db] = merge_stats(parts)
    for d in (1, 2, 3):
        stat_b_copy(d).start()
    for head in range(32):
        raw[head] = product(0, head)
    for piece in (4, 5):
        far_copy(piece).wait_recv()
        pass_copy(piece).start()
    for d in (1, 2, 3):
        stat_b_copy(d).wait_recv()
    for flow in range(2):
        for db in range(4):
            parts = [(stats_mid[0, flow, db], stats_mid[1, flow, db])]
            for d in (1, 2, 3):
                other = (db - d) % 4 if flow == 0 else (db + d) % 4
                parts.append((stats_b[d - 1, 0, flow, other], stats_b[d - 1, 1, flow, other]))
            top, total = merge_stats(parts)
            value = jnp.exp2(stats[0, flow, db] - top) / total
            turned = value
            for z in (1, 2, 3):
                shifted = jnp.concatenate([value[:, 32 * z :], value[:, : 32 * z]], axis=1)
                turned = jnp.where(group == z, shifted, turned)
            factor[32 * flow + 8 * db : 32 * flow + 8 * db + 8] = turned

    def chain(gi):
        for flow in range(2):
            ring_copy(flow, gi, 2).wait_recv()
            value = partial[flow, gi, 3].astype(jnp.float32)
            value += ring_in[flow, gi, 1].astype(jnp.float32)
            partial[flow, gi, 3] = value.astype(jnp.bfloat16)
            ring_copy(flow, gi, 3).start()

    for gi in range(4):
        if gi:
            up_copy(gi).wait()
            fill_group(gi)
        weight = factor[...]
        for hj in range(16):
            values = [raw[head] if gi == 0 else product(gi, head) for head in (hj, 16 + hj)]
            values = [scaled(gi, 16 * c + hj, value, weight) for c, value in enumerate(values)]
            store_pair(gi, hj, values)
        for db in (2, 1):
            for flow in range(2):
                ring_copy(flow, gi, db).start()
        if gi == 0:
            for piece in (2, 3):
                pass_copy(piece).wait_recv()
            up_copy(2).start()
        if gi == 1:
            for piece in (4, 5):
                pass_copy(piece).wait_recv()
            up_copy(3).start()
        if gi >= 1:
            chain(gi - 1)
    chain(3)

    whole = []
    for flow in range(2):
        ends = []
        for gi in range(4):
            ring_copy(flow, gi, 1).wait_recv()
            ring_copy(flow, gi, 3).wait_recv()
            value = partial[flow, gi, 0].astype(jnp.float32)
            value += ring_in[flow, gi, 0].astype(jnp.float32)
            ends.append(value + ring_in[flow, gi, 2].astype(jnp.float32))

        def rows_of(da):
            picked = [end[8 * c + 2 * da : 8 * c + 2 * da + 2] for end in ends for c in range(2)]
            return jnp.concatenate(picked, axis=0)

        for da in (1, 2, 3):
            last_out[flow, da - 1] = rows_of(da).astype(jnp.bfloat16)
            last_copy(flow, da).start()
        whole.append(rows_of(0))
    for flow in range(2):
        for da in (1, 2, 3):
            last_copy(flow, da).wait_recv()
            whole[flow] = whole[flow] + last_in[flow, da - 1].astype(jnp.float32)
    for gi in range(4):
        picked = [whole[flow][4 * gi + 2 * c : 4 * gi + 2 * c + 2]
                  for c in range(2) for flow in range(2)]
        out_ref[gi] = jnp.concatenate(picked, axis=0)

    for flow in range(2):
        def drain(slot, carry):
            sib_copy(flow, slot).wait_send()
            return carry

        lax.fori_loop(0, slots, drain, 0)
        for slot in (14, 15):
            part_copy(flow, slot).wait_send()
        for slot in range(4, 16):
            b_copy(flow, slot, slot // 4).wait_send()
        for da in (1, 2, 3):
            a_copy(flow, da).wait_send()
            last_copy(flow, da).wait_send()
            for gi in range(4):
                ring_copy(flow, gi, da).wait_send()
    for piece in range(6):
        far_copy(piece).wait_send()
        pass_copy(piece).wait_send()
    for d in (1, 2, 3):
        stat_a_copy(d).wait_send()
        stat_b_copy(d).wait_send()
    for copy in ones + twos + [three]:
        copy.wait_send()


def gather_attend(span_map, lengths, top_rows, query_t, cache_t, up_weight):
    dma = pltpu.SemaphoreType.DMA
    bf16, f32 = jnp.bfloat16, jnp.float32
    return pl.pallas_call(
        gather_attend_kernel,
        in_specs=[pl.BlockSpec(memory_space=pltpu.SMEM)] * 2
        + [pl.BlockSpec(memory_space=pltpu.VMEM)]
        + [pl.BlockSpec(memory_space=pl.ANY)] * 3,
        out_specs=[pl.BlockSpec(memory_space=pltpu.VMEM), pl.BlockSpec(memory_space=pl.ANY)],
        out_shape=[
            jax.ShapeDtypeStruct((4, 8, 2048), f32),
            jax.ShapeDtypeStruct((3,) + up_weight.shape, bf16),
        ],
        scratch_shapes=[
            pltpu.VMEM((2, slots, key_rows, 256), bf16),
            pltpu.VMEM((2, slots, key_rows, 256), bf16),
            pltpu.VMEM((2, slots, 256, 512), bf16),
            pltpu.VMEM((2, 2, 256, 640), bf16),
            pltpu.VMEM((2, 4, 256, 640), bf16),
            pltpu.VMEM((2, 2, 2, 256, 128), f32),
            pltpu.VMEM((2, 4, key_rows, 512), bf16),
            pltpu.VMEM((4, 2048), jnp.int32),
            pltpu.VMEM((4, 2048), jnp.int32),
            pltpu.VMEM((4, 2, 16, 512), bf16),
            pltpu.VMEM((4, 2, 16, 512), bf16),
            pltpu.VMEM((4, 2, 16, 512), bf16),
            pltpu.VMEM((4, 2, 16, 512), bf16),
            pltpu.VMEM((8, 16, 512), bf16),
            pltpu.VMEM((4, 16, 512), bf16),
            pltpu.VMEM((2, 2, 4, 8, 128), f32),
            pltpu.VMEM((3, 2, 2, 4, 8, 128), f32),
            pltpu.VMEM((2, 2, 4, 8, 128), f32),
            pltpu.VMEM((3, 2, 2, 4, 8, 128), f32),
            pltpu.VMEM((64, 128), f32),
            pltpu.VMEM((2, 32, 512, 128), bf16),
            pltpu.VMEM((4, 2048, 128), f32),
            pltpu.VMEM((32, 64, 128), f32),
            pltpu.VMEM((2, 4, 4, 16, 2048), bf16),
            pltpu.VMEM((2, 4, 3, 16, 2048), bf16),
            pltpu.VMEM((2, 3, 16, 2048), bf16),
            pltpu.VMEM((2, 3, 16, 2048), bf16),
            dma((3,)),
            dma((3,)),
            dma((3,)),
            dma((3,)),
            dma,
            dma,
            dma((2, 2)),
            dma((2, 4)),
            dma((2, slots)),
            dma((2, slots)),
            dma((2, 3)),
            dma((2, 12)),
            dma((2, slots)),
            dma((2, 2)),
            dma((2, 4)),
            pltpu.SemaphoreType.REGULAR,
            dma((6,)),
            dma((6,)),
            dma((6,)),
            dma((6,)),
            dma((2,)),
            dma((3,)),
            dma((3,)),
            dma((3,)),
            dma((3,)),
            dma((2, 4, 3)),
            dma((2, 4, 3)),
            dma((2, 3)),
            dma((2, 3)),
        ],
        compiler_params=pltpu.CompilerParams(
            collective_id=0, has_side_effects=True, vmem_limit_bytes=60 * 2**20
        ),
        cost_estimate=pl.CostEstimate(
            flops=19_000_000_000, bytes_accessed=60_000_000, transcendentals=8_000_000
        ),
    )(span_map, lengths, top_rows, query_t, cache_t, up_weight)[0]


def project_kernel(
    head_ref, out_weight_ref, out_ref,
    taken, weight, values, sums, give, get,
    load_sem, take_send, take_recv, own_recv, sib_recv, a_send, b_send, sib_send,
    give_send, give_recv,
):
    me = lax.axis_index("ctx")
    group = lax.axis_index("req")
    core = me % 2
    chip = me // 2
    a_step = 4 - 3 * core
    b_step = 1 + 3 * core
    a = (chip // a_step) % 4
    b = (chip // b_step) % 4

    def device(da, db):
        return {"ctx": (((a + da) % 4) * a_step + ((b + db) % 4) * b_step) * 2 + core}

    def plane(d):
        return {"req": (group + d) % 4}

    sibling = {"ctx": chip * 2 + 1 - core}
    partners = [device(1, 0), device(3, 0), device(0, 1), device(0, 3), sibling]
    partners += [plane(1), plane(2), plane(3)]
    barrier = pltpu.get_barrier_semaphore()
    for partner in partners:
        pl.semaphore_signal(barrier, inc=1, device_id=partner, device_id_type=MESH)

    def remote(src, dst, send, recv, target):
        return pltpu.make_async_remote_copy(
            src_ref=src, dst_ref=dst, send_sem=send, recv_sem=recv,
            device_id=target, device_id_type=MESH)

    loads = [
        pltpu.make_async_copy(head_ref.at[0], taken.at[0], load_sem.at[0]),
        pltpu.make_async_copy(out_weight_ref, weight.at[pl.ds(0, 224)], load_sem.at[1]),
    ]
    for copy in loads:
        copy.start()
    pl.semaphore_wait(barrier, len(partners))
    takes = [
        remote(head_ref.at[(0, 2, 3, 1)[d]], taken.at[d], take_send.at[d - 1],
               take_recv.at[d - 1], plane(d))
        for d in (1, 2, 3)
    ]
    for copy in takes:
        copy.start()

    weight[224:256] = jnp.zeros((32, 4096), jnp.bfloat16)
    sums[...] = jnp.zeros_like(sums)
    loads[0].wait()
    for copy in takes:
        copy.wait_recv()

    def a_copy(flow, slot):
        side_step = 1 if (flow == 0) != (slot == 2) else 3
        return remote(values.at[flow, 1 if slot == 3 else 0, 0], values.at[flow, slot, 0],
                      a_send.at[flow, slot - 1], own_recv.at[flow, slot], device(side_step, 0))

    def b_copy(flow, slot):
        side_step = 1 if (flow == 0) != (slot // 4 == 2) else 3
        return remote(values.at[flow, slot - (4 if slot < 8 else 8), 0], values.at[flow, slot, 0],
                      b_send.at[flow, slot - 4], own_recv.at[flow, slot], device(0, side_step))

    def sib_copy(flow, slot):
        return remote(values.at[flow, slot, 0], values.at[flow, slot, 1],
                      sib_send.at[flow, slot], sib_recv.at[flow, slot], sibling)

    def forward(flow, slot):
        if slot == 0:
            a_copy(flow, 1).start()
            a_copy(flow, 2).start()
        if slot == 1:
            a_copy(flow, 3).start()
        if slot < 4:
            b_copy(flow, slot + 4).start()
            b_copy(flow, slot + 8).start()
        elif slot < 8:
            b_copy(flow, slot + 8).start()
        sib_copy(flow, slot).start()

    for flow in range(2):
        rows = [taken[d, 4 * flow : 4 * flow + 4] for d in range(4)]
        values[flow, 0, 0] = jnp.concatenate(rows, axis=0).astype(jnp.bfloat16)
        forward(flow, 0)

    loads[1].wait()
    for slot in range(slots):
        for flow in range(2):
            if slot:
                (a_copy if slot < 4 else b_copy)(flow, slot).wait_recv()
                forward(flow, slot)
        if slot % 4 != 3:
            continue
        row = slot // 4
        db = spread(row)
        for flow in range(2):
            for da in range(4):
                sib_copy(flow, 4 * row + da).wait_recv()
            left = values[flow, 4 * row : 4 * row + 4].reshape(128, 2048)
            term = lax.dot_general(
                left, weight[:, 2048 * flow : 2048 * flow + 2048],
                (((1,), (1,)), ((), ())), preferred_element_type=jnp.float32)
            for i in range(4):
                da = spread(i)
                ua, ub = (4 - da, 4 - db) if flow == 0 else (da, db)
                origins = (
                    (((a + ua) % 4) * a_step + ((b + ub) % 4) * b_step) * 2 + core,
                    (((b + ua) % 4) * b_step + ((a + ub) % 4) * a_step) * 2 + 1 - core,
                )
                for which, origin in enumerate(origins):
                    at = 16 * (2 * i + which)
                    place = pl.ds(pl.multiple_of(origin * 16, 16), 16)
                    for half in range(2):
                        sums[half, place] += term[at : at + 16, 128 * half : 128 * half + 128]

    def share(d, s):
        return jnp.concatenate(
            [sums[i, pl.ds(4 * d + s, 32, stride=16), :] for i in range(2)], axis=1)

    gives = []
    for d in (1, 2, 3):
        for s in range(4):
            give[d - 1, s] = share(d, s).astype(jnp.bfloat16)
        copy = remote(give.at[d - 1], get.at[d - 1], give_send.at[d - 1], give_recv.at[d - 1],
                      plane(4 - d))
        copy.start()
        gives.append(copy)
    for copy in gives:
        copy.wait_recv()
    for s in range(4):
        total = share(0, s)
        for i in range(3):
            total = total + get[i, s].astype(jnp.float32)
        out_ref[s] = total[:, :224].astype(jnp.bfloat16)

    for copy in takes + gives:
        copy.wait_send()
    for flow in range(2):
        for slot in range(slots):
            sib_copy(flow, slot).wait_send()
            if 0 < slot < 4:
                a_copy(flow, slot).wait_send()
            if slot >= 4:
                b_copy(flow, slot).wait_send()


def project(head_values, out_weight_t):
    dma = pltpu.SemaphoreType.DMA
    bf16, f32 = jnp.bfloat16, jnp.float32
    return pl.pallas_call(
        project_kernel,
        in_specs=[pl.BlockSpec(memory_space=pl.ANY)] * 2,
        out_specs=pl.BlockSpec(memory_space=pltpu.VMEM),
        out_shape=jax.ShapeDtypeStruct((4, 32, 224), bf16),
        scratch_shapes=[
            pltpu.VMEM((4, 8, 2048), f32),
            pltpu.VMEM((256, 4096), bf16),
            pltpu.VMEM((2, slots, 2, 16, 2048), bf16),
            pltpu.VMEM((2, 512, 128), f32),
            pltpu.VMEM((3, 4, 32, 256), bf16),
            pltpu.VMEM((3, 4, 32, 256), bf16),
            dma((2,)),
            dma((3,)),
            dma((3,)),
            dma((2, slots)),
            dma((2, slots)),
            dma((2, 3)),
            dma((2, 12)),
            dma((2, slots)),
            dma((3,)),
            dma((3,)),
        ],
        compiler_params=pltpu.CompilerParams(
            collective_id=1, has_side_effects=True, vmem_limit_bytes=40 * 2**20
        ),
        cost_estimate=pl.CostEstimate(
            flops=1_100_000_000, bytes_accessed=8_000_000, transcendentals=0
        ),
    )(head_values, out_weight_t)


def per_device(queries, top_rows, lengths, span_map, latent_cache, up_weight, out_weight):
    query_t = jnp.swapaxes(queries, 2, 3)[0]
    cache_t = jnp.swapaxes(latent_cache, 1, 2)
    head_values = gather_attend(span_map, lengths, top_rows[0], query_t, cache_t, up_weight)
    out = project(head_values, out_weight.T)
    return jnp.swapaxes(out, 0, 1)


def solution(mesh):
    return jax.shard_map(
        per_device,
        mesh=mesh,
        in_specs=(
            P(("req", "ctx"), None, None, None),
            P(("req", "ctx"), None, None),
            P(("req", "ctx")),
            P(),
            P("req", "ctx", None),
            P("req", None, None),
            P("req", "ctx"),
        ),
        out_specs=P("req", None, "ctx"),
        check_vma=False,
    )
```

```python
import functools

import jax
import jax.numpy as jnp
from jax import lax
from jax.experimental import pallas as pl
from jax.experimental.pallas import tpu as pltpu
from jax.sharding import PartitionSpec as P

score_scale = 192.0 ** (-0.5)
log2_scale = score_scale * 1.4426950408889634
masked = -1e30
lowest = -16384.0


MESH = pl.DeviceIdType.MESH
side = 4
slots = side * side
key_rows = 592
latent_rows = 512


def attend_unit(keys, query):
    scores = lax.dot_general(
        query, keys, (((0,), (0,)), ((), ())), preferred_element_type=jnp.float32
    )
    top = jnp.max(scores, axis=1, keepdims=True) * log2_scale
    top = jnp.maximum(top, lowest).astype(jnp.bfloat16).astype(jnp.float32)
    weights = jnp.exp2(scores * log2_scale - top)
    total = jnp.sum(weights, axis=1, keepdims=True)
    mixed = lax.dot_general(
        weights.astype(jnp.bfloat16),
        keys[:latent_rows],
        (((1,), (1,)), ((), ())),
        preferred_element_type=jnp.float32,
    )
    return mixed.astype(jnp.bfloat16), top, total


def pack_stats(top, total):
    lane = lax.broadcasted_iota(jnp.int32, (top.shape[0], 128), 1)
    high = total.astype(jnp.bfloat16).astype(jnp.float32)
    packed = jnp.where(lane == 0, top, jnp.where(lane == 1, high, total - high))
    return packed.astype(jnp.bfloat16)


def spread(i):
    return i + (i // 2) * (5 - 2 * i)


def merge_stats(stats):
    top = functools.reduce(jnp.maximum, [t for t, _ in stats])
    return top, sum(jnp.exp2(t - top) * l for t, l in stats)


def roll_rows(block, count):
    size = block.shape[0]
    return jnp.concatenate([block[size - count :], block[: size - count]], axis=0)


def make_mask(span_ref, length_ref, rows_ref, line, place_in, mask_one, core, a, b):
    picks = rows_ref[...]
    block = picks // 256
    holder = jnp.zeros_like(block)
    for c in range(64):
        holder = jnp.where(block == c, span_ref[c], holder)
    place_in[...] = jnp.where(block >= 32, 256, 0) + picks % 256
    x, y = holder // 8, (holder // 2) % 4
    ea = (x * (1 - core) + y * core - a + 4) % 4
    eb = (y * (1 - core) + x * core - b + 4) % 4
    ec = (holder + core) % 2
    step = lax.broadcasted_iota(jnp.int32, picks.shape, 0)
    limit = length_ref[0] - 3 + step
    line[...] = jnp.where(picks < limit, 32 * ea + 16 * ec + 4 * eb + step, -1)

    def chunk(i, count):
        columns = pl.ds(pl.multiple_of(i * 512, 512), 512)
        for s in range(4):
            left = lax.broadcasted_iota(jnp.int32, (128, 512), 0) == line[s : s + 1, columns]
            right = lax.broadcasted_iota(jnp.int32, (512, 512), 0) == place_in[s : s + 1, columns]
            count += lax.dot_general(
                left.astype(jnp.float32).astype(jnp.bfloat16),
                right.astype(jnp.float32).astype(jnp.bfloat16),
                (((1,), (1,)), ((), ())), preferred_element_type=jnp.float32)
        return count

    count = lax.fori_loop(0, 4, chunk, jnp.zeros((128, 512), jnp.float32))
    bias = jnp.where(count > 0.5, 0.0, masked).astype(jnp.bfloat16)
    mask_one[...] = bias.reshape(4, 2, 16, 512)


def gather_attend_kernel(
    span_ref, length_ref, rows_ref, query_ref, cache_ref, up_ref, out_ref, far_up,
    own, sib, kept, to_sib, from_sib, own_stat, keys,
    line, place_in, mask_one, mask_mid, mask_two, mask_got, mask_own, mask_sib,
    stats, stats_a, stats_mid, stats_b, factor, up, wide, raw, partial, ring_in, last_out, last_in,
    one_send, one_recv, two_send, two_recv, three_send, three_recv,
    load_sem, key_sem, own_recv, sib_recv, a_send, b_send, sib_send,
    part_send, part_recv, credit, far_send, far_recv, pass_send, pass_recv, up_sem,
    stat_a_send, stat_a_recv, stat_b_send, stat_b_recv,
    ring_send, ring_recv, last_send, last_recv,
):
    me = lax.axis_index("ctx")
    core = me % 2
    chip = me // 2
    a_step = 4 - 3 * core
    b_step = 1 + 3 * core
    a = (chip // a_step) % 4
    b = (chip // b_step) % 4

    def device(da, db):
        return (((a + da + 4) % 4) * a_step + ((b + db + 4) % 4) * b_step) * 2 + core

    group = lax.axis_index("req")
    sibling = chip * 2 + 1 - core
    barrier = pltpu.get_barrier_semaphore()
    partners = [device(d, 0) for d in (1, 2, 3)] + [device(0, d) for d in (1, 2, 3)] + [sibling]
    partners = [{"ctx": partner} for partner in partners]
    partners += [{"req": (group + 1) % 4}, {"req": (group + 3) % 4}]
    for partner in partners:
        pl.semaphore_signal(barrier, inc=1, device_id=partner, device_id_type=MESH)

    def requests(slot):
        ua, ub = 4 - spread(slot % 4), 4 - spread(slot // 4)
        return (
            (((a + ua) % 4) * a_step + ((b + ub) % 4) * b_step) * 2 + core,
            (((b + ua) % 4) * b_step + ((a + ub) % 4) * a_step) * 2 + 1 - core,
        )

    def key_copies(slot, place):
        return [
            pltpu.make_async_copy(
                cache_ref.at[request], keys.at[place, which, pl.ds(0, 576)],
                key_sem.at[place, which])
            for which, request in enumerate(requests(slot))
        ]

    def remote(src, dst, send, recv, target):
        return pltpu.make_async_remote_copy(
            src_ref=src, dst_ref=dst, send_sem=send, recv_sem=recv,
            device_id={"ctx": target}, device_id_type=MESH)

    body = pl.ds(0, 576)

    def a_copy(flow, slot):
        source, side_step = ((0, 1), (0, 3), (1, 1) if flow == 0 else (2, 3))[slot - 1]
        return remote(own.at[flow, source, body], own.at[flow, slot, body],
                      a_send.at[flow, slot - 1], own_recv.at[flow, slot], device(side_step, 0))

    def b_copy(flow, slot, row):
        back, side_step = ((4, 1), (8, 3), (8, 1) if flow == 0 else (4, 3))[row - 1]
        return remote(own.at[flow, slot - back, body], own.at[flow, slot, body],
                      b_send.at[flow, slot - 4], own_recv.at[flow, slot], device(0, side_step))

    def arrive(flow, slot):
        place = own.at[flow, slot, body]
        remote(place, place, sib_send.at[flow, slot], own_recv.at[flow, slot], sibling).wait_recv()

    def sib_copy(flow, slot):
        return remote(own.at[flow, slot, body], sib.at[flow, slot, body],
                      sib_send.at[flow, slot], sib_recv.at[flow, slot], sibling)

    def part_copy(slot):
        return remote(to_sib.at[slot % 2], from_sib.at[slot % 4],
                      part_send.at[slot % 2], part_recv.at[slot % 4], sibling)

    def far_copy(piece):
        quarter = pl.ds(16 * core + 8 * (piece % 2), 8)
        if piece < 4:
            src, ahead_z = up_ref.at[quarter], (1 if piece < 2 else 3)
        else:
            src = far_up.at[0 if piece == 4 else 1, quarter]
            ahead_z = 1 if piece == 4 else 3
        return pltpu.make_async_remote_copy(
            src_ref=src, dst_ref=far_up.at[piece // 2, quarter],
            send_sem=far_send.at[piece], recv_sem=far_recv.at[piece],
            device_id={"req": (group + ahead_z) % 4}, device_id_type=MESH)

    def pass_copy(piece):
        quarter = far_up.at[piece // 2, pl.ds(16 * core + 8 * (piece % 2), 8)]
        return remote(quarter, quarter, pass_send.at[piece], pass_recv.at[piece], sibling)

    def stat_a_copy(d):
        return remote(stats, stats_a.at[d - 1], stat_a_send.at[d - 1], stat_a_recv.at[d - 1],
                      device(d, 0))

    def stat_b_copy(d):
        return remote(stats_mid, stats_b.at[d - 1], stat_b_send.at[d - 1],
                      stat_b_recv.at[d - 1], device(0, d))

    def ring_copy(half, gi, db):
        side_step = (3, 1 if half == 0 else 3, 1)[db - 1]
        return remote(partial.at[half, gi, db], ring_in.at[half, gi, db - 1],
                      ring_send.at[half, gi, db - 1], ring_recv.at[half, gi, db - 1],
                      device(0, side_step))

    def last_copy(half, da):
        return remote(last_out.at[half, da - 1], last_in.at[half, da - 1],
                      last_send.at[half, da - 1], last_recv.at[half, da - 1], device(-da, 0))

    loads = [
        pltpu.make_async_copy(
            query_ref.at[2 * flow + half],
            own.at[flow, 0, body, pl.ds(128 * half, 128)],
            load_sem.at[flow, half])
        for flow in range(2) for half in range(2)
    ]
    for copy in loads:
        copy.start()
    for copy in key_copies(0, 0):
        copy.start()

    make_mask(span_ref, length_ref, rows_ref, line, place_in, mask_one, core, a, b)

    row = lax.broadcasted_iota(jnp.int32, (16, 256), 0)
    step = lax.broadcasted_iota(jnp.int32, (16, 256), 1) // 128
    for flow in range(2):

        def fill(slot, carry):
            da = spread(slot % 4)
            hot = jnp.where(row == step + 2 * flow + 4 * da, 1.0, 0.0).astype(jnp.bfloat16)
            own[flow, slot, 576:key_rows] = hot
            sib[flow, slot, 576:key_rows] = hot
            return carry

        lax.fori_loop(0, slots, fill, 0)
    for copy in loads:
        copy.wait()
    pl.semaphore_wait(barrier, len(partners))

    ones = [remote(mask_one.at[d], mask_mid.at[d], one_send.at[d - 1], one_recv.at[d - 1],
                   device(d, 0)) for d in (1, 2, 3)]
    for copy in ones:
        copy.start()
    for piece in (0, 3, 1, 2):
        far_copy(piece).start()
    for flow in range(2):
        for slot in (1, 2):
            a_copy(flow, slot).start()
        b_copy(flow, 4, 1).start()
        b_copy(flow, 8, 2).start()
        sib_copy(flow, 0).start()
    for copy in ones:
        copy.wait_recv()
    for which in range(2):
        lists = [mask_one[0, which].astype(jnp.float32)]
        lists += [mask_mid[d, which].astype(jnp.float32) for d in (1, 2, 3)]
        for eb in range(4):
            rows = [part[4 * eb : 4 * eb + 4] for part in lists]
            mask_two[eb, which] = jnp.concatenate(rows, axis=0).astype(jnp.bfloat16)
    twos = [remote(mask_two.at[d], mask_got.at[d], two_send.at[d - 1], two_recv.at[d - 1],
                   device(0, d)) for d in (1, 2, 3)]
    for copy in twos:
        copy.start()
    for copy in twos:
        copy.wait_recv()
    mask_own[0] = mask_two[0, 0]
    mask_own[4] = mask_two[0, 1]
    for d in (1, 2, 3):
        mask_own[d] = mask_got[d, 0]
        mask_own[4 + d] = mask_got[d, 1]
    three = remote(mask_own.at[pl.ds(4, 4)], mask_sib, three_send, three_recv, sibling)
    three.start()
    three.wait_recv()

    row16 = lax.broadcasted_iota(jnp.int32, (16, 128), 0)

    def combine(slot):
        db, da = spread(slot // 4), spread(slot % 4)
        part_copy(slot).wait_recv()
        for s in range(4):
            rows = slice(128 * s, 128 * s + 128)
            got = from_sib[slot % 4, rows, 512:640].astype(jnp.float32)
            top_1, total_1 = own_stat[slot % 2, 0, rows], own_stat[slot % 2, 1, rows]
            top_2 = jnp.broadcast_to(got[:, 0:1], (128, 128))
            total_2 = jnp.broadcast_to(got[:, 1:2] + got[:, 2:3], (128, 128))
            top = jnp.maximum(top_1, top_2)
            factor_1, factor_2 = jnp.exp2(top_1 - top), jnp.exp2(top_2 - top)
            total = factor_1 * total_1 + factor_2 * total_2
            for i in range(4):
                lanes = slice(128 * i, 128 * i + 128)
                value = factor_1 * kept[slot, rows, lanes].astype(jnp.float32)
                value += factor_2 * from_sib[slot % 4, rows, lanes].astype(jnp.float32)
                kept[slot, rows, lanes] = value.astype(jnp.bfloat16)
            for i, value in enumerate((top, total)):
                value = jnp.swapaxes(value, 0, 1)[0:16]
                stats[i, db] = jnp.where(row16 == 4 * da + s, value, stats[i, db])

    def give_credit():
        pl.semaphore_signal(credit, inc=1, device_id={"ctx": sibling}, device_id_type=MESH)

    def iteration(slot, carry):
        place = slot % 2

        def first_row(at):
            for flow in range(2):
                arrive(flow, at)
                if at == 1 + flow:
                    a_copy(flow, 3).start()
                b_copy(flow, 4 + at, 1).start()
                b_copy(flow, 8 + at, 2).start()
                sib_copy(flow, at).start()

        @pl.when(slot == 1)
        def _():
            first_row(1)
            first_row(2)

        @pl.when(slot == 2)
        def _():
            first_row(3)

        @pl.when((slot >= 2) & (slot < 14))
        def _():
            for flow in range(2):
                arrive(flow, slot + 2)

        @pl.when((slot >= 2) & (slot < 6))
        def _():
            b_copy(0, slot + 10, 3).start()

        @pl.when((slot >= 6) & (slot < 10))
        def _():
            b_copy(1, slot + 6, 3).start()

        @pl.when((slot >= 2) & (slot < 14))
        def _():
            for flow in range(2):
                sib_copy(flow, slot + 2).start()

        @pl.when(slot < slots - 1)
        def _():
            for copy in key_copies(slot + 1, 1 - place):
                copy.start()

        for copy in key_copies(slot, place):
            copy.wait()
        db = spread(slot // 4)
        keys[place, 0, 576:key_rows] = mask_own[db]
        keys[place, 1, 576:key_rows] = mask_sib[db]

        query = jnp.concatenate([own[0, slot], own[1, slot]], axis=1)
        mixed, top, total = attend_unit(keys[place, 0], query)
        kept[slot] = mixed
        own_stat[place, 0] = jnp.broadcast_to(top, (512, 128))
        own_stat[place, 1] = jnp.broadcast_to(total, (512, 128))

        for flow in range(2):
            sib_copy(flow, slot).wait_recv()

        @pl.when(slot >= 2)
        def _():
            part_copy(slot).wait_send()

        query = jnp.concatenate([sib[0, slot], sib[1, slot]], axis=1)
        mixed, top, total = attend_unit(keys[place, 1], query)
        to_sib[place, :, 0:512] = mixed
        to_sib[place, :, 512:640] = pack_stats(top, total)

        @pl.when(slot >= 4)
        def _():
            pl.semaphore_wait(credit, 1)

        part_copy(slot).start()

        @pl.when(slot > 0)
        def _():
            combine(slot - 1)

        @pl.when((slot > 0) & (slot < 13))
        def _():
            give_credit()

        @pl.when(slot == 8)
        def _():
            for piece in (0, 3):
                far_copy(piece).wait_recv()
                pass_copy(piece).start()
            far_copy(4).start()
            far_copy(5).start()

        @pl.when(slot == 12)
        def _():
            for piece in (1, 2):
                far_copy(piece).wait_recv()
                pass_copy(piece).start()

        return carry

    stats[...] = jnp.zeros_like(stats)
    lax.fori_loop(0, slots, iteration, 0)

    def up_copy(gi):
        src = up_ref if gi == 0 else far_up.at[gi - 1]
        return pltpu.make_async_copy(src, up.at[gi % 2], up_sem.at[gi % 2])

    def fill_group(gi):
        first_head = pl.multiple_of(32 * ((group + ahead_of[gi]) % 4), 32)

        def fill_wide(slot, carry):
            place = 4 * spread(slot // 4) + spread(slot % 4)
            for s in range(4):
                rows = pl.ds(pl.multiple_of(128 * s + first_head, 32), 32)
                value = kept[slot, rows].astype(jnp.float32)
                at = pl.ds(pl.multiple_of(32 * (4 * place + s), 32), 32)
                for i in range(4):
                    wide[i, at] = value[:, 128 * i : 128 * i + 128]
            return carry

        lax.fori_loop(0, slots, fill_wide, 0)

    def product(gi, head):
        rows = [wide[i, pl.ds(head, 64, stride=32), :] for i in range(4)]
        rows = jnp.concatenate(rows, axis=1).astype(jnp.bfloat16)
        return jnp.dot(rows, up[gi % 2, head], preferred_element_type=jnp.float32)

    def scaled(gi, head, value, weight):
        lane = 32 * ahead_of[gi] + head
        return value * weight[:, lane : lane + 1]

    def store(gi, head, value):
        lanes = slice(128 * (head % 16), 128 * (head % 16) + 128)
        for db in range(4):
            partial[head // 16, gi, db, :, lanes] = value[16 * db : 16 * db + 16].astype(jnp.bfloat16)

    ahead_of = (0, 3, 1, 2)
    up_copy(0).start()
    combine(slots - 1)
    for d in (1, 2, 3):
        stat_a_copy(d).start()
    for piece in (0, 1):
        pass_copy(piece).wait_recv()
    up_copy(1).start()
    fill_group(0)
    up_copy(0).wait()
    for d in (1, 2, 3):
        stat_a_copy(d).wait_recv()
    for db in range(4):
        parts = [(stats[0, db], stats[1, db])]
        for d in (1, 2, 3):
            parts.append(tuple(roll_rows(stats_a[d - 1, i, db], 4 * d) for i in range(2)))
        stats_mid[0, db], stats_mid[1, db] = merge_stats(parts)
    for d in (1, 2, 3):
        stat_b_copy(d).start()
    for head in range(32):
        raw[head] = product(0, head)
    for piece in (4, 5):
        far_copy(piece).wait_recv()
        pass_copy(piece).start()
    for d in (1, 2, 3):
        stat_b_copy(d).wait_recv()
    for db in range(4):
        parts = [(stats_mid[0, db], stats_mid[1, db])]
        for d in (1, 2, 3):
            parts.append((stats_b[d - 1, 0, (db - d) % 4], stats_b[d - 1, 1, (db - d) % 4]))
        top, total = merge_stats(parts)
        value = jnp.exp2(stats[0, db] - top) / total
        turned = value
        for z in (1, 2, 3):
            shifted = jnp.concatenate([value[:, 32 * z :], value[:, : 32 * z]], axis=1)
            turned = jnp.where(group == z, shifted, turned)
        factor[16 * db : 16 * db + 16] = turned

    def chain(gi):
        for half in range(2):
            by = 3 if half == 0 else 1
            ring_copy(half, gi, 2).wait_recv()
            value = partial[half, gi, by].astype(jnp.float32)
            value += ring_in[half, gi, 1].astype(jnp.float32)
            partial[half, gi, by] = value.astype(jnp.bfloat16)
            ring_copy(half, gi, by).start()

    for gi in range(4):
        if gi:
            up_copy(gi).wait()
            fill_group(gi)
        weight = factor[...]
        for head in range(32):
            value = raw[head] if gi == 0 else product(gi, head)
            store(gi, head, scaled(gi, head, value, weight))
            if head % 16 == 15:
                half = head // 16
                ring_copy(half, gi, 2).start()
                ring_copy(half, gi, 1 if half == 0 else 3).start()
        if gi == 0:
            for piece in (2, 3):
                pass_copy(piece).wait_recv()
            up_copy(2).start()
        if gi == 1:
            for piece in (4, 5):
                pass_copy(piece).wait_recv()
            up_copy(3).start()
        if gi >= 1:
            chain(gi - 1)
    chain(3)

    whole = []
    for half in range(2):
        ends = []
        for gi in range(4):
            ring_copy(half, gi, 1).wait_recv()
            ring_copy(half, gi, 3).wait_recv()
            value = partial[half, gi, 0].astype(jnp.float32)
            value += ring_in[half, gi, 0].astype(jnp.float32)
            ends.append(value + ring_in[half, gi, 2].astype(jnp.float32))
        for da in (1, 2, 3):
            rows = [end[4 * da : 4 * da + 4] for end in ends]
            last_out[half, da - 1] = jnp.concatenate(rows, axis=0).astype(jnp.bfloat16)
            last_copy(half, da).start()
        whole.append(jnp.concatenate([end[0:4] for end in ends], axis=0))
    for half in range(2):
        for da in (1, 2, 3):
            last_copy(half, da).wait_recv()
            whole[half] = whole[half] + last_in[half, da - 1].astype(jnp.float32)
    for gi in range(4):
        picked = [value[4 * gi : 4 * gi + 4] for value in whole]
        out_ref[gi] = jnp.concatenate(picked, axis=0)

    for flow in range(2):
        def drain(slot, carry):
            sib_copy(flow, slot).wait_send()
            return carry

        lax.fori_loop(0, slots, drain, 0)
        part_copy(14 + flow).wait_send()
        for slot in range(4, 16):
            b_copy(flow, slot, slot // 4).wait_send()
        for da in (1, 2, 3):
            a_copy(flow, da).wait_send()
            last_copy(flow, da).wait_send()
            for gi in range(4):
                ring_copy(flow, gi, da).wait_send()
    for piece in range(6):
        far_copy(piece).wait_send()
        pass_copy(piece).wait_send()
    for d in (1, 2, 3):
        stat_a_copy(d).wait_send()
        stat_b_copy(d).wait_send()
    for copy in ones + twos + [three]:
        copy.wait_send()


def gather_attend(span_map, lengths, top_rows, query_t, cache_t, up_weight):
    dma = pltpu.SemaphoreType.DMA
    bf16, f32 = jnp.bfloat16, jnp.float32
    return pl.pallas_call(
        gather_attend_kernel,
        in_specs=[pl.BlockSpec(memory_space=pltpu.SMEM)] * 2
        + [pl.BlockSpec(memory_space=pltpu.VMEM)]
        + [pl.BlockSpec(memory_space=pl.ANY)] * 3,
        out_specs=[pl.BlockSpec(memory_space=pltpu.VMEM), pl.BlockSpec(memory_space=pl.ANY)],
        out_shape=[
            jax.ShapeDtypeStruct((4, 8, 2048), f32),
            jax.ShapeDtypeStruct((3,) + up_weight.shape, bf16),
        ],
        scratch_shapes=[
            pltpu.VMEM((2, slots, key_rows, 256), bf16),
            pltpu.VMEM((2, slots, key_rows, 256), bf16),
            pltpu.VMEM((slots, 512, 512), bf16),
            pltpu.VMEM((2, 512, 640), bf16),
            pltpu.VMEM((4, 512, 640), bf16),
            pltpu.VMEM((2, 2, 512, 128), f32),
            pltpu.VMEM((2, 2, key_rows, 512), bf16),
            pltpu.VMEM((4, 2048), jnp.int32),
            pltpu.VMEM((4, 2048), jnp.int32),
            pltpu.VMEM((4, 2, 16, 512), bf16),
            pltpu.VMEM((4, 2, 16, 512), bf16),
            pltpu.VMEM((4, 2, 16, 512), bf16),
            pltpu.VMEM((4, 2, 16, 512), bf16),
            pltpu.VMEM((8, 16, 512), bf16),
            pltpu.VMEM((4, 16, 512), bf16),
            pltpu.VMEM((2, 4, 16, 128), f32),
            pltpu.VMEM((3, 2, 4, 16, 128), f32),
            pltpu.VMEM((2, 4, 16, 128), f32),
            pltpu.VMEM((3, 2, 4, 16, 128), f32),
            pltpu.VMEM((64, 128), f32),
            pltpu.VMEM((2, 32, 512, 128), bf16),
            pltpu.VMEM((4, 2048, 128), f32),
            pltpu.VMEM((32, 64, 128), f32),
            pltpu.VMEM((2, 4, 4, 16, 2048), bf16),
            pltpu.VMEM((2, 4, 3, 16, 2048), bf16),
            pltpu.VMEM((2, 3, 16, 2048), bf16),
            pltpu.VMEM((2, 3, 16, 2048), bf16),
            dma((3,)),
            dma((3,)),
            dma((3,)),
            dma((3,)),
            dma,
            dma,
            dma((2, 2)),
            dma((2, 2)),
            dma((2, slots)),
            dma((2, slots)),
            dma((2, 3)),
            dma((2, 12)),
            dma((2, slots)),
            dma((2,)),
            dma((4,)),
            pltpu.SemaphoreType.REGULAR,
            dma((6,)),
            dma((6,)),
            dma((6,)),
            dma((6,)),
            dma((2,)),
            dma((3,)),
            dma((3,)),
            dma((3,)),
            dma((3,)),
            dma((2, 4, 3)),
            dma((2, 4, 3)),
            dma((2, 3)),
            dma((2, 3)),
        ],
        compiler_params=pltpu.CompilerParams(
            collective_id=0, has_side_effects=True, vmem_limit_bytes=60 * 2**20
        ),
        cost_estimate=pl.CostEstimate(
            flops=19_000_000_000, bytes_accessed=60_000_000, transcendentals=8_000_000
        ),
    )(span_map, lengths, top_rows, query_t, cache_t, up_weight)[0]


def project_kernel(
    head_ref, out_weight_ref, out_ref,
    taken, weight, values, sums, give, get,
    load_sem, take_send, take_recv, own_recv, sib_recv, a_send, b_send, sib_send,
    give_send, give_recv,
):
    me = lax.axis_index("ctx")
    group = lax.axis_index("req")
    core = me % 2
    chip = me // 2
    a_step = 4 - 3 * core
    b_step = 1 + 3 * core
    a = (chip // a_step) % 4
    b = (chip // b_step) % 4

    def device(da, db):
        return {"ctx": (((a + da) % 4) * a_step + ((b + db) % 4) * b_step) * 2 + core}

    def plane(d):
        return {"req": (group + d) % 4}

    sibling = {"ctx": chip * 2 + 1 - core}
    partners = [device(1, 0), device(3, 0), device(0, 1), device(0, 3), sibling]
    partners += [plane(1), plane(2), plane(3)]
    barrier = pltpu.get_barrier_semaphore()
    for partner in partners:
        pl.semaphore_signal(barrier, inc=1, device_id=partner, device_id_type=MESH)

    def remote(src, dst, send, recv, target):
        return pltpu.make_async_remote_copy(
            src_ref=src, dst_ref=dst, send_sem=send, recv_sem=recv,
            device_id=target, device_id_type=MESH)

    loads = [
        pltpu.make_async_copy(head_ref.at[0], taken.at[0], load_sem.at[0]),
        pltpu.make_async_copy(out_weight_ref, weight.at[pl.ds(0, 224)], load_sem.at[1]),
    ]
    for copy in loads:
        copy.start()
    pl.semaphore_wait(barrier, len(partners))
    takes = [
        remote(head_ref.at[(0, 2, 3, 1)[d]], taken.at[d], take_send.at[d - 1],
               take_recv.at[d - 1], plane(d))
        for d in (1, 2, 3)
    ]
    for copy in takes:
        copy.start()

    weight[224:256] = jnp.zeros((32, 4096), jnp.bfloat16)
    loads[0].wait()
    for copy in takes:
        copy.wait_recv()

    def a_copy(flow, slot):
        source, side_step = ((0, 1), (0, 3), (1, 1) if flow == 0 else (2, 3))[slot - 1]
        return remote(values.at[flow, source, 0], values.at[flow, slot, 0],
                      a_send.at[flow, slot - 1], own_recv.at[flow, slot], device(side_step, 0))

    def b_copy(flow, slot):
        back, side_step = ((4, 1), (8, 3), (8, 1) if flow == 0 else (4, 3))[slot // 4 - 1]
        return remote(values.at[flow, slot - back, 0], values.at[flow, slot, 0],
                      b_send.at[flow, slot - 4], own_recv.at[flow, slot], device(0, side_step))

    def sib_copy(flow, slot):
        return remote(values.at[flow, slot, 0], values.at[flow, slot, 1],
                      sib_send.at[flow, slot], sib_recv.at[flow, slot], sibling)

    def forward(flow, slot):
        if slot == 0:
            a_copy(flow, 1).start()
            a_copy(flow, 2).start()
        if slot == 1 + flow:
            a_copy(flow, 3).start()
        if slot < 4:
            b_copy(flow, slot + 4).start()
            b_copy(flow, slot + 8).start()
        elif slot // 4 == 1 + flow:
            b_copy(flow, slot + (4 if flow else 8)).start()
        sib_copy(flow, slot).start()

    for flow in range(2):
        rows = [taken[d, 4 * flow : 4 * flow + 4] for d in range(4)]
        values[flow, 0, 0] = jnp.concatenate(rows, axis=0).astype(jnp.bfloat16)
        forward(flow, 0)

    loads[1].wait()
    for slot in range(slots):
        for flow in range(2):
            if slot:
                (a_copy if slot < 4 else b_copy)(flow, slot).wait_recv()
                forward(flow, slot)
        if slot % 4 != 3:
            continue
        row = slot // 4
        db = spread(row)
        left = []
        for flow in range(2):
            for i in range(4):
                sib_copy(flow, 4 * row + i).wait_recv()
            left.append(values[flow, 4 * row : 4 * row + 4].reshape(128, 2048))
        term = lax.dot_general(
            jnp.concatenate(left, axis=1), weight[...],
            (((1,), (1,)), ((), ())), preferred_element_type=jnp.float32)
        for i in range(4):
            ua, ub = 4 - spread(i), 4 - db
            origins = (
                (((a + ua) % 4) * a_step + ((b + ub) % 4) * b_step) * 2 + core,
                (((b + ua) % 4) * b_step + ((a + ub) % 4) * a_step) * 2 + 1 - core,
            )
            for which, origin in enumerate(origins):
                at = 16 * (2 * i + which)
                place = pl.ds(pl.multiple_of(origin * 16, 16), 16)
                for half in range(2):
                    sums[half, place] = term[at : at + 16, 128 * half : 128 * half + 128]

    def share(d, s):
        return jnp.concatenate(
            [sums[i, pl.ds(4 * d + s, 32, stride=16), :] for i in range(2)], axis=1)

    gives = []
    for d in (1, 2, 3):
        for s in range(4):
            give[d - 1, s] = share(d, s).astype(jnp.bfloat16)
        copy = remote(give.at[d - 1], get.at[d - 1], give_send.at[d - 1], give_recv.at[d - 1],
                      plane(4 - d))
        copy.start()
        gives.append(copy)
    for copy in gives:
        copy.wait_recv()
    for s in range(4):
        total = share(0, s)
        for i in range(3):
            total = total + get[i, s].astype(jnp.float32)
        out_ref[s] = total[:, :224].astype(jnp.bfloat16)

    for copy in takes + gives:
        copy.wait_send()
    for flow in range(2):
        for slot in range(slots):
            sib_copy(flow, slot).wait_send()
            if 0 < slot < 4:
                a_copy(flow, slot).wait_send()
            if slot >= 4:
                b_copy(flow, slot).wait_send()


def project(head_values, out_weight_t):
    dma = pltpu.SemaphoreType.DMA
    bf16, f32 = jnp.bfloat16, jnp.float32
    return pl.pallas_call(
        project_kernel,
        in_specs=[pl.BlockSpec(memory_space=pl.ANY)] * 2,
        out_specs=pl.BlockSpec(memory_space=pltpu.VMEM),
        out_shape=jax.ShapeDtypeStruct((4, 32, 224), bf16),
        scratch_shapes=[
            pltpu.VMEM((4, 8, 2048), f32),
            pltpu.VMEM((256, 4096), bf16),
            pltpu.VMEM((2, slots, 2, 16, 2048), bf16),
            pltpu.VMEM((2, 512, 128), f32),
            pltpu.VMEM((3, 4, 32, 256), bf16),
            pltpu.VMEM((3, 4, 32, 256), bf16),
            dma((2,)),
            dma((3,)),
            dma((3,)),
            dma((2, slots)),
            dma((2, slots)),
            dma((2, 3)),
            dma((2, 12)),
            dma((2, slots)),
            dma((3,)),
            dma((3,)),
        ],
        compiler_params=pltpu.CompilerParams(
            collective_id=1, has_side_effects=True, vmem_limit_bytes=40 * 2**20
        ),
        cost_estimate=pl.CostEstimate(
            flops=1_100_000_000, bytes_accessed=8_000_000, transcendentals=0
        ),
    )(head_values, out_weight_t)


def per_device(queries, top_rows, lengths, span_map, latent_cache, up_weight, out_weight):
    query_t = jnp.swapaxes(queries, 2, 3)[0]
    cache_t = jnp.swapaxes(latent_cache, 1, 2)
    head_values = gather_attend(span_map, lengths, top_rows[0], query_t, cache_t, up_weight)
    out = project(head_values, out_weight.T)
    return jnp.swapaxes(out, 0, 1)


def solution(mesh):
    return jax.shard_map(
        per_device,
        mesh=mesh,
        in_specs=(
            P(("req", "ctx"), None, None, None),
            P(("req", "ctx"), None, None),
            P(("req", "ctx")),
            P(),
            P("req", "ctx", None),
            P("req", None, None),
            P("req", "ctx"),
        ),
        out_specs=P("req", None, "ctx"),
        check_vma=False,
    )
```

```python
import functools

import jax
import jax.numpy as jnp
from jax import lax
from jax.experimental import pallas as pl
from jax.experimental.pallas import tpu as pltpu
from jax.sharding import PartitionSpec as P

score_scale = 192.0 ** (-0.5)
log2_scale = score_scale * 1.4426950408889634
masked = -1e30
lowest = -16384.0


MESH = pl.DeviceIdType.MESH
side = 4
slots = side * side
key_rows = 592
latent_rows = 512


def attend_unit(keys, query):
    scores = lax.dot_general(
        query, keys, (((0,), (0,)), ((), ())), preferred_element_type=jnp.float32
    )
    top = jnp.max(scores, axis=1, keepdims=True) * log2_scale
    top = jnp.maximum(top, lowest).astype(jnp.bfloat16).astype(jnp.float32)
    weights = jnp.exp2(scores * log2_scale - top)
    total = jnp.sum(weights, axis=1, keepdims=True)
    mixed = lax.dot_general(
        weights.astype(jnp.bfloat16),
        keys[:latent_rows],
        (((1,), (1,)), ((), ())),
        preferred_element_type=jnp.float32,
    )
    return mixed.astype(jnp.bfloat16), top, total


def pack_stats(top, total):
    lane = lax.broadcasted_iota(jnp.int32, (top.shape[0], 128), 1)
    high = total.astype(jnp.bfloat16).astype(jnp.float32)
    packed = jnp.where(lane == 0, top, jnp.where(lane == 1, high, total - high))
    return packed.astype(jnp.bfloat16)


def spread(i):
    return i + (i // 2) * (5 - 2 * i)


def row_of(slot):
    middle = ((slot // 4) % 3 + 1) // 2
    return (1 - middle) * (slot // 4) + middle * (1 + slot % 2)


def column_of(slot):
    middle = ((slot // 4) % 3 + 1) // 2
    return (1 - middle) * (slot % 4) + middle * ((slot + 4) // 2 - 4)


def merge_stats(stats):
    top = functools.reduce(jnp.maximum, [t for t, _ in stats])
    return top, sum(jnp.exp2(t - top) * l for t, l in stats)


def roll_rows(block, count):
    size = block.shape[0]
    return jnp.concatenate([block[size - count :], block[: size - count]], axis=0)


def make_mask(span_ref, length_ref, rows_ref, line, place_in, mask_one, core, a, b):
    picks = rows_ref[...]
    block = picks // 256
    holder = jnp.zeros_like(block)
    for c in range(64):
        holder = jnp.where(block == c, span_ref[c], holder)
    place_in[...] = jnp.where(block >= 32, 256, 0) + picks % 256
    x, y = holder // 8, (holder // 2) % 4
    ea = (x * (1 - core) + y * core - a + 4) % 4
    eb = (y * (1 - core) + x * core - b + 4) % 4
    ec = (holder + core) % 2
    step = lax.broadcasted_iota(jnp.int32, picks.shape, 0)
    limit = length_ref[0] - 3 + step
    line[...] = jnp.where(picks < limit, 32 * ea + 16 * ec + 4 * eb + step, -1)

    def chunk(i, count):
        columns = pl.ds(pl.multiple_of(i * 512, 512), 512)
        for s in range(4):
            left = lax.broadcasted_iota(jnp.int32, (128, 512), 0) == line[s : s + 1, columns]
            right = lax.broadcasted_iota(jnp.int32, (512, 512), 0) == place_in[s : s + 1, columns]
            count += lax.dot_general(
                left.astype(jnp.float32).astype(jnp.bfloat16),
                right.astype(jnp.float32).astype(jnp.bfloat16),
                (((1,), (1,)), ((), ())), preferred_element_type=jnp.float32)
        return count

    count = lax.fori_loop(0, 4, chunk, jnp.zeros((128, 512), jnp.float32))
    bias = jnp.where(count > 0.5, 0.0, masked).astype(jnp.bfloat16)
    mask_one[...] = bias.reshape(4, 2, 16, 512)


def gather_attend_kernel(
    span_ref, length_ref, rows_ref, query_ref, cache_ref, up_ref, out_ref, far_up,
    own, sib, kept, to_sib, from_sib, own_stat, keys,
    line, place_in, mask_one, mask_mid, mask_two, mask_got, mask_own, mask_sib,
    stats, stats_a, stats_mid, stats_b, factor, up, wide, raw, partial, ring_in, last_out, last_in,
    one_send, one_recv, two_send, two_recv, three_send, three_recv,
    load_sem, key_sem, own_recv, sib_recv, a_send, b_send, sib_send,
    part_send, part_recv, credit, far_send, far_recv, pass_send, pass_recv, up_sem,
    stat_a_send, stat_a_recv, stat_b_send, stat_b_recv,
    ring_send, ring_recv, last_send, last_recv,
):
    me = lax.axis_index("ctx")
    core = me % 2
    chip = me // 2
    a_step = 4 - 3 * core
    b_step = 1 + 3 * core
    a = (chip // a_step) % 4
    b = (chip // b_step) % 4

    def device(da, db):
        return (((a + da + 4) % 4) * a_step + ((b + db + 4) % 4) * b_step) * 2 + core

    group = lax.axis_index("req")
    sibling = chip * 2 + 1 - core
    barrier = pltpu.get_barrier_semaphore()
    partners = [device(d, 0) for d in (1, 2, 3)] + [device(0, d) for d in (1, 2, 3)] + [sibling]
    partners = [{"ctx": partner} for partner in partners]
    partners += [{"req": (group + 1) % 4}, {"req": (group + 3) % 4}]
    for partner in partners:
        pl.semaphore_signal(barrier, inc=1, device_id=partner, device_id_type=MESH)

    def requests(slot):
        ua, ub = 4 - spread(column_of(slot)), 4 - spread(row_of(slot))
        return (
            (((a + ua) % 4) * a_step + ((b + ub) % 4) * b_step) * 2 + core,
            (((b + ua) % 4) * b_step + ((a + ub) % 4) * a_step) * 2 + 1 - core,
        )

    def key_copies(slot, place):
        return [
            pltpu.make_async_copy(
                cache_ref.at[request], keys.at[place, which, pl.ds(0, 576)],
                key_sem.at[place, which])
            for which, request in enumerate(requests(slot))
        ]

    def remote(src, dst, send, recv, target):
        return pltpu.make_async_remote_copy(
            src_ref=src, dst_ref=dst, send_sem=send, recv_sem=recv,
            device_id={"ctx": target}, device_id_type=MESH)

    body = pl.ds(0, 576)

    def a_copy(flow, slot):
        source, side_step = ((0, 1), (0, 3), (1, 1) if flow == 0 else (2, 3))[slot - 1]
        return remote(own.at[flow, source, body], own.at[flow, slot, body],
                      a_send.at[flow, slot - 1], own_recv.at[flow, slot], device(side_step, 0))

    def b_copy(flow, source, slot, side_step):
        return remote(own.at[flow, source, body], own.at[flow, slot, body],
                      b_send.at[flow, slot - 4], own_recv.at[flow, slot], device(0, side_step))

    def arrive(flow, slot):
        place = own.at[flow, slot, body]
        remote(place, place, sib_send.at[flow, slot], own_recv.at[flow, slot], sibling).wait_recv()

    def sib_copy(flow, slot):
        return remote(own.at[flow, slot, body], sib.at[flow, slot, body],
                      sib_send.at[flow, slot], sib_recv.at[flow, slot], sibling)

    def part_copy(slot):
        return remote(to_sib.at[slot % 2], from_sib.at[slot % 4],
                      part_send.at[slot % 2], part_recv.at[slot % 4], sibling)

    def far_copy(piece):
        quarter = pl.ds(16 * core + 8 * (piece % 2), 8)
        if piece < 4:
            src, ahead_z = up_ref.at[quarter], (1 if piece < 2 else 3)
        else:
            src = far_up.at[0 if piece == 4 else 1, quarter]
            ahead_z = 1 if piece == 4 else 3
        return pltpu.make_async_remote_copy(
            src_ref=src, dst_ref=far_up.at[piece // 2, quarter],
            send_sem=far_send.at[piece], recv_sem=far_recv.at[piece],
            device_id={"req": (group + ahead_z) % 4}, device_id_type=MESH)

    def pass_copy(piece):
        quarter = far_up.at[piece // 2, pl.ds(16 * core + 8 * (piece % 2), 8)]
        return remote(quarter, quarter, pass_send.at[piece], pass_recv.at[piece], sibling)

    def stat_a_copy(d):
        return remote(stats, stats_a.at[d - 1], stat_a_send.at[d - 1], stat_a_recv.at[d - 1],
                      device(d, 0))

    def stat_b_copy(d):
        return remote(stats_mid, stats_b.at[d - 1], stat_b_send.at[d - 1],
                      stat_b_recv.at[d - 1], device(0, d))

    def ring_copy(half, gi, db):
        side_step = (3, 1 if half == 0 else 3, 1)[db - 1]
        return remote(partial.at[half, gi, db], ring_in.at[half, gi, db - 1],
                      ring_send.at[half, gi, db - 1], ring_recv.at[half, gi, db - 1],
                      device(0, side_step))

    def last_copy(half, da):
        return remote(last_out.at[half, da - 1], last_in.at[half, da - 1],
                      last_send.at[half, da - 1], last_recv.at[half, da - 1], device(-da, 0))

    loads = [
        pltpu.make_async_copy(
            query_ref.at[2 * flow + half],
            own.at[flow, 0, body, pl.ds(128 * half, 128)],
            load_sem.at[flow, half])
        for flow in range(2) for half in range(2)
    ]
    for copy in loads:
        copy.start()
    for copy in key_copies(0, 0):
        copy.start()

    make_mask(span_ref, length_ref, rows_ref, line, place_in, mask_one, core, a, b)

    row = lax.broadcasted_iota(jnp.int32, (16, 256), 0)
    step = lax.broadcasted_iota(jnp.int32, (16, 256), 1) // 128
    for flow in range(2):

        def fill(slot, carry):
            da = spread(column_of(slot))
            hot = jnp.where(row == step + 2 * flow + 4 * da, 1.0, 0.0).astype(jnp.bfloat16)
            own[flow, slot, 576:key_rows] = hot
            sib[flow, slot, 576:key_rows] = hot
            return carry

        lax.fori_loop(0, slots, fill, 0)
    for copy in loads:
        copy.wait()
    pl.semaphore_wait(barrier, len(partners))

    ones = [remote(mask_one.at[d], mask_mid.at[d], one_send.at[d - 1], one_recv.at[d - 1],
                   device(d, 0)) for d in (1, 2, 3)]
    for copy in ones:
        copy.start()
    for piece in (0, 3, 1, 2):
        far_copy(piece).start()
    for flow in range(2):
        for slot in (1, 2):
            a_copy(flow, slot).start()
        b_copy(flow, 0, 4, 1).start()
        b_copy(flow, 0, 5, 3).start()
        sib_copy(flow, 0).start()
    for copy in ones:
        copy.wait_recv()
    for which in range(2):
        lists = [mask_one[0, which].astype(jnp.float32)]
        lists += [mask_mid[d, which].astype(jnp.float32) for d in (1, 2, 3)]
        for eb in range(4):
            rows = [part[4 * eb : 4 * eb + 4] for part in lists]
            mask_two[eb, which] = jnp.concatenate(rows, axis=0).astype(jnp.bfloat16)
    twos = [remote(mask_two.at[d], mask_got.at[d], two_send.at[d - 1], two_recv.at[d - 1],
                   device(0, d)) for d in (1, 2, 3)]
    for copy in twos:
        copy.start()
    for copy in twos:
        copy.wait_recv()
    mask_own[0] = mask_two[0, 0]
    mask_own[4] = mask_two[0, 1]
    for d in (1, 2, 3):
        mask_own[d] = mask_got[d, 0]
        mask_own[4 + d] = mask_got[d, 1]
    three = remote(mask_own.at[pl.ds(4, 4)], mask_sib, three_send, three_recv, sibling)
    three.start()
    three.wait_recv()

    row16 = lax.broadcasted_iota(jnp.int32, (16, 128), 0)
    lane = lax.broadcasted_iota(jnp.int32, (128, 128), 1)

    def combine(slot):
        db, da = spread(row_of(slot)), spread(column_of(slot))
        part_copy(slot).wait_recv()
        for s in range(4):
            rows = slice(128 * s, 128 * s + 128)
            got = from_sib[slot % 4, rows, 512:640].astype(jnp.float32)
            top_1, total_1 = own_stat[slot % 2, 0, rows], own_stat[slot % 2, 1, rows]
            top_2 = jnp.broadcast_to(got[:, 0:1], (128, 128))
            total_2 = jnp.broadcast_to(got[:, 1:2] + got[:, 2:3], (128, 128))
            top = jnp.maximum(top_1, top_2)
            factor_1, factor_2 = jnp.exp2(top_1 - top), jnp.exp2(top_2 - top)
            total = factor_1 * total_1 + factor_2 * total_2
            for i in range(4):
                lanes = slice(128 * i, 128 * i + 128)
                value = factor_1 * kept[slot, rows, lanes].astype(jnp.float32)
                value += factor_2 * from_sib[slot % 4, rows, lanes].astype(jnp.float32)
                kept[slot, rows, lanes] = value.astype(jnp.bfloat16)
            both = jnp.swapaxes(jnp.where(lane < 64, top, total), 0, 1)
            for i in range(2):
                value = both[64 * i : 64 * i + 16]
                stats[i, db] = jnp.where(row16 == 4 * da + s, value, stats[i, db])

    def give_credit():
        pl.semaphore_signal(credit, inc=1, device_id={"ctx": sibling}, device_id_type=MESH)

    def iteration(slot, carry):
        place = slot % 2

        def first_row(at):
            for flow in range(2):
                arrive(flow, at)
                if at == 1 + flow:
                    a_copy(flow, 3).start()
                b_copy(flow, at, 4 + 2 * at, 1).start()
                b_copy(flow, at, 5 + 2 * at, 3).start()
                sib_copy(flow, at).start()

        @pl.when(slot == 1)
        def _():
            first_row(1)
            first_row(2)

        @pl.when(slot == 2)
        def _():
            first_row(3)

        @pl.when((slot >= 2) & (slot < 10))
        def _():
            for flow in range(2):
                arrive(flow, slot + 2)

        @pl.when((slot >= 2) & (slot < 10) & (slot % 2 == 0))
        def _():
            b_copy(0, slot + 2, 11 + slot // 2, 1).start()

        @pl.when((slot >= 2) & (slot < 10) & (slot % 2 == 1))
        def _():
            b_copy(1, slot + 2, 11 + slot // 2, 3).start()

        @pl.when((slot >= 2) & (slot < 10))
        def _():
            for flow in range(2):
                sib_copy(flow, slot + 2).start()

        @pl.when(slot >= 12)
        def _():
            for flow in range(2):
                arrive(flow, slot)
                sib_copy(flow, slot).start()

        @pl.when(slot < slots - 1)
        def _():
            for copy in key_copies(slot + 1, 1 - place):
                copy.start()

        for copy in key_copies(slot, place):
            copy.wait()
        db = spread(row_of(slot))
        keys[place, 0, 576:key_rows] = mask_own[db]
        keys[place, 1, 576:key_rows] = mask_sib[db]

        query = jnp.concatenate([own[0, slot], own[1, slot]], axis=1)
        mixed, top, total = attend_unit(keys[place, 0], query)
        kept[slot] = mixed
        own_stat[place, 0] = jnp.broadcast_to(top, (512, 128))
        own_stat[place, 1] = jnp.broadcast_to(total, (512, 128))

        for flow in range(2):
            sib_copy(flow, slot).wait_recv()

        @pl.when(slot >= 2)
        def _():
            part_copy(slot).wait_send()

        query = jnp.concatenate([sib[0, slot], sib[1, slot]], axis=1)
        mixed, top, total = attend_unit(keys[place, 1], query)
        to_sib[place, :, 0:512] = mixed
        to_sib[place, :, 512:640] = pack_stats(top, total)

        @pl.when(slot >= 4)
        def _():
            pl.semaphore_wait(credit, 1)

        part_copy(slot).start()

        @pl.when(slot > 0)
        def _():
            combine(slot - 1)

        @pl.when((slot > 0) & (slot < 13))
        def _():
            give_credit()

        @pl.when(slot == 8)
        def _():
            for piece in (0, 3):
                far_copy(piece).wait_recv()
                pass_copy(piece).start()
            far_copy(4).start()
            far_copy(5).start()

        @pl.when(slot == 12)
        def _():
            for piece in (1, 2):
                far_copy(piece).wait_recv()
                pass_copy(piece).start()

        return carry

    stats[...] = jnp.zeros_like(stats)
    lax.fori_loop(0, slots, iteration, 0)

    def up_copy(gi):
        src = up_ref if gi == 0 else far_up.at[gi - 1]
        return pltpu.make_async_copy(src, up.at[gi % 2], up_sem.at[gi % 2])

    def fill_group(gi):
        first_head = pl.multiple_of(32 * ((group + ahead_of[gi]) % 4), 32)

        def fill_wide(slot, carry):
            place = 4 * spread(row_of(slot)) + spread(column_of(slot))
            for s in range(4):
                rows = pl.ds(pl.multiple_of(128 * s + first_head, 32), 32)
                value = kept[slot, rows].astype(jnp.float32)
                at = pl.ds(pl.multiple_of(32 * (4 * place + s), 32), 32)
                for i in range(4):
                    wide[i, at] = value[:, 128 * i : 128 * i + 128]
            return carry

        lax.fori_loop(0, slots, fill_wide, 0)

    def product(gi, head):
        rows = [wide[i, pl.ds(head, 64, stride=32), :] for i in range(4)]
        rows = jnp.concatenate(rows, axis=1).astype(jnp.bfloat16)
        return jnp.dot(rows, up[gi % 2, head], preferred_element_type=jnp.float32)

    def scaled(gi, head, value, weight):
        lane = 32 * ahead_of[gi] + head
        return value * weight[:, lane : lane + 1]

    def store(gi, head, value):
        lanes = slice(128 * (head % 16), 128 * (head % 16) + 128)
        for db in range(4):
            partial[head // 16, gi, db, :, lanes] = value[16 * db : 16 * db + 16].astype(jnp.bfloat16)

    ahead_of = (0, 3, 1, 2)
    up_copy(0).start()
    combine(slots - 1)
    for d in (1, 2, 3):
        stat_a_copy(d).start()
    for piece in (0, 1):
        pass_copy(piece).wait_recv()
    up_copy(1).start()
    fill_group(0)
    up_copy(0).wait()
    for d in (1, 2, 3):
        stat_a_copy(d).wait_recv()
    for db in range(4):
        parts = [(stats[0, db], stats[1, db])]
        for d in (1, 2, 3):
            parts.append(tuple(roll_rows(stats_a[d - 1, i, db], 4 * d) for i in range(2)))
        stats_mid[0, db], stats_mid[1, db] = merge_stats(parts)
    for d in (1, 2, 3):
        stat_b_copy(d).start()
    for head in range(32):
        raw[head] = product(0, head)
    for piece in (4, 5):
        far_copy(piece).wait_recv()
        pass_copy(piece).start()
    for d in (1, 2, 3):
        stat_b_copy(d).wait_recv()
    for db in range(4):
        parts = [(stats_mid[0, db], stats_mid[1, db])]
        for d in (1, 2, 3):
            parts.append((stats_b[d - 1, 0, (db - d) % 4], stats_b[d - 1, 1, (db - d) % 4]))
        top, total = merge_stats(parts)
        value = jnp.exp2(stats[0, db] - top) / total
        turned = value
        for z in (1, 2, 3):
            shifted = jnp.concatenate([value[:, 32 * z :], value[:, : 32 * z]], axis=1)
            turned = jnp.where(group == z, shifted, turned)
        factor[16 * db : 16 * db + 16] = turned

    def chain(gi):
        for half in range(2):
            by = 3 if half == 0 else 1
            ring_copy(half, gi, 2).wait_recv()
            value = partial[half, gi, by].astype(jnp.float32)
            value += ring_in[half, gi, 1].astype(jnp.float32)
            partial[half, gi, by] = value.astype(jnp.bfloat16)
            ring_copy(half, gi, by).start()

    for gi in range(4):
        if gi:
            up_copy(gi).wait()
            fill_group(gi)
        weight = factor[...]
        for head in range(32):
            value = raw[head] if gi == 0 else product(gi, head)
            store(gi, head, scaled(gi, head, value, weight))
            if head % 16 == 15:
                half = head // 16
                ring_copy(half, gi, 2).start()
                ring_copy(half, gi, 1 if half == 0 else 3).start()
        if gi == 0:
            for piece in (2, 3):
                pass_copy(piece).wait_recv()
            up_copy(2).start()
        if gi == 1:
            for piece in (4, 5):
                pass_copy(piece).wait_recv()
            up_copy(3).start()
        if gi >= 1:
            chain(gi - 1)
    chain(3)

    whole = []
    for half in range(2):
        ends = []
        for gi in range(4):
            ring_copy(half, gi, 1).wait_recv()
            ring_copy(half, gi, 3).wait_recv()
            value = partial[half, gi, 0].astype(jnp.float32)
            value += ring_in[half, gi, 0].astype(jnp.float32)
            ends.append(value + ring_in[half, gi, 2].astype(jnp.float32))
        for da in (1, 2, 3):
            rows = [end[4 * da : 4 * da + 4] for end in ends]
            last_out[half, da - 1] = jnp.concatenate(rows, axis=0).astype(jnp.bfloat16)
            last_copy(half, da).start()
        whole.append(jnp.concatenate([end[0:4] for end in ends], axis=0))
    for half in range(2):
        for da in (1, 2, 3):
            last_copy(half, da).wait_recv()
            whole[half] = whole[half] + last_in[half, da - 1].astype(jnp.float32)
    for gi in range(4):
        picked = [value[4 * gi : 4 * gi + 4] for value in whole]
        out_ref[gi] = jnp.concatenate(picked, axis=0)

    for flow in range(2):
        def drain(slot, carry):
            sib_copy(flow, slot).wait_send()
            return carry

        lax.fori_loop(0, slots, drain, 0)
        part_copy(14 + flow).wait_send()
        for slot in range(4, 12):
            b_copy(flow, slot // 2 - 2, slot, 3 if slot % 2 else 1).wait_send()
        for slot in range(12, 16):
            b_copy(flow, 2 * slot - 20 + flow, slot, 3 if flow else 1).wait_send()
        for da in (1, 2, 3):
            a_copy(flow, da).wait_send()
            last_copy(flow, da).wait_send()
            for gi in range(4):
                ring_copy(flow, gi, da).wait_send()
    for piece in range(6):
        far_copy(piece).wait_send()
        pass_copy(piece).wait_send()
    for d in (1, 2, 3):
        stat_a_copy(d).wait_send()
        stat_b_copy(d).wait_send()
    for copy in ones + twos + [three]:
        copy.wait_send()


def gather_attend(span_map, lengths, top_rows, query_t, cache_t, up_weight):
    dma = pltpu.SemaphoreType.DMA
    bf16, f32 = jnp.bfloat16, jnp.float32
    return pl.pallas_call(
        gather_attend_kernel,
        in_specs=[pl.BlockSpec(memory_space=pltpu.SMEM)] * 2
        + [pl.BlockSpec(memory_space=pltpu.VMEM)]
        + [pl.BlockSpec(memory_space=pl.ANY)] * 3,
        out_specs=[pl.BlockSpec(memory_space=pltpu.VMEM), pl.BlockSpec(memory_space=pl.ANY)],
        out_shape=[
            jax.ShapeDtypeStruct((4, 8, 2048), f32),
            jax.ShapeDtypeStruct((3,) + up_weight.shape, bf16),
        ],
        scratch_shapes=[
            pltpu.VMEM((2, slots, key_rows, 256), bf16),
            pltpu.VMEM((2, slots, key_rows, 256), bf16),
            pltpu.VMEM((slots, 512, 512), bf16),
            pltpu.VMEM((2, 512, 640), bf16),
            pltpu.VMEM((4, 512, 640), bf16),
            pltpu.VMEM((2, 2, 512, 128), f32),
            pltpu.VMEM((2, 2, key_rows, 512), bf16),
            pltpu.VMEM((4, 2048), jnp.int32),
            pltpu.VMEM((4, 2048), jnp.int32),
            pltpu.VMEM((4, 2, 16, 512), bf16),
            pltpu.VMEM((4, 2, 16, 512), bf16),
            pltpu.VMEM((4, 2, 16, 512), bf16),
            pltpu.VMEM((4, 2, 16, 512), bf16),
            pltpu.VMEM((8, 16, 512), bf16),
            pltpu.VMEM((4, 16, 512), bf16),
            pltpu.VMEM((2, 4, 16, 128), f32),
            pltpu.VMEM((3, 2, 4, 16, 128), f32),
            pltpu.VMEM((2, 4, 16, 128), f32),
            pltpu.VMEM((3, 2, 4, 16, 128), f32),
            pltpu.VMEM((64, 128), f32),
            pltpu.VMEM((2, 32, 512, 128), bf16),
            pltpu.VMEM((4, 2048, 128), f32),
            pltpu.VMEM((32, 64, 128), f32),
            pltpu.VMEM((2, 4, 4, 16, 2048), bf16),
            pltpu.VMEM((2, 4, 3, 16, 2048), bf16),
            pltpu.VMEM((2, 3, 16, 2048), bf16),
            pltpu.VMEM((2, 3, 16, 2048), bf16),
            dma((3,)),
            dma((3,)),
            dma((3,)),
            dma((3,)),
            dma,
            dma,
            dma((2, 2)),
            dma((2, 2)),
            dma((2, slots)),
            dma((2, slots)),
            dma((2, 3)),
            dma((2, 12)),
            dma((2, slots)),
            dma((2,)),
            dma((4,)),
            pltpu.SemaphoreType.REGULAR,
            dma((6,)),
            dma((6,)),
            dma((6,)),
            dma((6,)),
            dma((2,)),
            dma((3,)),
            dma((3,)),
            dma((3,)),
            dma((3,)),
            dma((2, 4, 3)),
            dma((2, 4, 3)),
            dma((2, 3)),
            dma((2, 3)),
        ],
        compiler_params=pltpu.CompilerParams(
            collective_id=0, has_side_effects=True, vmem_limit_bytes=60 * 2**20
        ),
        cost_estimate=pl.CostEstimate(
            flops=19_000_000_000, bytes_accessed=60_000_000, transcendentals=8_000_000
        ),
    )(span_map, lengths, top_rows, query_t, cache_t, up_weight)[0]


def project_kernel(
    head_ref, out_weight_ref, out_ref,
    taken, weight, values, sums, give, get,
    load_sem, take_send, take_recv, own_recv, sib_recv, a_send, b_send, sib_send,
    give_send, give_recv,
):
    me = lax.axis_index("ctx")
    group = lax.axis_index("req")
    core = me % 2
    chip = me // 2
    a_step = 4 - 3 * core
    b_step = 1 + 3 * core
    a = (chip // a_step) % 4
    b = (chip // b_step) % 4

    def device(da, db):
        return {"ctx": (((a + da) % 4) * a_step + ((b + db) % 4) * b_step) * 2 + core}

    def plane(d):
        return {"req": (group + d) % 4}

    sibling = {"ctx": chip * 2 + 1 - core}
    partners = [device(1, 0), device(3, 0), device(0, 1), device(0, 3), sibling]
    partners += [plane(1), plane(2), plane(3)]
    barrier = pltpu.get_barrier_semaphore()
    for partner in partners:
        pl.semaphore_signal(barrier, inc=1, device_id=partner, device_id_type=MESH)

    def remote(src, dst, send, recv, target):
        return pltpu.make_async_remote_copy(
            src_ref=src, dst_ref=dst, send_sem=send, recv_sem=recv,
            device_id=target, device_id_type=MESH)

    loads = [
        pltpu.make_async_copy(head_ref.at[0], taken.at[0], load_sem.at[0]),
        pltpu.make_async_copy(out_weight_ref, weight.at[pl.ds(0, 224)], load_sem.at[1]),
    ]
    for copy in loads:
        copy.start()
    pl.semaphore_wait(barrier, len(partners))
    takes = [
        remote(head_ref.at[(0, 2, 3, 1)[d]], taken.at[d], take_send.at[d - 1],
               take_recv.at[d - 1], plane(d))
        for d in (1, 2, 3)
    ]
    for copy in takes:
        copy.start()

    weight[224:256] = jnp.zeros((32, 4096), jnp.bfloat16)
    loads[0].wait()
    for copy in takes:
        copy.wait_recv()

    def a_copy(flow, slot):
        source, side_step = ((0, 1), (0, 3), (1, 1) if flow == 0 else (2, 3))[slot - 1]
        return remote(values.at[flow, source, 0], values.at[flow, slot, 0],
                      a_send.at[flow, slot - 1], own_recv.at[flow, slot], device(side_step, 0))

    def b_copy(flow, slot):
        back, side_step = ((4, 1), (8, 3), (8, 1) if flow == 0 else (4, 3))[slot // 4 - 1]
        return remote(values.at[flow, slot - back, 0], values.at[flow, slot, 0],
                      b_send.at[flow, slot - 4], own_recv.at[flow, slot], device(0, side_step))

    def sib_copy(flow, slot):
        return remote(values.at[flow, slot, 0], values.at[flow, slot, 1],
                      sib_send.at[flow, slot], sib_recv.at[flow, slot], sibling)

    def forward(flow, slot):
        if slot == 0:
            a_copy(flow, 1).start()
            a_copy(flow, 2).start()
        if slot == 1 + flow:
            a_copy(flow, 3).start()
        if slot < 4:
            b_copy(flow, slot + 4).start()
            b_copy(flow, slot + 8).start()
        elif slot // 4 == 1 + flow:
            b_copy(flow, slot + (4 if flow else 8)).start()
        sib_copy(flow, slot).start()

    for flow in range(2):
        rows = [taken[d, 4 * flow : 4 * flow + 4] for d in range(4)]
        values[flow, 0, 0] = jnp.concatenate(rows, axis=0).astype(jnp.bfloat16)
        forward(flow, 0)

    loads[1].wait()
    for slot in range(slots):
        for flow in range(2):
            if slot:
                (a_copy if slot < 4 else b_copy)(flow, slot).wait_recv()
                forward(flow, slot)
        if slot % 4 != 3:
            continue
        row = slot // 4
        db = spread(row)
        left = []
        for flow in range(2):
            for i in range(4):
                sib_copy(flow, 4 * row + i).wait_recv()
            left.append(values[flow, 4 * row : 4 * row + 4].reshape(128, 2048))
        term = lax.dot_general(
            jnp.concatenate(left, axis=1), weight[...],
            (((1,), (1,)), ((), ())), preferred_element_type=jnp.float32)
        for i in range(4):
            ua, ub = 4 - spread(i), 4 - db
            origins = (
                (((a + ua) % 4) * a_step + ((b + ub) % 4) * b_step) * 2 + core,
                (((b + ua) % 4) * b_step + ((a + ub) % 4) * a_step) * 2 + 1 - core,
            )
            for which, origin in enumerate(origins):
                at = 16 * (2 * i + which)
                place = pl.ds(pl.multiple_of(origin * 16, 16), 16)
                for half in range(2):
                    sums[half, place] = term[at : at + 16, 128 * half : 128 * half + 128]

    def share(d, s):
        return jnp.concatenate(
            [sums[i, pl.ds(4 * d + s, 32, stride=16), :] for i in range(2)], axis=1)

    gives = []
    for d in (1, 2, 3):
        for s in range(4):
            give[d - 1, s] = share(d, s).astype(jnp.bfloat16)
        copy = remote(give.at[d - 1], get.at[d - 1], give_send.at[d - 1], give_recv.at[d - 1],
                      plane(4 - d))
        copy.start()
        gives.append(copy)
    for copy in gives:
        copy.wait_recv()
    for s in range(4):
        total = share(0, s)
        for i in range(3):
            total = total + get[i, s].astype(jnp.float32)
        out_ref[s] = total[:, :224].astype(jnp.bfloat16)

    for copy in takes + gives:
        copy.wait_send()
    for flow in range(2):
        for slot in range(slots):
            sib_copy(flow, slot).wait_send()
            if 0 < slot < 4:
                a_copy(flow, slot).wait_send()
            if slot >= 4:
                b_copy(flow, slot).wait_send()


def project(head_values, out_weight_t):
    dma = pltpu.SemaphoreType.DMA
    bf16, f32 = jnp.bfloat16, jnp.float32
    return pl.pallas_call(
        project_kernel,
        in_specs=[pl.BlockSpec(memory_space=pl.ANY)] * 2,
        out_specs=pl.BlockSpec(memory_space=pltpu.VMEM),
        out_shape=jax.ShapeDtypeStruct((4, 32, 224), bf16),
        scratch_shapes=[
            pltpu.VMEM((4, 8, 2048), f32),
            pltpu.VMEM((256, 4096), bf16),
            pltpu.VMEM((2, slots, 2, 16, 2048), bf16),
            pltpu.VMEM((2, 512, 128), f32),
            pltpu.VMEM((3, 4, 32, 256), bf16),
            pltpu.VMEM((3, 4, 32, 256), bf16),
            dma((2,)),
            dma((3,)),
            dma((3,)),
            dma((2, slots)),
            dma((2, slots)),
            dma((2, 3)),
            dma((2, 12)),
            dma((2, slots)),
            dma((3,)),
            dma((3,)),
        ],
        compiler_params=pltpu.CompilerParams(
            collective_id=1, has_side_effects=True, vmem_limit_bytes=40 * 2**20
        ),
        cost_estimate=pl.CostEstimate(
            flops=1_100_000_000, bytes_accessed=8_000_000, transcendentals=0
        ),
    )(head_values, out_weight_t)


def per_device(queries, top_rows, lengths, span_map, latent_cache, up_weight, out_weight):
    query_t = jnp.swapaxes(queries, 2, 3)[0]
    cache_t = jnp.swapaxes(latent_cache, 1, 2)
    head_values = gather_attend(span_map, lengths, top_rows[0], query_t, cache_t, up_weight)
    out = project(head_values, out_weight.T)
    return jnp.swapaxes(out, 0, 1)


def solution(mesh):
    return jax.shard_map(
        per_device,
        mesh=mesh,
        in_specs=(
            P(("req", "ctx"), None, None, None),
            P(("req", "ctx"), None, None),
            P(("req", "ctx")),
            P(),
            P("req", "ctx", None),
            P("req", None, None),
            P("req", "ctx"),
        ),
        out_specs=P("req", None, "ctx"),
        check_vma=False,
    )
```

```python
import functools

import jax
import jax.numpy as jnp
from jax import lax
from jax.experimental import pallas as pl
from jax.experimental.pallas import tpu as pltpu
from jax.sharding import PartitionSpec as P

score_scale = 192.0 ** (-0.5)
log2_scale = score_scale * 1.4426950408889634
masked = -1e30
lowest = -16384.0


MESH = pl.DeviceIdType.MESH
side = 4
slots = side * side
key_rows = 592
latent_rows = 512


def attend_unit(keys, query):
    scores = lax.dot_general(
        query, keys, (((0,), (0,)), ((), ())), preferred_element_type=jnp.float32
    )
    top = jnp.max(scores, axis=1, keepdims=True) * log2_scale
    top = jnp.maximum(top, lowest).astype(jnp.bfloat16).astype(jnp.float32)
    weights = jnp.exp2(scores * log2_scale - top)
    total = jnp.sum(weights, axis=1, keepdims=True)
    mixed = lax.dot_general(
        weights.astype(jnp.bfloat16),
        keys[:latent_rows],
        (((1,), (1,)), ((), ())),
        preferred_element_type=jnp.float32,
    )
    return mixed.astype(jnp.bfloat16), top, total


def pack_stats(top, total):
    lane = lax.broadcasted_iota(jnp.int32, (top.shape[0], 128), 1)
    high = total.astype(jnp.bfloat16).astype(jnp.float32)
    packed = jnp.where(lane == 0, top, jnp.where(lane == 1, high, total - high))
    return packed.astype(jnp.bfloat16)


def spread(i):
    return i + (i // 2) * (5 - 2 * i)


def row_of(slot):
    middle = ((slot // 4) % 3 + 1) // 2
    return (1 - middle) * (slot // 4) + middle * (1 + slot % 2)


def column_of(slot):
    middle = ((slot // 4) % 3 + 1) // 2
    return (1 - middle) * (slot % 4) + middle * ((slot + 4) // 2 - 4)


def merge_stats(stats):
    top = functools.reduce(jnp.maximum, [t for t, _ in stats])
    return top, sum(jnp.exp2(t - top) * l for t, l in stats)


def roll_rows(block, count):
    size = block.shape[0]
    return jnp.concatenate([block[size - count :], block[: size - count]], axis=0)


def make_mask(span_ref, length_ref, rows_ref, line, place_in, mask_one, core, a, b):
    picks = rows_ref[...]
    block = picks // 256
    holder = jnp.zeros_like(block)
    for c in range(64):
        holder = jnp.where(block == c, span_ref[c], holder)
    place_in[...] = jnp.where(block >= 32, 256, 0) + picks % 256
    x, y = holder // 8, (holder // 2) % 4
    ea = (x * (1 - core) + y * core - a + 4) % 4
    eb = (y * (1 - core) + x * core - b + 4) % 4
    ec = (holder + core) % 2
    step = lax.broadcasted_iota(jnp.int32, picks.shape, 0)
    limit = length_ref[0] - 3 + step
    line[...] = jnp.where(picks < limit, 32 * ea + 16 * ec + 4 * eb + step, -1)

    def chunk(i, count):
        columns = pl.ds(pl.multiple_of(i * 512, 512), 512)
        for s in range(4):
            left = lax.broadcasted_iota(jnp.int32, (128, 512), 0) == line[s : s + 1, columns]
            right = lax.broadcasted_iota(jnp.int32, (512, 512), 0) == place_in[s : s + 1, columns]
            count += lax.dot_general(
                left.astype(jnp.float32).astype(jnp.bfloat16),
                right.astype(jnp.float32).astype(jnp.bfloat16),
                (((1,), (1,)), ((), ())), preferred_element_type=jnp.float32)
        return count

    count = lax.fori_loop(0, 4, chunk, jnp.zeros((128, 512), jnp.float32))
    bias = jnp.where(count > 0.5, 0.0, masked).astype(jnp.bfloat16)
    mask_one[...] = bias.reshape(4, 2, 16, 512)


def gather_attend_kernel(
    span_ref, length_ref, rows_ref, query_ref, cache_ref, up_ref, out_ref, far_up,
    own, sib, kept, to_sib, from_sib, own_stat, keys,
    line, place_in, mask_one, mask_mid, mask_two, mask_got, mask_own, mask_sib,
    stats, stats_a, stats_mid, stats_b, factor, up, wide, raw, partial, ring_in, last_out, last_in,
    one_send, one_recv, two_send, two_recv, three_send, three_recv,
    load_sem, key_sem, own_recv, sib_recv, a_send, b_send, sib_send,
    part_send, part_recv, credit, far_send, far_recv, pass_send, pass_recv, up_sem,
    stat_a_send, stat_a_recv, stat_b_send, stat_b_recv,
    ring_send, ring_recv, last_send, last_recv,
):
    me = lax.axis_index("ctx")
    core = me % 2
    chip = me // 2
    a_step = 4 - 3 * core
    b_step = 1 + 3 * core
    a = (chip // a_step) % 4
    b = (chip // b_step) % 4

    def device(da, db):
        return (((a + da + 4) % 4) * a_step + ((b + db + 4) % 4) * b_step) * 2 + core

    group = lax.axis_index("req")
    sibling = chip * 2 + 1 - core
    barrier = pltpu.get_barrier_semaphore()
    partners = [device(d, 0) for d in (1, 2, 3)] + [device(0, d) for d in (1, 2, 3)] + [sibling]
    partners = [{"ctx": partner} for partner in partners]
    partners += [{"req": (group + 1) % 4}, {"req": (group + 3) % 4}]
    for partner in partners:
        pl.semaphore_signal(barrier, inc=1, device_id=partner, device_id_type=MESH)

    def requests(slot):
        ua, ub = 4 - spread(column_of(slot)), 4 - spread(row_of(slot))
        return (
            (((a + ua) % 4) * a_step + ((b + ub) % 4) * b_step) * 2 + core,
            (((b + ua) % 4) * b_step + ((a + ub) % 4) * a_step) * 2 + 1 - core,
        )

    def key_copies(slot, place):
        return [
            pltpu.make_async_copy(
                cache_ref.at[request], keys.at[place, which, pl.ds(0, 576)],
                key_sem.at[place, which])
            for which, request in enumerate(requests(slot))
        ]

    def remote(src, dst, send, recv, target):
        return pltpu.make_async_remote_copy(
            src_ref=src, dst_ref=dst, send_sem=send, recv_sem=recv,
            device_id={"ctx": target}, device_id_type=MESH)

    body = pl.ds(0, 576)

    def a_copy(flow, slot):
        source, side_step = ((0, 1), (0, 3), (1, 1) if flow == 0 else (2, 3))[slot - 1]
        return remote(own.at[flow, source, body], own.at[flow, slot, body],
                      a_send.at[flow, slot - 1], own_recv.at[flow, slot], device(side_step, 0))

    def b_copy(flow, source, slot, side_step):
        return remote(own.at[flow, source, body], own.at[flow, slot, body],
                      b_send.at[flow, slot - 4], own_recv.at[flow, slot], device(0, side_step))

    def arrive(flow, slot):
        place = own.at[flow, slot, body]
        remote(place, place, sib_send.at[flow, slot], own_recv.at[flow, slot], sibling).wait_recv()

    def sib_copy(flow, slot):
        return remote(own.at[flow, slot, body], sib.at[flow, slot, body],
                      sib_send.at[flow, slot], sib_recv.at[flow, slot], sibling)

    def part_copy(slot):
        return remote(to_sib.at[slot % 2], from_sib.at[slot % 4],
                      part_send.at[slot % 2], part_recv.at[slot % 4], sibling)

    def far_copy(piece):
        quarter = pl.ds(16 * core + 8 * (piece % 2), 8)
        if piece < 4:
            src, ahead_z = up_ref.at[quarter], (1 if piece < 2 else 3)
        else:
            src = far_up.at[0 if piece == 4 else 1, quarter]
            ahead_z = 1 if piece == 4 else 3
        return pltpu.make_async_remote_copy(
            src_ref=src, dst_ref=far_up.at[piece // 2, quarter],
            send_sem=far_send.at[piece], recv_sem=far_recv.at[piece],
            device_id={"req": (group + ahead_z) % 4}, device_id_type=MESH)

    def pass_copy(piece):
        quarter = far_up.at[piece // 2, pl.ds(16 * core + 8 * (piece % 2), 8)]
        return remote(quarter, quarter, pass_send.at[piece], pass_recv.at[piece], sibling)

    def stat_a_copy(d):
        return remote(stats, stats_a.at[d - 1], stat_a_send.at[d - 1], stat_a_recv.at[d - 1],
                      device(d, 0))

    def stat_b_copy(d):
        return remote(stats_mid, stats_b.at[d - 1], stat_b_send.at[d - 1],
                      stat_b_recv.at[d - 1], device(0, d))

    def ring_copy(half, gi, db):
        side_step = (3, 1 if half == 0 else 3, 1)[db - 1]
        return remote(partial.at[half, gi, db], ring_in.at[half, gi, db - 1],
                      ring_send.at[half, gi, db - 1], ring_recv.at[half, gi, db - 1],
                      device(0, side_step))

    def last_copy(half, da):
        return remote(last_out.at[half, da - 1], last_in.at[half, da - 1],
                      last_send.at[half, da - 1], last_recv.at[half, da - 1], device(-da, 0))

    loads = [
        pltpu.make_async_copy(
            query_ref.at[2 * flow + half],
            own.at[flow, 0, body, pl.ds(128 * half, 128)],
            load_sem.at[flow, half])
        for flow in range(2) for half in range(2)
    ]
    for copy in loads:
        copy.start()
    for copy in key_copies(0, 0):
        copy.start()

    make_mask(span_ref, length_ref, rows_ref, line, place_in, mask_one, core, a, b)

    row = lax.broadcasted_iota(jnp.int32, (16, 256), 0)
    step = lax.broadcasted_iota(jnp.int32, (16, 256), 1) // 128
    for flow in range(2):

        def fill(slot, carry):
            da = spread(column_of(slot))
            hot = jnp.where(row == step + 2 * flow + 4 * da, 1.0, 0.0).astype(jnp.bfloat16)
            own[flow, slot, 576:key_rows] = hot
            sib[flow, slot, 576:key_rows] = hot
            return carry

        lax.fori_loop(0, slots, fill, 0)
    for copy in loads:
        copy.wait()
    pl.semaphore_wait(barrier, len(partners))

    ones = [remote(mask_one.at[d], mask_mid.at[d], one_send.at[d - 1], one_recv.at[d - 1],
                   device(d, 0)) for d in (1, 2, 3)]
    for copy in ones:
        copy.start()
    for piece in (0, 3, 1, 2):
        far_copy(piece).start()
    for flow in range(2):
        for slot in (1, 2):
            a_copy(flow, slot).start()
        b_copy(flow, 0, 4, 1).start()
        b_copy(flow, 0, 5, 3).start()
        sib_copy(flow, 0).start()
    for copy in ones:
        copy.wait_recv()
    for which in range(2):
        lists = [mask_one[0, which].astype(jnp.float32)]
        lists += [mask_mid[d, which].astype(jnp.float32) for d in (1, 2, 3)]
        for eb in range(4):
            rows = [part[4 * eb : 4 * eb + 4] for part in lists]
            mask_two[eb, which] = jnp.concatenate(rows, axis=0).astype(jnp.bfloat16)
    twos = [remote(mask_two.at[d], mask_got.at[d], two_send.at[d - 1], two_recv.at[d - 1],
                   device(0, d)) for d in (1, 2, 3)]
    for copy in twos:
        copy.start()
    for copy in twos:
        copy.wait_recv()
    mask_own[0] = mask_two[0, 0]
    mask_own[4] = mask_two[0, 1]
    for d in (1, 2, 3):
        mask_own[d] = mask_got[d, 0]
        mask_own[4 + d] = mask_got[d, 1]
    three = remote(mask_own.at[pl.ds(4, 4)], mask_sib, three_send, three_recv, sibling)
    three.start()
    three.wait_recv()

    row16 = lax.broadcasted_iota(jnp.int32, (16, 128), 0)
    lane = lax.broadcasted_iota(jnp.int32, (128, 128), 1)

    def combine(slot):
        db, da = spread(row_of(slot)), spread(column_of(slot))
        part_copy(slot).wait_recv()

        def one_step(s, carry):
            rows = pl.ds(pl.multiple_of(128 * s, 128), 128)
            got = from_sib[slot % 4, rows, 512:640].astype(jnp.float32)
            top_1, total_1 = own_stat[slot % 2, 0, rows], own_stat[slot % 2, 1, rows]
            top_2 = jnp.broadcast_to(got[:, 0:1], (128, 128))
            total_2 = jnp.broadcast_to(got[:, 1:2] + got[:, 2:3], (128, 128))
            top = jnp.maximum(top_1, top_2)
            factor_1, factor_2 = jnp.exp2(top_1 - top), jnp.exp2(top_2 - top)
            total = factor_1 * total_1 + factor_2 * total_2
            for i in range(4):
                lanes = slice(128 * i, 128 * i + 128)
                value = factor_1 * kept[slot, rows, lanes].astype(jnp.float32)
                value += factor_2 * from_sib[slot % 4, rows, lanes].astype(jnp.float32)
                kept[slot, rows, lanes] = value.astype(jnp.bfloat16)
            both = jnp.swapaxes(jnp.where(lane < 64, top, total), 0, 1)
            for i in range(2):
                value = both[64 * i : 64 * i + 16]
                stats[i, db] = jnp.where(row16 == 4 * da + s, value, stats[i, db])
            return carry

        lax.fori_loop(0, 4, one_step, 0)

    def give_credit():
        pl.semaphore_signal(credit, inc=1, device_id={"ctx": sibling}, device_id_type=MESH)

    def iteration(slot, carry):
        place = slot % 2

        def first_row(at):
            for flow in range(2):
                arrive(flow, at)
                if at == 1 + flow:
                    a_copy(flow, 3).start()
                b_copy(flow, at, 4 + 2 * at, 1).start()
                b_copy(flow, at, 5 + 2 * at, 3).start()
                sib_copy(flow, at).start()

        @pl.when(slot == 1)
        def _():
            first_row(1)
            first_row(2)

        @pl.when(slot == 2)
        def _():
            first_row(3)

        @pl.when((slot >= 2) & (slot < 10))
        def _():
            for flow in range(2):
                arrive(flow, slot + 2)

        @pl.when((slot >= 2) & (slot < 10) & (slot % 2 == 0))
        def _():
            b_copy(0, slot + 2, 11 + slot // 2, 1).start()

        @pl.when((slot >= 2) & (slot < 10) & (slot % 2 == 1))
        def _():
            b_copy(1, slot + 2, 11 + slot // 2, 3).start()

        @pl.when((slot >= 2) & (slot < 10))
        def _():
            for flow in range(2):
                sib_copy(flow, slot + 2).start()

        @pl.when(slot >= 12)
        def _():
            for flow in range(2):
                arrive(flow, slot)
                sib_copy(flow, slot).start()

        @pl.when(slot < slots - 1)
        def _():
            for copy in key_copies(slot + 1, 1 - place):
                copy.start()

        for copy in key_copies(slot, place):
            copy.wait()
        db = spread(row_of(slot))
        keys[place, 0, 576:key_rows] = mask_own[db]
        keys[place, 1, 576:key_rows] = mask_sib[db]

        query = jnp.concatenate([own[0, slot], own[1, slot]], axis=1)
        mixed, top, total = attend_unit(keys[place, 0], query)
        kept[slot] = mixed
        own_stat[place, 0] = jnp.broadcast_to(top, (512, 128))
        own_stat[place, 1] = jnp.broadcast_to(total, (512, 128))

        for flow in range(2):
            sib_copy(flow, slot).wait_recv()

        @pl.when(slot >= 2)
        def _():
            part_copy(slot).wait_send()

        query = jnp.concatenate([sib[0, slot], sib[1, slot]], axis=1)
        mixed, top, total = attend_unit(keys[place, 1], query)
        to_sib[place, :, 0:512] = mixed
        to_sib[place, :, 512:640] = pack_stats(top, total)

        @pl.when(slot >= 4)
        def _():
            pl.semaphore_wait(credit, 1)

        part_copy(slot).start()

        @pl.when(slot > 0)
        def _():
            combine(slot - 1)

        @pl.when((slot > 0) & (slot < 13))
        def _():
            give_credit()

        @pl.when(slot == 8)
        def _():
            for piece in (0, 3):
                far_copy(piece).wait_recv()
                pass_copy(piece).start()
            far_copy(4).start()
            far_copy(5).start()

        @pl.when(slot == 12)
        def _():
            for piece in (1, 2):
                far_copy(piece).wait_recv()
                pass_copy(piece).start()

        return carry

    stats[...] = jnp.zeros_like(stats)
    lax.fori_loop(0, slots, iteration, 0)

    def up_copy(gi):
        src = up_ref if gi == 0 else far_up.at[(1, 0, 2)[gi - 1]]
        return pltpu.make_async_copy(src, up.at[gi % 2], up_sem.at[gi % 2])

    def fill_group(gi):
        first_head = pl.multiple_of(32 * ((group + spread(gi)) % 4), 32)

        def fill_wide(slot, carry):
            place = 4 * spread(row_of(slot)) + spread(column_of(slot))
            for s in range(4):
                rows = pl.ds(pl.multiple_of(128 * s + first_head, 32), 32)
                value = kept[slot, rows].astype(jnp.float32)
                at = pl.ds(pl.multiple_of(32 * (4 * place + s), 32), 32)
                for i in range(4):
                    wide[i, at] = value[:, 128 * i : 128 * i + 128]
            return carry

        lax.fori_loop(0, slots, fill_wide, 0)

    def product(gi, head):
        rows = [wide[i, pl.ds(head, 64, stride=32), :] for i in range(4)]
        rows = jnp.concatenate(rows, axis=1).astype(jnp.bfloat16)
        return jnp.dot(rows, up[gi % 2, head], preferred_element_type=jnp.float32)

    def store(gi, head, value):
        lanes = slice(128 * (head % 16), 128 * (head % 16) + 128)
        for db in range(4):
            partial[head // 16, gi, db, :, lanes] = value[16 * db : 16 * db + 16].astype(jnp.bfloat16)

    up_copy(0).start()
    combine(slots - 1)
    for d in (1, 2, 3):
        stat_a_copy(d).start()
    for piece in (2, 3):
        pass_copy(piece).wait_recv()
    up_copy(1).start()
    fill_group(0)
    for d in (1, 2, 3):
        stat_a_copy(d).wait_recv()
    for db in range(4):
        parts = [(stats[0, db], stats[1, db])]
        for d in (1, 2, 3):
            parts.append(tuple(roll_rows(stats_a[d - 1, i, db], 4 * d) for i in range(2)))
        stats_mid[0, db], stats_mid[1, db] = merge_stats(parts)
    for d in (1, 2, 3):
        stat_b_copy(d).start()
    def finish_stats():
        for d in (1, 2, 3):
            stat_b_copy(d).wait_recv()
        for db in range(4):
            parts = [(stats_mid[0, db], stats_mid[1, db])]
            for d in (1, 2, 3):
                parts.append((stats_b[d - 1, 0, (db - d) % 4], stats_b[d - 1, 1, (db - d) % 4]))
            top, total = merge_stats(parts)
            value = jnp.exp2(stats[0, db] - top) / total
            for z in range(4):
                shifted = value
                if z:
                    shifted = jnp.concatenate([value[:, 32 * z :], value[:, : 32 * z]], axis=1)
                for gi in range(4):

                    @pl.when((group + spread(gi)) % 4 == z)
                    def _():
                        factor[gi, 16 * db : 16 * db + 16] = shifted

    def chain(gi):
        for half in range(2):
            by = 3 if half == 0 else 1
            ring_copy(half, gi, 2).wait_recv()
            value = partial[half, gi, by].astype(jnp.float32)
            value += ring_in[half, gi, 1].astype(jnp.float32)
            partial[half, gi, by] = value.astype(jnp.bfloat16)
            ring_copy(half, gi, by).start()

    def one_group(gi, carry):
        pltpu.make_async_copy(up_ref, up.at[gi % 2], up_sem.at[gi % 2]).wait()

        @pl.when(gi > 0)
        def _():
            fill_group(gi)

        for head in range(32):
            raw[head] = product(gi, head)

        @pl.when(gi == 0)
        def _():
            for piece in (4, 5):
                far_copy(piece).wait_recv()
                pass_copy(piece).start()
            for piece in (0, 1):
                pass_copy(piece).wait_recv()
            up_copy(2).start()
            finish_stats()

        @pl.when(gi == 1)
        def _():
            for piece in (4, 5):
                pass_copy(piece).wait_recv()
            up_copy(3).start()

        weight = factor[gi]
        for head in range(32):
            store(gi, head, raw[head] * weight[:, head : head + 1])
            if head % 16 == 15:
                half = head // 16
                ring_copy(half, gi, 2).start()
                ring_copy(half, gi, 1 if half == 0 else 3).start()

        @pl.when(gi > 0)
        def _():
            chain(gi - 1)

        return carry

    lax.fori_loop(0, 4, one_group, 0)
    chain(3)

    whole = []
    for half in range(2):
        ends = []
        for gi in range(4):
            ring_copy(half, gi, 1).wait_recv()
            ring_copy(half, gi, 3).wait_recv()
            value = partial[half, gi, 0].astype(jnp.float32)
            value += ring_in[half, gi, 0].astype(jnp.float32)
            ends.append(value + ring_in[half, gi, 2].astype(jnp.float32))
        for da in (1, 2, 3):
            rows = [end[4 * da : 4 * da + 4] for end in ends]
            last_out[half, da - 1] = jnp.concatenate(rows, axis=0).astype(jnp.bfloat16)
            last_copy(half, da).start()
        whole.append(jnp.concatenate([end[0:4] for end in ends], axis=0))
    for half in range(2):
        for da in (1, 2, 3):
            last_copy(half, da).wait_recv()
            whole[half] = whole[half] + last_in[half, da - 1].astype(jnp.float32)
    for gi in range(4):
        picked = [value[4 * gi : 4 * gi + 4] for value in whole]
        out_ref[gi] = jnp.concatenate(picked, axis=0)

    for flow in range(2):
        def drain(slot, carry):
            sib_copy(flow, slot).wait_send()
            return carry

        lax.fori_loop(0, slots, drain, 0)
        part_copy(14 + flow).wait_send()
        for slot in range(4, 12):
            b_copy(flow, slot // 2 - 2, slot, 3 if slot % 2 else 1).wait_send()
        for slot in range(12, 16):
            b_copy(flow, 2 * slot - 20 + flow, slot, 3 if flow else 1).wait_send()
        for da in (1, 2, 3):
            a_copy(flow, da).wait_send()
            last_copy(flow, da).wait_send()
            for gi in range(4):
                ring_copy(flow, gi, da).wait_send()
    for piece in range(6):
        far_copy(piece).wait_send()
        pass_copy(piece).wait_send()
    for d in (1, 2, 3):
        stat_a_copy(d).wait_send()
        stat_b_copy(d).wait_send()
    for copy in ones + twos + [three]:
        copy.wait_send()


def gather_attend(span_map, lengths, top_rows, query_t, cache_t, up_weight):
    dma = pltpu.SemaphoreType.DMA
    bf16, f32 = jnp.bfloat16, jnp.float32
    return pl.pallas_call(
        gather_attend_kernel,
        in_specs=[pl.BlockSpec(memory_space=pltpu.SMEM)] * 2
        + [pl.BlockSpec(memory_space=pltpu.VMEM)]
        + [pl.BlockSpec(memory_space=pl.ANY)] * 3,
        out_specs=[pl.BlockSpec(memory_space=pltpu.VMEM), pl.BlockSpec(memory_space=pl.ANY)],
        out_shape=[
            jax.ShapeDtypeStruct((4, 8, 2048), f32),
            jax.ShapeDtypeStruct((3,) + up_weight.shape, bf16),
        ],
        scratch_shapes=[
            pltpu.VMEM((2, slots, key_rows, 256), bf16),
            pltpu.VMEM((2, slots, key_rows, 256), bf16),
            pltpu.VMEM((slots, 512, 512), bf16),
            pltpu.VMEM((2, 512, 640), bf16),
            pltpu.VMEM((4, 512, 640), bf16),
            pltpu.VMEM((2, 2, 512, 128), f32),
            pltpu.VMEM((2, 2, key_rows, 512), bf16),
            pltpu.VMEM((4, 2048), jnp.int32),
            pltpu.VMEM((4, 2048), jnp.int32),
            pltpu.VMEM((4, 2, 16, 512), bf16),
            pltpu.VMEM((4, 2, 16, 512), bf16),
            pltpu.VMEM((4, 2, 16, 512), bf16),
            pltpu.VMEM((4, 2, 16, 512), bf16),
            pltpu.VMEM((8, 16, 512), bf16),
            pltpu.VMEM((4, 16, 512), bf16),
            pltpu.VMEM((2, 4, 16, 128), f32),
            pltpu.VMEM((3, 2, 4, 16, 128), f32),
            pltpu.VMEM((2, 4, 16, 128), f32),
            pltpu.VMEM((3, 2, 4, 16, 128), f32),
            pltpu.VMEM((4, 64, 128), f32),
            pltpu.VMEM((2, 32, 512, 128), bf16),
            pltpu.VMEM((4, 2048, 128), f32),
            pltpu.VMEM((32, 64, 128), f32),
            pltpu.VMEM((2, 4, 4, 16, 2048), bf16),
            pltpu.VMEM((2, 4, 3, 16, 2048), bf16),
            pltpu.VMEM((2, 3, 16, 2048), bf16),
            pltpu.VMEM((2, 3, 16, 2048), bf16),
            dma((3,)),
            dma((3,)),
            dma((3,)),
            dma((3,)),
            dma,
            dma,
            dma((2, 2)),
            dma((2, 2)),
            dma((2, slots)),
            dma((2, slots)),
            dma((2, 3)),
            dma((2, 12)),
            dma((2, slots)),
            dma((2,)),
            dma((4,)),
            pltpu.SemaphoreType.REGULAR,
            dma((6,)),
            dma((6,)),
            dma((6,)),
            dma((6,)),
            dma((2,)),
            dma((3,)),
            dma((3,)),
            dma((3,)),
            dma((3,)),
            dma((2, 4, 3)),
            dma((2, 4, 3)),
            dma((2, 3)),
            dma((2, 3)),
        ],
        compiler_params=pltpu.CompilerParams(
            collective_id=0, has_side_effects=True, vmem_limit_bytes=60 * 2**20
        ),
        cost_estimate=pl.CostEstimate(
            flops=19_000_000_000, bytes_accessed=60_000_000, transcendentals=8_000_000
        ),
    )(span_map, lengths, top_rows, query_t, cache_t, up_weight)[0]


def project_kernel(
    head_ref, out_weight_ref, out_ref,
    taken, weight, values, sums, give, get,
    load_sem, take_send, take_recv, own_recv, sib_recv, a_send, b_send, sib_send,
    give_send, give_recv,
):
    me = lax.axis_index("ctx")
    group = lax.axis_index("req")
    core = me % 2
    chip = me // 2
    a_step = 4 - 3 * core
    b_step = 1 + 3 * core
    a = (chip // a_step) % 4
    b = (chip // b_step) % 4

    def device(da, db):
        return {"ctx": (((a + da) % 4) * a_step + ((b + db) % 4) * b_step) * 2 + core}

    def plane(d):
        return {"req": (group + d) % 4}

    sibling = {"ctx": chip * 2 + 1 - core}
    partners = [device(1, 0), device(3, 0), device(0, 1), device(0, 3), sibling]
    partners += [plane(1), plane(2), plane(3)]
    barrier = pltpu.get_barrier_semaphore()
    for partner in partners:
        pl.semaphore_signal(barrier, inc=1, device_id=partner, device_id_type=MESH)

    def remote(src, dst, send, recv, target):
        return pltpu.make_async_remote_copy(
            src_ref=src, dst_ref=dst, send_sem=send, recv_sem=recv,
            device_id=target, device_id_type=MESH)

    loads = [
        pltpu.make_async_copy(head_ref.at[0], taken.at[0], load_sem.at[0]),
        pltpu.make_async_copy(out_weight_ref, weight.at[pl.ds(0, 224)], load_sem.at[1]),
    ]
    for copy in loads:
        copy.start()
    pl.semaphore_wait(barrier, len(partners))
    takes = [
        remote(head_ref.at[(0, 1, 3, 2)[d]], taken.at[d], take_send.at[d - 1],
               take_recv.at[d - 1], plane(d))
        for d in (1, 2, 3)
    ]
    for copy in takes:
        copy.start()

    weight[224:256] = jnp.zeros((32, 4096), jnp.bfloat16)
    loads[0].wait()
    for copy in takes:
        copy.wait_recv()

    def a_copy(flow, slot):
        source, side_step = ((0, 1), (0, 3), (1, 1) if flow == 0 else (2, 3))[slot - 1]
        return remote(values.at[flow, source, 0], values.at[flow, slot, 0],
                      a_send.at[flow, slot - 1], own_recv.at[flow, slot], device(side_step, 0))

    def b_copy(flow, slot):
        back, side_step = ((4, 1), (8, 3), (8, 1) if flow == 0 else (4, 3))[slot // 4 - 1]
        return remote(values.at[flow, slot - back, 0], values.at[flow, slot, 0],
                      b_send.at[flow, slot - 4], own_recv.at[flow, slot], device(0, side_step))

    def sib_copy(flow, slot):
        return remote(values.at[flow, slot, 0], values.at[flow, slot, 1],
                      sib_send.at[flow, slot], sib_recv.at[flow, slot], sibling)

    def forward(flow, slot):
        if slot == 0:
            a_copy(flow, 1).start()
            a_copy(flow, 2).start()
        if slot == 1 + flow:
            a_copy(flow, 3).start()
        if slot < 4:
            b_copy(flow, slot + 4).start()
            b_copy(flow, slot + 8).start()
        elif slot // 4 == 1 + flow:
            b_copy(flow, slot + (4 if flow else 8)).start()
        sib_copy(flow, slot).start()

    for flow in range(2):
        rows = [taken[d, 4 * flow : 4 * flow + 4] for d in range(4)]
        values[flow, 0, 0] = jnp.concatenate(rows, axis=0).astype(jnp.bfloat16)
        forward(flow, 0)

    loads[1].wait()
    for slot in range(slots):
        for flow in range(2):
            if slot:
                (a_copy if slot < 4 else b_copy)(flow, slot).wait_recv()
                forward(flow, slot)
        if slot % 4 != 3:
            continue
        row = slot // 4
        db = spread(row)
        left = []
        for flow in range(2):
            for i in range(4):
                sib_copy(flow, 4 * row + i).wait_recv()
            left.append(values[flow, 4 * row : 4 * row + 4].reshape(128, 2048))
        term = lax.dot_general(
            jnp.concatenate(left, axis=1), weight[...],
            (((1,), (1,)), ((), ())), preferred_element_type=jnp.float32)
        for i in range(4):
            ua, ub = 4 - spread(i), 4 - db
            origins = (
                (((a + ua) % 4) * a_step + ((b + ub) % 4) * b_step) * 2 + core,
                (((b + ua) % 4) * b_step + ((a + ub) % 4) * a_step) * 2 + 1 - core,
            )
            for which, origin in enumerate(origins):
                at = 16 * (2 * i + which)
                place = pl.ds(pl.multiple_of(origin * 16, 16), 16)
                for half in range(2):
                    sums[half, place] = term[at : at + 16, 128 * half : 128 * half + 128]

    def share(d, s):
        return jnp.concatenate(
            [sums[i, pl.ds(4 * d + s, 32, stride=16), :] for i in range(2)], axis=1)

    gives = []
    for d in (1, 2, 3):
        for s in range(4):
            give[d - 1, s] = share(d, s).astype(jnp.bfloat16)
        copy = remote(give.at[d - 1], get.at[d - 1], give_send.at[d - 1], give_recv.at[d - 1],
                      plane(4 - d))
        copy.start()
        gives.append(copy)
    for copy in gives:
        copy.wait_recv()
    for s in range(4):
        total = share(0, s)
        for i in range(3):
            total = total + get[i, s].astype(jnp.float32)
        out_ref[s] = total[:, :224].astype(jnp.bfloat16)

    for copy in takes + gives:
        copy.wait_send()
    for flow in range(2):
        for slot in range(slots):
            sib_copy(flow, slot).wait_send()
            if 0 < slot < 4:
                a_copy(flow, slot).wait_send()
            if slot >= 4:
                b_copy(flow, slot).wait_send()


def project(head_values, out_weight_t):
    dma = pltpu.SemaphoreType.DMA
    bf16, f32 = jnp.bfloat16, jnp.float32
    return pl.pallas_call(
        project_kernel,
        in_specs=[pl.BlockSpec(memory_space=pl.ANY)] * 2,
        out_specs=pl.BlockSpec(memory_space=pltpu.VMEM),
        out_shape=jax.ShapeDtypeStruct((4, 32, 224), bf16),
        scratch_shapes=[
            pltpu.VMEM((4, 8, 2048), f32),
            pltpu.VMEM((256, 4096), bf16),
            pltpu.VMEM((2, slots, 2, 16, 2048), bf16),
            pltpu.VMEM((2, 512, 128), f32),
            pltpu.VMEM((3, 4, 32, 256), bf16),
            pltpu.VMEM((3, 4, 32, 256), bf16),
            dma((2,)),
            dma((3,)),
            dma((3,)),
            dma((2, slots)),
            dma((2, slots)),
            dma((2, 3)),
            dma((2, 12)),
            dma((2, slots)),
            dma((3,)),
            dma((3,)),
        ],
        compiler_params=pltpu.CompilerParams(
            collective_id=1, has_side_effects=True, vmem_limit_bytes=60 * 2**20
        ),
        cost_estimate=pl.CostEstimate(
            flops=1_100_000_000, bytes_accessed=8_000_000, transcendentals=0
        ),
    )(head_values, out_weight_t)


def per_device(queries, top_rows, lengths, span_map, latent_cache, up_weight, out_weight):
    query_t = jnp.swapaxes(queries, 2, 3)[0]
    cache_t = jnp.swapaxes(latent_cache, 1, 2)
    head_values = gather_attend(span_map, lengths, top_rows[0], query_t, cache_t, up_weight)
    out = project(head_values, out_weight.T)
    return jnp.swapaxes(out, 0, 1)


def solution(mesh):
    return jax.shard_map(
        per_device,
        mesh=mesh,
        in_specs=(
            P(("req", "ctx"), None, None, None),
            P(("req", "ctx"), None, None),
            P(("req", "ctx")),
            P(),
            P("req", "ctx", None),
            P("req", None, None),
            P("req", "ctx"),
        ),
        out_specs=P("req", None, "ctx"),
        check_vma=False,
    )
```

```python
import functools

import jax
import jax.numpy as jnp
from jax import lax
from jax.experimental import pallas as pl
from jax.experimental.pallas import tpu as pltpu
from jax.sharding import PartitionSpec as P

score_scale = 192.0 ** (-0.5)
log2_scale = score_scale * 1.4426950408889634
masked = -1e30
lowest = -16384.0


MESH = pl.DeviceIdType.MESH
side = 4
slots = side * side
key_rows = 592
latent_rows = 512


def attend_unit(keys, query):
    scores = lax.dot_general(
        query, keys, (((0,), (0,)), ((), ())), preferred_element_type=jnp.float32
    )
    top = jnp.max(scores, axis=1, keepdims=True) * log2_scale
    top = jnp.maximum(top, lowest).astype(jnp.bfloat16).astype(jnp.float32)
    weights = jnp.exp2(scores * log2_scale - top)
    total = jnp.sum(weights, axis=1, keepdims=True)
    mixed = lax.dot_general(
        weights.astype(jnp.bfloat16),
        keys[:latent_rows],
        (((1,), (1,)), ((), ())),
        preferred_element_type=jnp.float32,
    )
    return mixed.astype(jnp.bfloat16), top, total


def pack_stats(top, total):
    lane = lax.broadcasted_iota(jnp.int32, (top.shape[0], 128), 1)
    high = total.astype(jnp.bfloat16).astype(jnp.float32)
    packed = jnp.where(lane == 0, top, jnp.where(lane == 1, high, total - high))
    return packed.astype(jnp.bfloat16)


def spread(i):
    return i + (i // 2) * (5 - 2 * i)


def row_of(slot):
    middle = ((slot // 4) % 3 + 1) // 2
    return (1 - middle) * (slot // 4) + middle * (1 + slot % 2)


def column_of(slot):
    middle = ((slot // 4) % 3 + 1) // 2
    return (1 - middle) * (slot % 4) + middle * ((slot + 4) // 2 - 4)


def merge_stats(stats):
    top = functools.reduce(jnp.maximum, [t for t, _ in stats])
    return top, sum(jnp.exp2(t - top) * l for t, l in stats)


def roll_rows(block, count):
    size = block.shape[0]
    return jnp.concatenate([block[size - count :], block[: size - count]], axis=0)


def make_mask(span_ref, length_ref, rows_ref, line, place_in, mask_one, core, a, b):
    picks = rows_ref[...]
    block = picks // 256
    holder = jnp.zeros_like(block)
    for c in range(64):
        holder = jnp.where(block == c, span_ref[c], holder)
    place_in[...] = jnp.where(block >= 32, 256, 0) + picks % 256
    x, y = holder // 8, (holder // 2) % 4
    ea = (x * (1 - core) + y * core - a + 4) % 4
    eb = (y * (1 - core) + x * core - b + 4) % 4
    ec = (holder + core) % 2
    step = lax.broadcasted_iota(jnp.int32, picks.shape, 0)
    limit = length_ref[0] - 3 + step
    line[...] = jnp.where(picks < limit, 32 * ea + 16 * ec + 4 * eb + step, -1)

    def chunk(i, count):
        columns = pl.ds(pl.multiple_of(i * 512, 512), 512)
        for s in range(4):
            left = lax.broadcasted_iota(jnp.int32, (128, 512), 0) == line[s : s + 1, columns]
            right = lax.broadcasted_iota(jnp.int32, (512, 512), 0) == place_in[s : s + 1, columns]
            count += lax.dot_general(
                left.astype(jnp.float32).astype(jnp.bfloat16),
                right.astype(jnp.float32).astype(jnp.bfloat16),
                (((1,), (1,)), ((), ())), preferred_element_type=jnp.float32)
        return count

    count = lax.fori_loop(0, 4, chunk, jnp.zeros((128, 512), jnp.float32))
    bias = jnp.where(count > 0.5, 0.0, masked).astype(jnp.bfloat16)
    mask_one[...] = bias.reshape(4, 2, 16, 512)


def gather_attend_kernel(
    span_ref, length_ref, rows_ref, query_ref, cache_ref, up_ref, out_ref, far_up,
    own, sib, kept, to_sib, from_sib, own_stat, keys,
    line, place_in, mask_one, mask_mid, mask_two, mask_got, mask_own, mask_sib,
    stats, stats_a, stats_mid, stats_b, factor, up, wide, raw, partial, ring_in, last_out, last_in,
    one_send, one_recv, two_send, two_recv, three_send, three_recv,
    load_sem, key_sem, own_recv, sib_recv, a_send, b_send, sib_send,
    part_send, part_recv, credit, far_send, far_recv, pass_send, pass_recv, up_sem,
    stat_a_send, stat_a_recv, stat_b_send, stat_b_recv,
    ring_send, ring_recv, last_send, last_recv,
):
    me = lax.axis_index("ctx")
    core = me % 2
    chip = me // 2
    a_step = 4 - 3 * core
    b_step = 1 + 3 * core
    a = (chip // a_step) % 4
    b = (chip // b_step) % 4

    def device(da, db):
        return (((a + da + 4) % 4) * a_step + ((b + db + 4) % 4) * b_step) * 2 + core

    group = lax.axis_index("req")
    sibling = chip * 2 + 1 - core
    barrier = pltpu.get_barrier_semaphore()
    partners = [device(d, 0) for d in (1, 2, 3)] + [device(0, d) for d in (1, 2, 3)] + [sibling]
    partners = [{"ctx": partner} for partner in partners]
    partners += [{"req": (group + 1) % 4}, {"req": (group + 3) % 4}]
    for partner in partners:
        pl.semaphore_signal(barrier, inc=1, device_id=partner, device_id_type=MESH)

    def requests(slot):
        ua, ub = 4 - spread(column_of(slot)), 4 - spread(row_of(slot))
        return (
            (((a + ua) % 4) * a_step + ((b + ub) % 4) * b_step) * 2 + core,
            (((b + ua) % 4) * b_step + ((a + ub) % 4) * a_step) * 2 + 1 - core,
        )

    def key_copies(slot, place):
        return [
            pltpu.make_async_copy(
                cache_ref.at[request], keys.at[place, which, pl.ds(0, 576)],
                key_sem.at[place, which])
            for which, request in enumerate(requests(slot))
        ]

    def remote(src, dst, send, recv, target):
        return pltpu.make_async_remote_copy(
            src_ref=src, dst_ref=dst, send_sem=send, recv_sem=recv,
            device_id={"ctx": target}, device_id_type=MESH)

    body = pl.ds(0, 576)

    def a_copy(flow, slot):
        source, side_step = ((0, 1), (0, 3), (1, 1) if flow == 0 else (2, 3))[slot - 1]
        return remote(own.at[flow, source, body], own.at[flow, slot, body],
                      a_send.at[flow, slot - 1], own_recv.at[flow, slot], device(side_step, 0))

    def b_copy(flow, source, slot, side_step):
        return remote(own.at[flow, source, body], own.at[flow, slot, body],
                      b_send.at[flow, slot - 4], own_recv.at[flow, slot], device(0, side_step))

    def arrive(flow, slot):
        place = own.at[flow, slot, body]
        remote(place, place, sib_send.at[flow, slot], own_recv.at[flow, slot], sibling).wait_recv()

    def sib_copy(flow, slot):
        return remote(own.at[flow, slot, body], sib.at[flow, slot, body],
                      sib_send.at[flow, slot], sib_recv.at[flow, slot], sibling)

    def part_copy(slot):
        return remote(to_sib.at[slot % 2], from_sib.at[slot % 4],
                      part_send.at[slot % 2], part_recv.at[slot % 4], sibling)

    def far_copy(piece):
        quarter = pl.ds(16 * core + 8 * (piece % 2), 8)
        if piece < 4:
            src, ahead_z = up_ref.at[quarter], (1 if piece < 2 else 3)
        else:
            src = far_up.at[0 if piece == 4 else 1, quarter]
            ahead_z = 1 if piece == 4 else 3
        return pltpu.make_async_remote_copy(
            src_ref=src, dst_ref=far_up.at[piece // 2, quarter],
            send_sem=far_send.at[piece], recv_sem=far_recv.at[piece],
            device_id={"req": (group + ahead_z) % 4}, device_id_type=MESH)

    def pass_copy(piece):
        quarter = far_up.at[piece // 2, pl.ds(16 * core + 8 * (piece % 2), 8)]
        return remote(quarter, quarter, pass_send.at[piece], pass_recv.at[piece], sibling)

    def stat_a_copy(d):
        return remote(stats, stats_a.at[d - 1], stat_a_send.at[d - 1], stat_a_recv.at[d - 1],
                      device(d, 0))

    def stat_b_copy(d):
        return remote(stats_mid, stats_b.at[d - 1], stat_b_send.at[d - 1],
                      stat_b_recv.at[d - 1], device(0, d))

    def ring_copy(half, gi, db):
        side_step = (3, 1 if half == 0 else 3, 1)[db - 1]
        return remote(partial.at[half, gi, db], ring_in.at[half, gi, db - 1],
                      ring_send.at[half, gi, db - 1], ring_recv.at[half, gi, db - 1],
                      device(0, side_step))

    def last_copy(half, da):
        return remote(last_out.at[half, da - 1], last_in.at[half, da - 1],
                      last_send.at[half, da - 1], last_recv.at[half, da - 1], device(-da, 0))

    loads = [
        pltpu.make_async_copy(
            query_ref.at[2 * flow + half],
            own.at[flow, 0, body, pl.ds(128 * half, 128)],
            load_sem.at[flow, half])
        for flow in range(2) for half in range(2)
    ]
    for copy in loads:
        copy.start()
    for copy in key_copies(0, 0):
        copy.start()

    make_mask(span_ref, length_ref, rows_ref, line, place_in, mask_one, core, a, b)

    row = lax.broadcasted_iota(jnp.int32, (16, 256), 0)
    step = lax.broadcasted_iota(jnp.int32, (16, 256), 1) // 128
    for flow in range(2):

        def fill(slot, carry):
            da = spread(column_of(slot))
            hot = jnp.where(row == step + 2 * flow + 4 * da, 1.0, 0.0).astype(jnp.bfloat16)
            own[flow, slot, 576:key_rows] = hot
            sib[flow, slot, 576:key_rows] = hot
            return carry

        lax.fori_loop(0, slots, fill, 0)
    for copy in loads:
        copy.wait()
    pl.semaphore_wait(barrier, len(partners))

    ones = [remote(mask_one.at[d], mask_mid.at[d], one_send.at[d - 1], one_recv.at[d - 1],
                   device(d, 0)) for d in (1, 2, 3)]
    for copy in ones:
        copy.start()
    for piece in (0, 3, 1, 2):
        far_copy(piece).start()
    for flow in range(2):
        for slot in (1, 2):
            a_copy(flow, slot).start()
        b_copy(flow, 0, 4, 1).start()
        b_copy(flow, 0, 5, 3).start()
        sib_copy(flow, 0).start()
    for copy in ones:
        copy.wait_recv()
    for which in range(2):
        lists = [mask_one[0, which].astype(jnp.float32)]
        lists += [mask_mid[d, which].astype(jnp.float32) for d in (1, 2, 3)]
        for eb in range(4):
            rows = [part[4 * eb : 4 * eb + 4] for part in lists]
            mask_two[eb, which] = jnp.concatenate(rows, axis=0).astype(jnp.bfloat16)
    twos = [remote(mask_two.at[d], mask_got.at[d], two_send.at[d - 1], two_recv.at[d - 1],
                   device(0, d)) for d in (1, 2, 3)]
    for copy in twos:
        copy.start()
    for copy in twos:
        copy.wait_recv()
    mask_own[0] = mask_two[0, 0]
    mask_own[4] = mask_two[0, 1]
    for d in (1, 2, 3):
        mask_own[d] = mask_got[d, 0]
        mask_own[4 + d] = mask_got[d, 1]
    three = remote(mask_own.at[pl.ds(4, 4)], mask_sib, three_send, three_recv, sibling)
    three.start()
    three.wait_recv()

    row16 = lax.broadcasted_iota(jnp.int32, (16, 128), 0)
    lane = lax.broadcasted_iota(jnp.int32, (128, 128), 1)

    def combine(slot):
        db, da = spread(row_of(slot)), spread(column_of(slot))
        part_copy(slot).wait_recv()
        for s in range(4):
            rows = slice(128 * s, 128 * s + 128)
            got = from_sib[slot % 4, rows, 512:640].astype(jnp.float32)
            top_1, total_1 = own_stat[slot % 2, 0, rows], own_stat[slot % 2, 1, rows]
            top_2 = jnp.broadcast_to(got[:, 0:1], (128, 128))
            total_2 = jnp.broadcast_to(got[:, 1:2] + got[:, 2:3], (128, 128))
            top = jnp.maximum(top_1, top_2)
            factor_1, factor_2 = jnp.exp2(top_1 - top), jnp.exp2(top_2 - top)
            total = factor_1 * total_1 + factor_2 * total_2
            for i in range(4):
                lanes = slice(128 * i, 128 * i + 128)
                value = factor_1 * kept[slot, rows, lanes].astype(jnp.float32)
                value += factor_2 * from_sib[slot % 4, rows, lanes].astype(jnp.float32)
                kept[slot, rows, lanes] = value.astype(jnp.bfloat16)
            both = jnp.swapaxes(jnp.where(lane < 64, top, total), 0, 1)
            for i in range(2):
                value = both[64 * i : 64 * i + 16]
                stats[i, db] = jnp.where(row16 == 4 * da + s, value, stats[i, db])

    def give_credit():
        pl.semaphore_signal(credit, inc=1, device_id={"ctx": sibling}, device_id_type=MESH)

    def iteration(slot, carry):
        place = slot % 2

        def first_row(at):
            for flow in range(2):
                arrive(flow, at)
                if at == 1 + flow:
                    a_copy(flow, 3).start()
                b_copy(flow, at, 4 + 2 * at, 1).start()
                b_copy(flow, at, 5 + 2 * at, 3).start()
                sib_copy(flow, at).start()

        @pl.when(slot == 1)
        def _():
            first_row(1)
            first_row(2)

        @pl.when(slot == 2)
        def _():
            first_row(3)

        @pl.when((slot >= 2) & (slot < 10))
        def _():
            for flow in range(2):
                arrive(flow, slot + 2)

        @pl.when((slot >= 2) & (slot < 10) & (slot % 2 == 0))
        def _():
            b_copy(0, slot + 2, 11 + slot // 2, 1).start()

        @pl.when((slot >= 2) & (slot < 10) & (slot % 2 == 1))
        def _():
            b_copy(1, slot + 2, 11 + slot // 2, 3).start()

        @pl.when((slot >= 2) & (slot < 10))
        def _():
            for flow in range(2):
                sib_copy(flow, slot + 2).start()

        @pl.when((slot >= 11) & (slot < 15))
        def _():
            for flow in range(2):
                arrive(flow, slot + 1)
                sib_copy(flow, slot + 1).start()

        @pl.when(slot < slots - 1)
        def _():
            for copy in key_copies(slot + 1, 1 - place):
                copy.start()

        for copy in key_copies(slot, place):
            copy.wait()
        db = spread(row_of(slot))
        keys[place, 0, 576:key_rows] = mask_own[db]
        keys[place, 1, 576:key_rows] = mask_sib[db]

        for flow in range(2):
            sib_copy(flow, slot).wait_recv()

        @pl.when(slot >= 2)
        def _():
            part_copy(slot).wait_send()

        query = jnp.concatenate([own[0, slot], own[1, slot]], axis=1)
        other = jnp.concatenate([sib[0, slot], sib[1, slot]], axis=1)
        mixed, top, total = attend_unit(keys[place, 0], query)
        mixed_2, top_2, total_2 = attend_unit(keys[place, 1], other)
        kept[slot] = mixed
        own_stat[place, 0] = jnp.broadcast_to(top, (512, 128))
        own_stat[place, 1] = jnp.broadcast_to(total, (512, 128))
        to_sib[place, :, 0:512] = mixed_2
        to_sib[place, :, 512:640] = pack_stats(top_2, total_2)

        @pl.when(slot >= 4)
        def _():
            pl.semaphore_wait(credit, 1)

        part_copy(slot).start()

        @pl.when(slot > 0)
        def _():
            combine(slot - 1)

        @pl.when((slot > 0) & (slot < 13))
        def _():
            give_credit()

        @pl.when(slot == 8)
        def _():
            for piece in (0, 3):
                far_copy(piece).wait_recv()
                pass_copy(piece).start()
            far_copy(4).start()
            far_copy(5).start()

        @pl.when(slot == 12)
        def _():
            for piece in (1, 2):
                far_copy(piece).wait_recv()
                pass_copy(piece).start()

        return carry

    stats[...] = jnp.zeros_like(stats)
    lax.fori_loop(0, slots, iteration, 0)

    def up_copy(gi):
        src = up_ref if gi == 0 else far_up.at[gi - 1]
        return pltpu.make_async_copy(src, up.at[gi % 2], up_sem.at[gi % 2])

    def fill_group(gi):
        first_head = pl.multiple_of(32 * ((group + ahead_of[gi]) % 4), 32)

        def fill_wide(slot, carry):
            place = 4 * spread(row_of(slot)) + spread(column_of(slot))
            for s in range(4):
                rows = pl.ds(pl.multiple_of(128 * s + first_head, 32), 32)
                value = kept[slot, rows].astype(jnp.float32)
                at = pl.ds(pl.multiple_of(32 * (4 * place + s), 32), 32)
                for i in range(4):
                    wide[i, at] = value[:, 128 * i : 128 * i + 128]
            return carry

        lax.fori_loop(0, slots, fill_wide, 0)

    def product(gi, head):
        rows = [wide[i, pl.ds(head, 64, stride=32), :] for i in range(4)]
        rows = jnp.concatenate(rows, axis=1).astype(jnp.bfloat16)
        return jnp.dot(rows, up[gi % 2, head], preferred_element_type=jnp.float32)

    def scaled(gi, head, value, weight):
        lane = 32 * ahead_of[gi] + head
        return value * weight[:, lane : lane + 1]

    def store(gi, head, value):
        lanes = slice(128 * (head % 16), 128 * (head % 16) + 128)
        for db in range(4):
            partial[head // 16, gi, db, :, lanes] = value[16 * db : 16 * db + 16].astype(jnp.bfloat16)

    ahead_of = (0, 3, 1, 2)
    up_copy(0).start()
    combine(slots - 1)
    for d in (1, 2, 3):
        stat_a_copy(d).start()
    for piece in (0, 1):
        pass_copy(piece).wait_recv()
    up_copy(1).start()
    fill_group(0)
    up_copy(0).wait()
    for d in (1, 2, 3):
        stat_a_copy(d).wait_recv()
    for db in range(4):
        parts = [(stats[0, db], stats[1, db])]
        for d in (1, 2, 3):
            parts.append(tuple(roll_rows(stats_a[d - 1, i, db], 4 * d) for i in range(2)))
        stats_mid[0, db], stats_mid[1, db] = merge_stats(parts)
    for d in (1, 2, 3):
        stat_b_copy(d).start()
    for head in range(32):
        raw[head] = product(0, head)
    for piece in (4, 5):
        far_copy(piece).wait_recv()
        pass_copy(piece).start()
    for d in (1, 2, 3):
        stat_b_copy(d).wait_recv()
    for db in range(4):
        parts = [(stats_mid[0, db], stats_mid[1, db])]
        for d in (1, 2, 3):
            parts.append((stats_b[d - 1, 0, (db - d) % 4], stats_b[d - 1, 1, (db - d) % 4]))
        top, total = merge_stats(parts)
        value = jnp.exp2(stats[0, db] - top) / total
        turned = value
        for z in (1, 2, 3):
            shifted = jnp.concatenate([value[:, 32 * z :], value[:, : 32 * z]], axis=1)
            turned = jnp.where(group == z, shifted, turned)
        factor[16 * db : 16 * db + 16] = turned

    def chain(gi):
        for half in range(2):
            by = 3 if half == 0 else 1
            ring_copy(half, gi, 2).wait_recv()
            value = partial[half, gi, by].astype(jnp.float32)
            value += ring_in[half, gi, 1].astype(jnp.float32)
            partial[half, gi, by] = value.astype(jnp.bfloat16)
            ring_copy(half, gi, by).start()

    for gi in range(4):
        if gi:
            up_copy(gi).wait()
            fill_group(gi)
        weight = factor[...]
        for head in range(32):
            value = raw[head] if gi == 0 else product(gi, head)
            store(gi, head, scaled(gi, head, value, weight))
            if head % 16 == 15:
                half = head // 16
                ring_copy(half, gi, 2).start()
                ring_copy(half, gi, 1 if half == 0 else 3).start()
        if gi == 0:
            for piece in (2, 3):
                pass_copy(piece).wait_recv()
            up_copy(2).start()
        if gi == 1:
            for piece in (4, 5):
                pass_copy(piece).wait_recv()
            up_copy(3).start()
        if gi >= 1:
            chain(gi - 1)
    chain(3)

    whole = []
    for half in range(2):
        ends = []
        for gi in range(4):
            ring_copy(half, gi, 1).wait_recv()
            ring_copy(half, gi, 3).wait_recv()
            value = partial[half, gi, 0].astype(jnp.float32)
            value += ring_in[half, gi, 0].astype(jnp.float32)
            ends.append(value + ring_in[half, gi, 2].astype(jnp.float32))
        for da in (1, 2, 3):
            rows = [end[4 * da : 4 * da + 4] for end in ends]
            last_out[half, da - 1] = jnp.concatenate(rows, axis=0).astype(jnp.bfloat16)
            last_copy(half, da).start()
        whole.append(jnp.concatenate([end[0:4] for end in ends], axis=0))
    for half in range(2):
        for da in (1, 2, 3):
            last_copy(half, da).wait_recv()
            whole[half] = whole[half] + last_in[half, da - 1].astype(jnp.float32)
    for gi in range(4):
        picked = [value[4 * gi : 4 * gi + 4] for value in whole]
        out_ref[gi] = jnp.concatenate(picked, axis=0)

    for flow in range(2):
        def drain(slot, carry):
            sib_copy(flow, slot).wait_send()
            return carry

        lax.fori_loop(0, slots, drain, 0)
        part_copy(14 + flow).wait_send()
        for slot in range(4, 12):
            b_copy(flow, slot // 2 - 2, slot, 3 if slot % 2 else 1).wait_send()
        for slot in range(12, 16):
            b_copy(flow, 2 * slot - 20 + flow, slot, 3 if flow else 1).wait_send()
        for da in (1, 2, 3):
            a_copy(flow, da).wait_send()
            last_copy(flow, da).wait_send()
            for gi in range(4):
                ring_copy(flow, gi, da).wait_send()
    for piece in range(6):
        far_copy(piece).wait_send()
        pass_copy(piece).wait_send()
    for d in (1, 2, 3):
        stat_a_copy(d).wait_send()
        stat_b_copy(d).wait_send()
    for copy in ones + twos + [three]:
        copy.wait_send()


def gather_attend(span_map, lengths, top_rows, query_t, cache_t, up_weight):
    dma = pltpu.SemaphoreType.DMA
    bf16, f32 = jnp.bfloat16, jnp.float32
    return pl.pallas_call(
        gather_attend_kernel,
        in_specs=[pl.BlockSpec(memory_space=pltpu.SMEM)] * 2
        + [pl.BlockSpec(memory_space=pltpu.VMEM)]
        + [pl.BlockSpec(memory_space=pl.ANY)] * 3,
        out_specs=[pl.BlockSpec(memory_space=pltpu.VMEM), pl.BlockSpec(memory_space=pl.ANY)],
        out_shape=[
            jax.ShapeDtypeStruct((4, 8, 2048), f32),
            jax.ShapeDtypeStruct((3,) + up_weight.shape, bf16),
        ],
        scratch_shapes=[
            pltpu.VMEM((2, slots, key_rows, 256), bf16),
            pltpu.VMEM((2, slots, key_rows, 256), bf16),
            pltpu.VMEM((slots, 512, 512), bf16),
            pltpu.VMEM((2, 512, 640), bf16),
            pltpu.VMEM((4, 512, 640), bf16),
            pltpu.VMEM((2, 2, 512, 128), f32),
            pltpu.VMEM((2, 2, key_rows, 512), bf16),
            pltpu.VMEM((4, 2048), jnp.int32),
            pltpu.VMEM((4, 2048), jnp.int32),
            pltpu.VMEM((4, 2, 16, 512), bf16),
            pltpu.VMEM((4, 2, 16, 512), bf16),
            pltpu.VMEM((4, 2, 16, 512), bf16),
            pltpu.VMEM((4, 2, 16, 512), bf16),
            pltpu.VMEM((8, 16, 512), bf16),
            pltpu.VMEM((4, 16, 512), bf16),
            pltpu.VMEM((2, 4, 16, 128), f32),
            pltpu.VMEM((3, 2, 4, 16, 128), f32),
            pltpu.VMEM((2, 4, 16, 128), f32),
            pltpu.VMEM((3, 2, 4, 16, 128), f32),
            pltpu.VMEM((64, 128), f32),
            pltpu.VMEM((2, 32, 512, 128), bf16),
            pltpu.VMEM((4, 2048, 128), f32),
            pltpu.VMEM((32, 64, 128), f32),
            pltpu.VMEM((2, 4, 4, 16, 2048), bf16),
            pltpu.VMEM((2, 4, 3, 16, 2048), bf16),
            pltpu.VMEM((2, 3, 16, 2048), bf16),
            pltpu.VMEM((2, 3, 16, 2048), bf16),
            dma((3,)),
            dma((3,)),
            dma((3,)),
            dma((3,)),
            dma,
            dma,
            dma((2, 2)),
            dma((2, 2)),
            dma((2, slots)),
            dma((2, slots)),
            dma((2, 3)),
            dma((2, 12)),
            dma((2, slots)),
            dma((2,)),
            dma((4,)),
            pltpu.SemaphoreType.REGULAR,
            dma((6,)),
            dma((6,)),
            dma((6,)),
            dma((6,)),
            dma((2,)),
            dma((3,)),
            dma((3,)),
            dma((3,)),
            dma((3,)),
            dma((2, 4, 3)),
            dma((2, 4, 3)),
            dma((2, 3)),
            dma((2, 3)),
        ],
        compiler_params=pltpu.CompilerParams(
            collective_id=0, has_side_effects=True, vmem_limit_bytes=60 * 2**20
        ),
        cost_estimate=pl.CostEstimate(
            flops=19_000_000_000, bytes_accessed=60_000_000, transcendentals=8_000_000
        ),
    )(span_map, lengths, top_rows, query_t, cache_t, up_weight)[0]


def project_kernel(
    head_ref, out_weight_ref, out_ref,
    taken, weight, values, sums, give, get,
    load_sem, take_send, take_recv, own_recv, sib_recv, a_send, b_send, sib_send,
    give_send, give_recv,
):
    me = lax.axis_index("ctx")
    group = lax.axis_index("req")
    core = me % 2
    chip = me // 2
    a_step = 4 - 3 * core
    b_step = 1 + 3 * core
    a = (chip // a_step) % 4
    b = (chip // b_step) % 4

    def device(da, db):
        return {"ctx": (((a + da) % 4) * a_step + ((b + db) % 4) * b_step) * 2 + core}

    def plane(d):
        return {"req": (group + d) % 4}

    sibling = {"ctx": chip * 2 + 1 - core}
    partners = [device(1, 0), device(3, 0), device(0, 1), device(0, 3), sibling]
    partners += [plane(1), plane(2), plane(3)]
    barrier = pltpu.get_barrier_semaphore()
    for partner in partners:
        pl.semaphore_signal(barrier, inc=1, device_id=partner, device_id_type=MESH)

    def remote(src, dst, send, recv, target):
        return pltpu.make_async_remote_copy(
            src_ref=src, dst_ref=dst, send_sem=send, recv_sem=recv,
            device_id=target, device_id_type=MESH)

    loads = [
        pltpu.make_async_copy(head_ref.at[0], taken.at[0], load_sem.at[0]),
        pltpu.make_async_copy(out_weight_ref, weight.at[pl.ds(0, 224)], load_sem.at[1]),
    ]
    for copy in loads:
        copy.start()
    pl.semaphore_wait(barrier, len(partners))
    takes = [
        remote(head_ref.at[(0, 2, 3, 1)[d]], taken.at[d], take_send.at[d - 1],
               take_recv.at[d - 1], plane(d))
        for d in (1, 2, 3)
    ]
    for copy in takes:
        copy.start()

    weight[224:256] = jnp.zeros((32, 4096), jnp.bfloat16)
    loads[0].wait()
    for copy in takes:
        copy.wait_recv()

    def a_copy(flow, slot):
        source, side_step = ((0, 1), (0, 3), (1, 1) if flow == 0 else (2, 3))[slot - 1]
        return remote(values.at[flow, source, 0], values.at[flow, slot, 0],
                      a_send.at[flow, slot - 1], own_recv.at[flow, slot], device(side_step, 0))

    def b_copy(flow, slot):
        back, side_step = ((4, 1), (8, 3), (8, 1) if flow == 0 else (4, 3))[slot // 4 - 1]
        return remote(values.at[flow, slot - back, 0], values.at[flow, slot, 0],
                      b_send.at[flow, slot - 4], own_recv.at[flow, slot], device(0, side_step))

    def sib_copy(flow, slot):
        return remote(values.at[flow, slot, 0], values.at[flow, slot, 1],
                      sib_send.at[flow, slot], sib_recv.at[flow, slot], sibling)

    def forward(flow, slot):
        if slot == 0:
            a_copy(flow, 1).start()
            a_copy(flow, 2).start()
        if slot == 1 + flow:
            a_copy(flow, 3).start()
        if slot < 4:
            b_copy(flow, slot + 4).start()
            b_copy(flow, slot + 8).start()
        elif slot // 4 == 1 + flow:
            b_copy(flow, slot + (4 if flow else 8)).start()
        sib_copy(flow, slot).start()

    for flow in range(2):
        rows = [taken[d, 4 * flow : 4 * flow + 4] for d in range(4)]
        values[flow, 0, 0] = jnp.concatenate(rows, axis=0).astype(jnp.bfloat16)
        forward(flow, 0)

    loads[1].wait()
    def products(row):
        db = spread(row)
        left = []
        for flow in range(2):
            for i in range(4):
                sib_copy(flow, 4 * row + i).wait_recv()
            left.append(values[flow, 4 * row : 4 * row + 4].reshape(128, 2048))
        term = lax.dot_general(
            jnp.concatenate(left, axis=1), weight[...],
            (((1,), (1,)), ((), ())), preferred_element_type=jnp.float32)
        for i in range(4):
            ua, ub = 4 - spread(i), 4 - db
            origins = (
                (((a + ua) % 4) * a_step + ((b + ub) % 4) * b_step) * 2 + core,
                (((b + ua) % 4) * b_step + ((a + ub) % 4) * a_step) * 2 + 1 - core,
            )
            for which, origin in enumerate(origins):
                at = 16 * (2 * i + which)
                place = pl.ds(pl.multiple_of(origin * 16, 16), 16)
                for half in range(2):
                    sums[half, place] = term[at : at + 16, 128 * half : 128 * half + 128]

    for slot in (0, 1, 2, 3, 4, 8, 5, 9, 6, 10, 7, 11):
        for flow in range(2):
            if slot:
                (a_copy if slot < 4 else b_copy)(flow, slot).wait_recv()
                forward(flow, slot)
    for row in range(3):
        products(row)
    for slot in (12, 13, 14, 15):
        for flow in range(2):
            b_copy(flow, slot).wait_recv()
            forward(flow, slot)
    products(3)

    def share(d, s):
        return jnp.concatenate(
            [sums[i, pl.ds(4 * d + s, 32, stride=16), :] for i in range(2)], axis=1)

    gives = []
    for d in (1, 2, 3):
        for s in range(4):
            give[d - 1, s] = share(d, s).astype(jnp.bfloat16)
        copy = remote(give.at[d - 1], get.at[d - 1], give_send.at[d - 1], give_recv.at[d - 1],
                      plane(4 - d))
        copy.start()
        gives.append(copy)
    for copy in gives:
        copy.wait_recv()
    for s in range(4):
        total = share(0, s)
        for i in range(3):
            total = total + get[i, s].astype(jnp.float32)
        out_ref[s] = total[:, :224].astype(jnp.bfloat16)

    for copy in takes + gives:
        copy.wait_send()
    for flow in range(2):
        for slot in range(slots):
            sib_copy(flow, slot).wait_send()
            if 0 < slot < 4:
                a_copy(flow, slot).wait_send()
            if slot >= 4:
                b_copy(flow, slot).wait_send()


def project(head_values, out_weight_t):
    dma = pltpu.SemaphoreType.DMA
    bf16, f32 = jnp.bfloat16, jnp.float32
    return pl.pallas_call(
        project_kernel,
        in_specs=[pl.BlockSpec(memory_space=pl.ANY)] * 2,
        out_specs=pl.BlockSpec(memory_space=pltpu.VMEM),
        out_shape=jax.ShapeDtypeStruct((4, 32, 224), bf16),
        scratch_shapes=[
            pltpu.VMEM((4, 8, 2048), f32),
            pltpu.VMEM((256, 4096), bf16),
            pltpu.VMEM((2, slots, 2, 16, 2048), bf16),
            pltpu.VMEM((2, 512, 128), f32),
            pltpu.VMEM((3, 4, 32, 256), bf16),
            pltpu.VMEM((3, 4, 32, 256), bf16),
            dma((2,)),
            dma((3,)),
            dma((3,)),
            dma((2, slots)),
            dma((2, slots)),
            dma((2, 3)),
            dma((2, 12)),
            dma((2, slots)),
            dma((3,)),
            dma((3,)),
        ],
        compiler_params=pltpu.CompilerParams(
            collective_id=1, has_side_effects=True, vmem_limit_bytes=40 * 2**20
        ),
        cost_estimate=pl.CostEstimate(
            flops=1_100_000_000, bytes_accessed=8_000_000, transcendentals=0
        ),
    )(head_values, out_weight_t)


def per_device(queries, top_rows, lengths, span_map, latent_cache, up_weight, out_weight):
    query_t = jnp.swapaxes(queries, 2, 3)[0]
    cache_t = jnp.swapaxes(latent_cache, 1, 2)
    head_values = gather_attend(span_map, lengths, top_rows[0], query_t, cache_t, up_weight)
    out = project(head_values, out_weight.T)
    return jnp.swapaxes(out, 0, 1)


def solution(mesh):
    return jax.shard_map(
        per_device,
        mesh=mesh,
        in_specs=(
            P(("req", "ctx"), None, None, None),
            P(("req", "ctx"), None, None),
            P(("req", "ctx")),
            P(),
            P("req", "ctx", None),
            P("req", None, None),
            P("req", "ctx"),
        ),
        out_specs=P("req", None, "ctx"),
        check_vma=False,
    )
```
